32 devices in a mesh: seq: 16 (over z, y, x), rep: 2 (over core).
Axes of the slice: x: 2, y: 2, z: 4, core: 2. Of those that a mesh axis runs over, the one named last changes fastest.
Arguments:
- series: float32 [2, 160, 1440], P('rep', None, 'seq'), may hold values from -60 to 60
- group_ids: int32 [160], replicated, may hold values from 0 to 3
- rev_gain: float32 [160], replicated, may hold values from 0.5 to 1.5
- rev_bias: float32 [160], replicated, may hold values from -4 to 4
- mode_in: float32 [256, 4], replicated, may hold values from -0.375 to 0.375
- mode_out: float32 [256, 4], replicated, may hold values from -0.375 to 0.375
- mode_re: float32 [4, 32], replicated, may hold values from -24 to 24
- mode_im: float32 [4, 32], replicated, may hold values from -24 to 24
- mixing: float32 [160, 160], replicated, may hold values from -1 to 1
- out_bias: float32 [160], replicated, may hold values from -6 to 6
- cotangent: float32 [2, 160, 1440], P('rep', None, 'seq'), may hold values from -6 to 6
Outputs:
- layer_out: float32 [2, 160, 1440], P('rep', None, 'seq')
- series_grad: float32 [2, 160, 1440], P('rep', None, 'seq')
- rev_gain_grad: float32 [160], replicated
- rev_bias_grad: float32 [160], replicated
- mode_in_grad: float32 [256, 4], replicated
- mode_out_grad: float32 [256, 4], replicated
- mode_re_grad: float32 [4, 32], replicated
- mode_im_grad: float32 [4, 32], replicated
- mixing_grad: float32 [160, 160], replicated
- out_bias_grad: float32 [160], replicated
The draws below stay inside these ranges and needn't reach their ends.
All inputs are finite; a program needn't handle non-finite values.
Results may differ from the reference program's by a relative error of at most 0.0003.
Values sent between devices are 32-bit elements; how exact they have to be, the bound alone decides.
No kernel may reach another device: no remote copies, remote signals or barrier semaphores. Data moves between devices by JAX's collectives and lax.ppermute only.
A program may use at most 192 MiB of HBM per device.

```python
import jax
import jax.numpy as jnp
from jax import lax

ORDER = 256
MODES = 32
RANK = 4
WINDOW = 720
CH_DEV = 10
CHANNELS = 160
TIME = 1440
BATCH = 2
N_SEQ = 16


def draw_series(key, part):
    key = jax.random.fold_in(key, 11)
    keys = jax.random.split(key, 4)
    layout = (BATCH, CHANNELS, TIME)
    noise = jax.random.truncated_normal(keys[0], -5.0, 5.0, layout, jnp.float32)
    scales = jnp.exp(jax.random.uniform(keys[1], (CHANNELS,), jnp.float32, jnp.log(0.5), jnp.log(4.0)))
    slopes = jax.random.uniform(keys[2], (CHANNELS,), jnp.float32, 0.5, 1.5)
    levels = jax.random.uniform(keys[3], (CHANNELS,), jnp.float32, -1.0, 1.0)
    ramp = jnp.arange(TIME).astype(jnp.float32) / TIME
    values = noise + levels[None, :, None] + slopes[None, :, None] * ramp[None, None, :]
    return values * scales[None, :, None]


def place_ends(entries, rng, smallest, high):
    longest = entries.shape.index(max(entries.shape))
    spots = []
    for shift in (0, 1):
        where = [jax.random.randint(jax.random.fold_in(rng, axis), (), 0, length) for axis, length in enumerate(entries.shape)]
        where[longest] = (where[longest] + shift) % entries.shape[longest]
        spots.append(tuple(where))
    return entries.at[spots[0]].set(smallest).at[spots[1]].set(high)


def block_levels(rng, dims, cuts, smallest, high):
    level, own = 1.0, jax.random.fold_in(rng, 6)
    for position, blocks in cuts:
        draws = jnp.exp(jax.random.uniform(jax.random.fold_in(own, position), (blocks,), jnp.float32, smallest / len(cuts), high / len(cuts)))
        level = level * jnp.repeat(draws, dims[position] // blocks).reshape([-1 if axis == position else 1 for axis in range(len(dims))])
    return level


def centred(rng, extent, scale, bound, cuts=(), kind=jnp.bfloat16):
    loudness = block_levels(rng, extent, cuts, -0.22, 0.18) if cuts else 1.0
    values = jax.random.normal(rng, extent, jnp.float32) * scale * loudness
    return jnp.minimum(jnp.maximum(values, -bound), bound).astype(kind)


def setup_inputs(seed: int = 0) -> dict:
    key_list = jax.random.split(jax.random.key(seed), 12)
    return {
        "series": draw_series(jax.random.fold_in(key_list[11], 71), 0),
        "group_ids": place_ends(jax.random.randint(key_list[1], (CHANNELS,), 0, 4), jax.random.fold_in(key_list[1], 1), 0, 3).astype(jnp.int32),
        "rev_gain": jnp.clip(1.0 + 0.1 * jax.random.normal(key_list[2], (CHANNELS,), jnp.float32), 0.5, 1.5),
        "rev_bias": centred(key_list[3], (CHANNELS,), 0.3, 4.0, (), jnp.float32),
        "mode_in": centred(key_list[4], (ORDER, RANK), ORDER ** -0.5, 0.375, (), jnp.float32),
        "mode_out": centred(key_list[5], (ORDER, RANK), ORDER ** -0.5, 0.375, (), jnp.float32),
        "mode_re": centred(key_list[6], (RANK, MODES), 4.0, 24.0, (), jnp.float32),
        "mode_im": centred(key_list[7], (RANK, MODES), 4.0, 24.0, (), jnp.float32),
        "mixing": centred(key_list[8], (CHANNELS, CHANNELS), (CHANNELS // 4) ** -0.5, 1.0, (), jnp.float32),
        "out_bias": centred(key_list[9], (CHANNELS,), 0.5, 6.0, (), jnp.float32),
        "cotangent": centred(key_list[10], (BATCH, CHANNELS, TIME), 1.0, 6.0, ((0, 2), (2, 16)), jnp.float32),
    }


epsilon = 1e-05
precise = lax.Precision.HIGHEST

@jax.custom_vjp
def low(v):
    return lax.optimization_barrier(v.astype(jnp.bfloat16)).astype(jnp.float32)

@jax.custom_vjp
def low_back(v):
    return v

def low_keep(v):
    return (low(v), None)

def low_pass(kept, grad):
    return (grad,)

def back_keep(v):
    return (v, None)

def back_low(kept, grad):
    return (low(grad),)
low.defvjp(low_keep, low_pass)
low_back.defvjp(back_keep, back_low)

def legendre_rows(degrees, window):
    lag_index = jnp.arange(window).astype(jnp.float32)
    points = 1.0 - 2.0 * (lag_index + 0.5) / window

    def advance(state_pair, degree):
        lower_poly, this_poly = state_pair
        upper_poly = ((2.0 * degree + 1.0) * points * this_poly - degree * lower_poly) / (degree + 1.0)
        return ((this_poly, upper_poly), this_poly)
    initial = (jnp.zeros_like(points), jnp.ones_like(points))
    unused, legendre = lax.scan(advance, initial, jnp.arange(degrees).astype(jnp.float32))
    return legendre

def channel_branch(series_part, gain_part, offset_part, kernel, mode_re, mode_im, recon_mix):
    total_steps = series_part.shape[-1]
    denominator = jnp.arange(total_steps).astype(jnp.float32) + 1.0 + WINDOW
    running_mean = jnp.cumsum(series_part, axis=-1) / denominator
    variance = (jnp.cumsum(series_part * series_part, axis=-1) + WINDOW) / denominator - running_mean * running_mean
    spread = jnp.sqrt(variance + epsilon)
    normal = gain_part[None, :, None] * (series_part - running_mean) / spread + offset_part[None, :, None]
    length = total_steps + WINDOW
    product = jnp.fft.rfft(normal, n=length)[:, :, None, :] * jnp.fft.rfft(kernel, n=length)[None, None]
    coeffs = jnp.fft.irfft(product, n=length)[..., :total_steps]
    windows = coeffs.reshape(coeffs.shape[:3] + (total_steps // WINDOW, WINDOW))
    spectra = jnp.fft.rfft(windows, axis=-1)[..., :MODES]
    factor = (mode_re + 1j * mode_im)[None, None, :, None, :]
    filtered = spectra * factor
    padded_spec = jnp.zeros(windows.shape[:-1] + (WINDOW // 2 + 1,), filtered.dtype).at[..., :MODES].set(filtered)
    rebuilt = jnp.fft.irfft(padded_spec, n=WINDOW, axis=-1).reshape(coeffs.shape)
    recon = jnp.einsum('bcrt,r->bct', rebuilt, recon_mix, precision=precise)
    return (recon - offset_part[None, :, None]) / gain_part[None, :, None] * spread + running_mean

def forward(series, rev_gain, rev_bias, mode_in, mode_out, mode_re, mode_im, mixing, out_bias, same_group):
    samples = series.shape[0]
    total_steps = series.shape[2]
    legendre = legendre_rows(ORDER, WINDOW)
    degree = jnp.arange(ORDER).astype(jnp.float32)
    weights = legendre * ((2.0 * degree + 1.0) / WINDOW)[:, None]
    kernel = jnp.dot(mode_in.T, weights, precision=precise)
    recon_mix = jnp.dot(legendre[:, 0], mode_out, precision=precise)
    grouped = series.reshape(samples, N_SEQ, CH_DEV, total_steps).transpose(1, 0, 2, 3)
    gains = rev_gain.reshape(N_SEQ, CH_DEV)
    offsets = rev_bias.reshape(N_SEQ, CH_DEV)

    def one_group(packed):
        return channel_branch(packed[0], packed[1], packed[2], kernel, mode_re, mode_im, recon_mix)
    restored = lax.map(jax.checkpoint(one_group), (grouped, gains, offsets))
    restored = restored.transpose(1, 0, 2, 3).reshape(series.shape)
    masked = mixing * same_group
    mixed = jnp.einsum('ij,bjt->bit', masked, restored, precision=precise)
    return series + mixed + out_bias[None, :, None]

def reference(series, group_ids, rev_gain, rev_bias, mode_in, mode_out, mode_re, mode_im, mixing, out_bias, cotangent):
    same_group = (group_ids[:, None] == group_ids[None, :]).astype(jnp.float32)

    def layer(series_in, gain_in, offset_in, factor_in, factor_out, part_re, part_im, mixing_in, bias_in):
        return forward(series_in, gain_in, offset_in, factor_in, factor_out, part_re, part_im, mixing_in, bias_in, same_group)
    layer_out, pullback = jax.vjp(layer, series, rev_gain, rev_bias, mode_in, mode_out, mode_re, mode_im, mixing, out_bias)
    grads = pullback(cotangent)
    return (layer_out, grads[0], grads[1], grads[2], grads[3], grads[4], grads[5], grads[6], grads[7], grads[8])
```

```python
import functools
import math

import jax
import jax.numpy as jnp
import ml_dtypes
import numpy as np
from jax import lax
from jax.experimental import pallas as pl
from jax.experimental.pallas import tpu as pltpu
from jax.sharding import PartitionSpec as P

ORDER = 256
MODES = 32
RANK = 4
WINDOW = 720
EPSILON = 1e-05

LANES = 128
SLOT = 16
SEND = 24
f32 = jnp.float32
bf16 = jnp.bfloat16


def up(value, multiple):
    return -(-value // multiple) * multiple


def legendre_table():
    one, two = np.float32(1.0), np.float32(2.0)
    lags = np.arange(WINDOW).astype(np.float32)
    points = one - (two * (lags + np.float32(0.5))) * np.float32(1.0 / WINDOW)
    lower, this = np.zeros_like(points), np.ones_like(points)
    rows = []
    for degree in np.arange(ORDER).astype(np.float32):
        rows.append(this)
        upper = ((two * degree + one) * points * this - degree * lower) / (degree + one)
        lower, this = this, upper
    return np.stack(rows)


def in_blocks(values, steps):
    blocks = WINDOW // steps
    framed = np.zeros(values.shape[:-1] + (blocks, LANES))
    framed[..., :steps] = values.reshape(values.shape[:-1] + (blocks, steps))
    return framed.reshape(values.shape[:-1] + (blocks * LANES,))


def halves(values):
    high = values.astype(np.float32).astype(ml_dtypes.bfloat16)
    low = (values - high.astype(np.float64)).astype(ml_dtypes.bfloat16)
    return high, low


def constants(steps):
    legendre = legendre_table()
    degree = np.arange(ORDER).astype(np.float32)
    weights = legendre * ((np.float32(2.0) * degree + np.float32(1.0)) / np.float32(WINDOW))[:, None]
    flipped = in_blocks(weights[:, ::-1], steps)
    high, low = halves(flipped)
    table = {}
    table["weights"] = np.concatenate([high, low], 1)
    table["weights_t"] = np.concatenate([high.T, low.T], 1)
    table["endpoint"] = legendre[:, 0][None, :].astype(np.float32)
    mode = np.arange(MODES)[:, None]
    step = np.arange(WINDOW)[None, :]
    angle = 2.0 * math.pi / WINDOW * (mode * step % WINDOW)
    cosine, sine = np.cos(angle), np.sin(angle)
    back = 2.0 * math.pi / WINDOW * (mode * (WINDOW - 1 - step) % WINDOW)
    table["turn"] = np.concatenate(
        [in_blocks(v, steps) for v in (cosine, sine, np.cos(back), np.sin(back))]
    ).astype(np.float32)
    scale = np.where(np.arange(MODES) == 0, 1.0, 2.0) / WINDOW
    table["scale"] = np.concatenate([scale, scale])[None, :].astype(np.float32)
    table["scale_t"] = np.concatenate([scale, scale])[:, None].astype(np.float32)
    high, low = halves(in_blocks(np.concatenate([cosine, -sine]), steps))
    table["to_modes"] = np.concatenate([high.T, low.T], 1)
    wave = in_blocks(np.concatenate([scale[:, None] * cosine, -scale[:, None] * sine]), steps)
    high, low = halves(np.concatenate([wave, wave]))
    table["from_modes"] = np.concatenate([high, low, high])
    lane = np.arange(LANES)
    upper = (lane[:, None] <= lane[None, :]).astype(np.float32)
    ones = np.ones((LANES, LANES), np.float32)
    for name, part in (("earlier", upper), ("later", upper.T)):
        both = np.concatenate([part, ones], 1)
        table[name] = np.concatenate([both, both]).astype(ml_dtypes.bfloat16)
    return table


def split(value):
    high = value.astype(bf16)
    return high, (value - high.astype(f32)).astype(bf16)


def dot(a, b):
    return lax.dot_general(a, b, (((1,), (0,)), ((), ())), preferred_element_type=f32)


def dot_nt(a, b):
    return lax.dot_general(a, b, (((1,), (1,)), ((), ())), preferred_element_type=f32)


def stacked_dot(value, table):
    rows, width = value.shape[0], table.shape[1] // 2
    high, low = split(value)
    out = dot(jnp.concatenate([high, low], 0), table)
    return out[:rows, :width] + out[:rows, width:] + out[rows:, :width]


def thrice(value):
    high, low = split(value)
    return jnp.concatenate([high, high, low], 1)


def scan_lanes(value, table):
    high, low = split(value)
    out = dot(jnp.concatenate([high, low], 1), table)
    return out[:, :LANES], out[:, LANES:]


def row_of(i, kind):
    return 8 * kind + i if i < 8 else 16 + (i - 8) + 2 * kind


def to_wide(blocks, windows):
    per = len(blocks) // windows
    return jnp.concatenate(
        [jnp.concatenate(blocks[w * per : (w + 1) * per], 1) for w in range(windows)], 0
    )


def to_blocks(wide, windows):
    per = wide.shape[1] // LANES
    return [
        wide[w * SLOT : (w + 1) * SLOT, b * LANES : (b + 1) * LANES]
        for w in range(windows)
        for b in range(per)
    ]


def blocks_of(value):
    return [value[k * SLOT : (k + 1) * SLOT] for k in range(value.shape[0] // SLOT)]


def same_rows(groups_ref, start, rows):
    channels = groups_ref.shape[1]
    ids = groups_ref[...].astype(f32)
    row = lax.broadcasted_iota(jnp.int32, (rows, channels), 0) + start
    lane = lax.broadcasted_iota(jnp.int32, (rows, channels), 1)
    column = jnp.sum(jnp.where(row == lane, ids, 0.0), axis=1, keepdims=True)
    return column == ids


def own_lanes(place, channels, width, count, blocks):
    row = lax.broadcasted_iota(jnp.int32, (SLOT, width), 0)
    lane = lax.broadcasted_iota(jnp.int32, (SLOT, width), 1)
    return (lane == row * blocks + place) & (row < count)


def send_kernel(own, series_ref, cot_ref, mixing_ref, groups_ref, send_ref, pad_ref, grad_ref):
    channels, steps = mixing_ref.shape[0], series_ref.shape[2]
    blocks = channels // own
    chunk = channels if channels <= 512 else 256
    zero = jnp.zeros((blocks, LANES), f32)
    for r in range(16 + 4 * (own - 8) // 2, SEND):
        send_ref[pl.ds(r, blocks, stride=SEND), :] = zero
    pad_ref[...] = jnp.zeros_like(pad_ref)
    pad_ref[:, :steps] = series_ref[0]
    for i in range(own):
        send_ref[pl.ds(row_of(i, 0), blocks, stride=SEND), :] = pad_ref[
            blocks * i : blocks * (i + 1), :
        ]
    pad_ref[:, :steps] = cot_ref[0]
    total = None
    for start in range(0, channels, chunk):
        same = same_rows(groups_ref, start, chunk)
        masked = jnp.where(same, mixing_ref[start : start + chunk, :], 0.0)
        high, low = split(masked.T)
        both = jnp.concatenate(split(pad_ref[start : start + chunk, :]), 1)
        out = dot(jnp.concatenate([high, low], 0), both)
        part = out[:channels, :LANES] + out[:channels, LANES:] + out[channels:, :LANES]
        total = part if total is None else total + part
    grad_ref[...] = total
    for i in range(own):
        send_ref[pl.ds(row_of(i, 1), blocks, stride=SEND), :] = grad_ref[
            blocks * i : blocks * (i + 1), :
        ]


def table_kernel(
    own,
    place_ref,
    series_ref,
    cot_ref,
    mixing_ref,
    groups_ref,
    gain_ref,
    bias_ref,
    out_bias_ref,
    mode_in_ref,
    mode_out_ref,
    mode_re_ref,
    mode_im_ref,
    weights_ref,
    endpoint_ref,
    turn_ref,
    scale_ref,
    scale_t_ref,
    later_ref,
    ahead_ref,
    back_ref,
    kernel_ref,
    small_ref,
    own_ref,
    base_ref,
    masked_ref,
    same_ref,
    cot3_ref,
    cot_sum_ref,
    pad_ref,
    turned_ref,
):
    channels, steps = mixing_ref.shape[0], series_ref.shape[2]
    width = ahead_ref.shape[0]
    per = width // LANES
    blocks = channels // own
    turned_ref[...] = jnp.zeros_like(turned_ref)
    turned_ref[:, 0:RANK] = mode_in_ref[...]
    turned_ref[:, RANK : 2 * RANK] = mode_out_ref[...]
    factors = turned_ref[...].T
    high, low = split(factors[0:8])
    out = dot(jnp.concatenate([high, low], 0), weights_ref[...])
    kernel = out[0:8, :width] + out[0:8, width:] + out[8:16, :width]
    kernel_ref[...] = kernel
    mix = jnp.sum(factors[0:8] * endpoint_ref[...], axis=1, keepdims=True)[RANK : 2 * RANK]
    scale = scale_ref[...]
    gain_re, gain_im = mode_re_ref[...], mode_im_ref[...]
    mixed = jnp.concatenate([gain_re, gain_im], 1) * mix
    signed = jnp.concatenate([gain_re, -gain_im], 1) * scale
    sign = jnp.where(lax.broadcasted_iota(jnp.int32, (RANK, 2 * MODES), 1) < MODES, 1.0, -1.0)
    small_ref[...] = jnp.zeros_like(small_ref)
    small_ref[0:RANK, 0 : 2 * MODES] = signed * mix
    small_ref[8 : 8 + RANK, 0 : 2 * MODES] = sign * scale * mix
    small_ref[16 : 16 + RANK, 0 : 2 * MODES] = signed
    turned_ref[...] = jnp.zeros_like(turned_ref)
    turned_ref[0:RANK, 0 : 2 * MODES] = mixed
    columns = turned_ref[0:LANES, :].T[0 : 2 * MODES]
    response = None
    for r in range(RANK):
        term = columns[:, r : r + 1] * kernel[r : r + 1, :]
        response = term if response is None else response + term
    real, imag = response[:MODES], response[MODES:]
    cosine, sine = turn_ref[0:MODES], turn_ref[MODES : 2 * MODES]
    cos_b, sin_b = turn_ref[2 * MODES : 3 * MODES], turn_ref[3 * MODES : 4 * MODES]
    turned = jnp.concatenate([real * cos_b + imag * sin_b, imag * cos_b - real * sin_b], 0)
    rows = jnp.concatenate([turned[:, b * LANES : (b + 1) * LANES] for b in range(per)], 0)
    local, total = scan_lanes(rows, later_ref[...])
    count = 2 * MODES
    run = jnp.zeros((count, LANES), f32)
    suffix = [None] * per
    for b in reversed(range(per)):
        suffix[b] = local[b * count : (b + 1) * count] + run
        run = run + total[b * count : (b + 1) * count]
    scale_t = scale_t_ref[...]
    for b in range(per):
        at = slice(b * LANES, (b + 1) * LANES)
        c, s = cosine[:, at], sine[:, at]
        parts = []
        for value in (suffix[b], run - suffix[b]):
            re, im = value[:MODES], value[MODES:]
            parts += [re * c + im * s, im * c - re * s]
        both = jnp.concatenate(parts, 0)
        high, low = split(both.T)
        ahead_ref[at, 0:LANES] = high
        ahead_ref[at, LANES : 2 * LANES] = low
        high, low = split(both * jnp.concatenate([scale_t, scale_t], 0))
        back_ref[0:LANES, at] = high
        back_ref[LANES : 2 * LANES, at] = low
        back_ref[2 * LANES : 3 * LANES, at] = high
    mine = own_lanes(place_ref[0], channels, channels, own, blocks)
    real_row = lax.broadcasted_iota(jnp.int32, (SLOT, 1), 0) < own
    gain = jnp.sum(jnp.where(mine, gain_ref[...], 0.0), axis=1, keepdims=True)
    gain = jnp.where(real_row, gain, 1.0)
    bias = jnp.sum(jnp.where(mine, bias_ref[...], 0.0), axis=1, keepdims=True)
    own_ref[0:SLOT, :] = jnp.broadcast_to(gain, (SLOT, LANES))
    own_ref[SLOT : 2 * SLOT, :] = jnp.broadcast_to(bias, (SLOT, LANES))
    own_ref[2 * SLOT : 3 * SLOT, :] = jnp.broadcast_to(1.0 / gain, (SLOT, LANES))
    chunk = channels if channels <= 512 else 256
    for start in range(0, channels, chunk):
        at = slice(start, start + chunk)
        same = same_rows(groups_ref, start, chunk)
        high, low = split(jnp.where(same, mixing_ref[at, :], 0.0))
        masked_ref[0, at, :] = high
        masked_ref[1, at, :] = low
        same_ref[at, 0:channels] = jnp.where(same, 1.0, 0.0)
        row = lax.broadcasted_iota(jnp.int32, (chunk, channels), 0) + start
        lane = lax.broadcasted_iota(jnp.int32, (chunk, channels), 1)
        shift = jnp.sum(jnp.where(row == lane, out_bias_ref[...], 0.0), axis=1, keepdims=True)
        base_ref[at, :] = series_ref[0, at, :] + shift
    pad_ref[...] = jnp.zeros_like(pad_ref)
    pad_ref[0:channels, :steps] = cot_ref[0]
    three = thrice(pad_ref[...])
    cot3_ref[...] = three
    cot_sum_ref[...] = dot_nt(jnp.ones((8, 2 * LANES), bf16), three[:, LANES : 3 * LANES])


def normalized(x, blocks, steps, earlier):
    rows = x.shape[0]
    local, total = scan_lanes(jnp.concatenate([x, x * x], 0), earlier)
    first, second = blocks_of(local[:rows]), blocks_of(local[rows:])
    first_all, second_all = blocks_of(total[:rows]), blocks_of(total[rows:])
    run_one = jnp.zeros((SLOT, LANES), f32)
    run_two = jnp.zeros((SLOT, LANES), f32)
    lane = lax.broadcasted_iota(jnp.int32, (SLOT, LANES), 1)
    means, variances, inverses = [], [], []
    for k in range(blocks):
        inverse = 1.0 / (lane + (k * steps + 1 + WINDOW)).astype(f32)
        mean = (first[k] + run_one) * inverse
        means.append(mean)
        variances.append((second[k] + run_two + WINDOW) * inverse - mean * mean + EPSILON)
        inverses.append(inverse)
        run_one = run_one + first_all[k]
        run_two = run_two + second_all[k]
    return means, variances, inverses


def forward_kernel(
    blocks,
    steps,
    recv_ref,
    own_ref,
    ahead_ref,
    from_modes_ref,
    earlier_ref,
    send_ref,
    mean_ref,
    inverse_ref,
    shifted_ref,
):
    windows = blocks * steps // WINDOW
    got = recv_ref[...].reshape(blocks, SEND, LANES)
    x = jnp.concatenate([got[:, 0:8], got[:, 16:24]], 1).reshape(blocks * SLOT, LANES)
    means, variances, unused = normalized(x, blocks, steps, earlier_ref[...])
    gain, bias, over = own_ref[0:SLOT], own_ref[SLOT : 2 * SLOT], own_ref[2 * SLOT : 3 * SLOT]
    normal, spreads = [], []
    for k, series in enumerate(blocks_of(x)):
        at = slice(k * SLOT, (k + 1) * SLOT)
        inverse = lax.rsqrt(variances[k])
        normal.append(gain * ((series - means[k]) * inverse) + bias)
        spreads.append(variances[k] * inverse)
        mean_ref[at, :] = means[k]
        inverse_ref[at, :] = inverse
    spectra = stacked_dot(to_wide(normal, windows), ahead_ref[...])
    zero = jnp.zeros((SLOT, LANES), f32)
    before = jnp.concatenate([zero, spectra[:-SLOT]], 0) if windows > 1 else zero
    lane = lax.broadcasted_iota(jnp.int32, spectra.shape, 1)
    spectra = jnp.where(lane < 2 * MODES, spectra, before)
    recon = dot(thrice(spectra), from_modes_ref[...])
    for k, value in enumerate(to_blocks(recon, windows)):
        at = slice(k * SLOT, (k + 1) * SLOT)
        shifted = (value - bias) * over
        shifted_ref[at, :] = shifted
        send_ref[at, :] = shifted * spreads[k] + means[k]


def backward_kernel(
    own,
    blocks,
    steps,
    place_ref,
    recv_ref,
    own_ref,
    mean_ref,
    inverse_ref,
    shifted_ref,
    back_ref,
    kernel_ref,
    small_ref,
    turn_ref,
    to_modes_ref,
    weights_t_ref,
    earlier_ref,
    later_ref,
    cot_sum_ref,
    part_ref,
    misc_ref,
):
    windows = blocks * steps // WINDOW
    wide = cot_sum_ref.shape[1]
    got = recv_ref[...].reshape(blocks, SEND, LANES)
    x = blocks_of(
        jnp.concatenate([got[:, 0:8], got[:, 16:24]], 1).reshape(blocks * SLOT, LANES)
    )
    tail = pltpu.roll(got[:, 16:24], 6, 1)
    grad = blocks_of(jnp.concatenate([got[:, 8:16], tail], 1).reshape(blocks * SLOT, LANES))
    mean, inverse = blocks_of(mean_ref[...]), blocks_of(inverse_ref[...])
    shifted = blocks_of(shifted_ref[...])
    gain, bias, over = own_ref[0:SLOT], own_ref[SLOT : 2 * SLOT], own_ref[2 * SLOT : 3 * SLOT]
    row = lax.broadcasted_iota(jnp.int32, (SLOT, LANES), 0)
    lane = lax.broadcasted_iota(jnp.int32, (SLOT, LANES), 1)
    held = (row < own) & (lane < steps)
    centered, normal, recon_grad = [], [], []
    for k in range(blocks):
        centered.append((x[k] - mean[k]) * inverse[k])
        normal.append(gain * centered[k] + bias)
        recon_grad.append(jnp.where(held, grad[k] / inverse[k] * over, 0.0))
    waves = stacked_dot(to_wide(recon_grad, windows), to_modes_ref[...])
    zero = jnp.zeros((SLOT, 2 * MODES), f32)
    after = jnp.concatenate([waves[SLOT:], zero], 0) if windows > 1 else zero
    waves = jnp.concatenate([waves, after], 1)
    normal_grad = to_blocks(dot(thrice(waves), back_ref[...]), windows)
    gain_sum = jnp.zeros((SLOT, LANES), f32)
    bias_sum = jnp.zeros((SLOT, LANES), f32)
    scaled, ones, twos = [], [], []
    for k in range(blocks):
        over_q = 1.0 / (lane + (k * steps + 1 + WINDOW)).astype(f32)
        scaled.append(normal_grad[k] * gain * inverse[k])
        gain_sum = gain_sum + jnp.where(
            held, normal_grad[k] * centered[k] - recon_grad[k] * shifted[k], 0.0
        )
        bias_sum = bias_sum + jnp.where(held, normal_grad[k] - recon_grad[k], 0.0)
        spread_grad = grad[k] * shifted[k] - scaled[k] * centered[k]
        mean_grad = grad[k] - scaled[k]
        variance_grad = spread_grad * (0.5 * inverse[k])
        first = (mean_grad - 2.0 * mean[k] * variance_grad) * over_q
        ones.append(jnp.where(held, first, 0.0))
        twos.append(jnp.where(held, variance_grad * over_q, 0.0))
    rows = blocks * SLOT
    local, total = scan_lanes(jnp.concatenate(ones + twos, 0), later_ref[...])
    run_one = jnp.zeros((SLOT, LANES), f32)
    run_two = jnp.zeros((SLOT, LANES), f32)
    for k in reversed(range(blocks)):
        at = slice(k * SLOT, (k + 1) * SLOT)
        there = slice(rows + k * SLOT, rows + (k + 1) * SLOT)
        part_ref[at, :] = (
            scaled[k] + local[at] + run_one + 2.0 * x[k] * (local[there] + run_two)
        )
        run_one = run_one + total[at]
        run_two = run_two + total[there]
    signal = to_wide([jnp.where(held, v, 0.0) for v in normal], windows)
    high, low = split(signal)
    pairs = dot(thrice(waves.T), jnp.concatenate([high, low, high], 0))
    cosine, sine = turn_ref[0:MODES], turn_ref[MODES : 2 * MODES]
    cos_b, sin_b = turn_ref[2 * MODES : 3 * MODES], turn_ref[3 * MODES : 4 * MODES]
    count = 2 * MODES

    def turned(value):
        re, im = value[:MODES], value[MODES:]
        return jnp.concatenate([re * cosine - im * sine, -(re * sine + im * cosine)], 0)

    per = pairs.shape[1] // LANES
    after = turned(pairs[count:])
    left = turned(pairs[:count]) - after
    after_all = jnp.sum(sum(after[:, b * LANES : (b + 1) * LANES] for b in range(per)), 1, keepdims=True)
    rows = jnp.concatenate([left[:, b * LANES : (b + 1) * LANES] for b in range(per)], 0)
    local, total = scan_lanes(rows, earlier_ref[...])
    run = jnp.broadcast_to(after_all, (count, LANES))
    sums = []
    for b in range(per):
        sums.append(local[b * count : (b + 1) * count] + run)
        run = run + total[b * count : (b + 1) * count]
    sums = jnp.concatenate(sums, 1)
    re, im = sums[:MODES], sums[MODES:]
    crossed = jnp.concatenate([re * cos_b + im * sin_b, im * cos_b - re * sin_b], 0)
    high, low = split(crossed)
    kernel_grad = dot(
        thrice_narrow(small_ref[0:8, 0:count]), jnp.concatenate([high, low, high], 0)
    )
    mode_in_grad = stacked_dot(kernel_grad, weights_t_ref[...])
    k_high, k_low = split(kernel_ref[...])
    overlap = dot_nt(
        jnp.concatenate([k_high, k_high, k_low], 1), jnp.concatenate([high, low, high], 1)
    )
    modes = overlap * small_ref[8:16, 0:count]
    mix_grad = jnp.sum(overlap * small_ref[16:24, 0:count], axis=1, keepdims=True)
    misc_ref[...] = jnp.zeros_like(misc_ref)
    misc_ref[0:RANK, :] = mode_in_grad[0:RANK, :LANES]
    misc_ref[RANK : 2 * RANK, :] = mode_in_grad[0:RANK, LANES:]
    misc_ref[8 : 8 + RANK, 0:count] = modes[0:RANK]
    misc_ref[8 : 8 + RANK, count : 2 * count] = jnp.broadcast_to(mix_grad, (8, count))[0:RANK]
    mine = own_lanes(place_ref[0], 0, wide, own, blocks)
    at = 12
    gain_row = jnp.sum(
        jnp.where(mine, jnp.sum(gain_sum, 1, keepdims=True), 0.0), axis=0, keepdims=True
    )
    bias_row = jnp.sum(
        jnp.where(mine, jnp.sum(bias_sum, 1, keepdims=True), 0.0), axis=0, keepdims=True
    )
    for value in (gain_row, bias_row, cot_sum_ref[0:1, :]):
        for j in range(wide // LANES):
            misc_ref[at : at + 1, :] = value[:, j * LANES : (j + 1) * LANES]
            at += 1


def thrice_narrow(value):
    high, low = split(value)
    return jnp.concatenate([high, high, low], 1)


def pieces(channels, devices):
    tiles, rest = channels // LANES, channels % LANES
    each = channels // devices
    rest_rows = channels * rest // LANES
    misc_rows = 12 + 3 * (up(channels, LANES) // LANES)
    extra = up(rest_rows + misc_rows, devices) // devices
    return tiles, rest, each, rest_rows, misc_rows, extra


def mix_kernel(
    own,
    devices,
    recv_ref,
    base_ref,
    masked_ref,
    same_ref,
    cot3_ref,
    misc_ref,
    part_ref,
    out_ref,
    send_ref,
    rest_ref,
    misc_all_ref,
):
    channels, steps = base_ref.shape
    blocks = channels // own
    tiles, rest, each, rest_rows, misc_rows, extra = pieces(channels, devices)
    share = up(tiles * each + extra, 8)
    slot = send_ref.shape[0] // devices
    if rest_ref.shape[0] > channels:
        rest_ref[channels:, :] = jnp.zeros((rest_ref.shape[0] - channels, LANES), f32)
    for i in range(own):
        rest_ref[blocks * i : blocks * (i + 1), :] = recv_ref[pl.ds(i, blocks, stride=SLOT), :]
    high, low = split(rest_ref[...])
    both = jnp.concatenate([high[:channels], low[:channels]], 1)
    three = jnp.concatenate([high, low, high], 1)
    chunk = channels if channels <= 512 else devices
    for start in range(0, channels, chunk):
        at = slice(start, start + chunk)
        out = dot(jnp.concatenate([masked_ref[0, at, :], masked_ref[1, at, :]], 0), both)
        mixed = out[:chunk, :LANES] + out[:chunk, LANES:] + out[chunk:, :LANES]
        out_ref[0, at, :] = base_ref[at, :] + mixed[:, :steps]
        grad = dot_nt(cot3_ref[at, :], three)
        for j in range(tiles):
            lanes = slice(j * LANES, (j + 1) * LANES)
            tile = grad[:, lanes] * same_ref[at, lanes]
            for i in range(chunk // devices):
                send_ref[pl.ds(j * each + start // devices + i, devices, stride=slot), :] = tile[
                    devices * i : devices * (i + 1)
                ]
        if rest:
            lanes = slice(tiles * LANES, tiles * LANES + LANES)
            last = grad[:, lanes]
            last = last * same_ref[at, lanes]
            folded = last[0:rest_rows]
            for g in range(1, LANES // rest):
                folded = folded + pltpu.roll(
                    last[g * rest_rows : (g + 1) * rest_rows], g * rest, 1
                )
            misc_all_ref[0:rest_rows, :] = folded
    misc_all_ref[rest_rows : rest_rows + misc_rows, :] = misc_ref[0:misc_rows, :]
    if misc_all_ref.shape[0] > rest_rows + misc_rows:
        misc_all_ref[rest_rows + misc_rows :, :] = jnp.zeros(
            (misc_all_ref.shape[0] - rest_rows - misc_rows, LANES), f32
        )
    for k in range(extra):
        send_ref[pl.ds(tiles * each + k, devices, stride=slot), :] = misc_all_ref[
            devices * k : devices * (k + 1), :
        ]
    half = own // 2
    for i in range(own):
        to_core, k = i // half, i % half
        send_ref[pl.ds(to_core * slot + share + k, blocks, stride=2 * slot), :] = part_ref[
            pl.ds(i, blocks, stride=SLOT), :
        ]


def sum_kernel(own, devices, share, core_ref, recv_ref, send_ref, mine_ref, theirs_ref):
    slot = recv_ref.shape[0] // devices
    total = recv_ref[0:share, :]
    for s in range(1, devices):
        total = total + recv_ref[s * slot : s * slot + share, :]
    for s in range(devices):
        send_ref[s * share : (s + 1) * share, :] = total
    blocks = devices // 2
    first = core_ref[0] == 0
    for k in range(own // 2):
        even = recv_ref[pl.ds(share + k, blocks, stride=2 * slot), :]
        odd = recv_ref[pl.ds(slot + share + k, blocks, stride=2 * slot), :]
        at = slice(k * blocks, (k + 1) * blocks)
        mine_ref[at, :] = jnp.where(first, even, odd)
        theirs_ref[at, :] = jnp.where(first, odd, even)


def series_kernel(own, core_ref, cot_ref, mine_ref, theirs_ref, out_ref):
    steps = cot_ref.shape[2]
    first = core_ref[0] == 0
    half = mine_ref.shape[0]
    low = jnp.where(first, mine_ref[...], theirs_ref[...])
    high = jnp.where(first, theirs_ref[...], mine_ref[...])
    out_ref[0, 0:half, :] = cot_ref[0, 0:half, :] + low[:, :steps]
    out_ref[0, half : 2 * half, :] = cot_ref[0, half : 2 * half, :] + high[:, :steps]


def spread_kernel(
    devices,
    recv_ref,
    endpoint_ref,
    gain_ref,
    bias_ref,
    mode_in_ref,
    mode_out_ref,
    mode_re_ref,
    mode_im_ref,
    mixing_ref,
    out_bias_ref,
    misc_ref,
    turned_ref,
):
    channels = mixing_ref.shape[0]
    tiles, rest, each, rest_rows, misc_rows, extra = pieces(channels, devices)
    share = recv_ref.shape[0] // devices
    for j in range(tiles):
        for i in range(each):
            mixing_ref[devices * i : devices * (i + 1), j * LANES : (j + 1) * LANES] = recv_ref[
                pl.ds(j * each + i, devices, stride=share), :
            ]
    for k in range(extra):
        misc_ref[devices * k : devices * (k + 1), :] = recv_ref[
            pl.ds(tiles * each + k, devices, stride=share), :
        ]
    if rest:
        folded = misc_ref[0:rest_rows, :]
        for g in range(LANES // rest):
            piece = folded if g == 0 else pltpu.roll(folded, LANES - g * rest, 1)
            mixing_ref[g * rest_rows : (g + 1) * rest_rows, tiles * LANES :] = piece[:, :rest]
    at = rest_rows
    modes = misc_ref[at + 8 : at + 8 + RANK, :]
    mode_re_ref[...] = modes[:, 0:MODES]
    mode_im_ref[...] = modes[:, MODES : 2 * MODES]
    mix_grad = modes[:, 2 * MODES : 2 * MODES + 1]
    turned_ref[...] = jnp.zeros_like(turned_ref)
    turned_ref[0:RANK, 0:LANES] = misc_ref[at : at + RANK, :]
    turned_ref[0:RANK, LANES : 2 * LANES] = misc_ref[at + RANK : at + 2 * RANK, :]
    turned_ref[RANK : 2 * RANK, :] = mix_grad * endpoint_ref[...]
    columns = turned_ref[...].T
    mode_in_ref[...] = columns[:, 0:RANK]
    mode_out_ref[...] = columns[:, RANK : 2 * RANK]
    at += 12
    for ref in (gain_ref, bias_ref, out_bias_ref):
        for start in range(0, channels, LANES):
            size = min(LANES, channels - start)
            ref[:, start : start + size] = misc_ref[at : at + 1, 0:size]
            at += 1


def call(kernel, outs, scratch=(), scalars=0, count=0, cost=None, limit=None):
    vmem = pl.BlockSpec(memory_space=pltpu.VMEM)
    smem = pl.BlockSpec(memory_space=pltpu.SMEM)
    return pl.pallas_call(
        kernel,
        out_shape=tuple(jax.ShapeDtypeStruct(shape, kind) for shape, kind in outs),
        in_specs=[smem] * scalars + [vmem] * count,
        out_specs=tuple(vmem for unused in outs),
        scratch_shapes=[pltpu.VMEM(shape, kind) for shape, kind in scratch],
        compiler_params=pltpu.CompilerParams(vmem_limit_bytes=limit),
        cost_estimate=cost,
    )


def exchange(value, axis, count):
    rows = value.shape[0] // count
    out = lax.all_to_all(
        value.reshape(count, rows, value.shape[1]), axis, split_axis=0, concat_axis=0
    )
    return out.reshape(value.shape)


def body(
    series,
    group_ids,
    rev_gain,
    rev_bias,
    mode_in,
    mode_out,
    mode_re,
    mode_im,
    mixing,
    out_bias,
    cotangent,
):
    samples, channels, steps = series.shape
    blocks = lax.axis_size("seq")
    devices = blocks * lax.axis_size("rep")
    own = channels // blocks
    per = WINDOW // steps
    width = per * LANES
    padded = up(channels, LANES)
    place = lax.axis_index("seq").astype(jnp.int32).reshape(1)
    core = lax.axis_index("rep").astype(jnp.int32).reshape(1)
    const = {name: jnp.asarray(value) for name, value in constants(steps).items()}
    groups = group_ids.reshape(1, channels)
    limit = (16 if channels <= 512 else 56) * 2**20
    run = functools.partial(call, limit=limit)
    busy = pl.CostEstimate(flops=4_000_000_000, bytes_accessed=8_000_000, transcendentals=0)
    brief = pl.CostEstimate(flops=100_000_000, bytes_accessed=1_000_000, transcendentals=0)

    (send,) = run(
        functools.partial(send_kernel, own),
        [((blocks * SEND, LANES), f32)],
        [((channels, LANES), f32)] * 2,
        count=4,
        cost=brief,
    )(series, cotangent, mixing, groups)
    tables = run(
        functools.partial(table_kernel, own),
        [
            ((width, 2 * LANES), bf16),
            ((3 * LANES, width), bf16),
            ((8, width), f32),
            ((24, LANES), f32),
            ((3 * SLOT, LANES), f32),
            ((channels, steps), f32),
            ((2, channels, channels), bf16),
            ((channels, padded), f32),
            ((padded, 3 * LANES), bf16),
            ((8, padded), f32),
        ],
        [((padded, LANES), f32), ((ORDER, LANES), f32)],
        scalars=1,
        count=17,
        cost=busy,
    )(
        place,
        series,
        cotangent,
        mixing,
        groups,
        rev_gain.reshape(1, channels),
        rev_bias.reshape(1, channels),
        out_bias.reshape(1, channels),
        mode_in,
        mode_out,
        mode_re,
        mode_im,
        const["weights"],
        const["endpoint"],
        const["turn"],
        const["scale"],
        const["scale_t"],
        const["later"],
    )
    ahead, back, kernel, small, mine, base, masked, same, cot3, cot_sum = tables
    owned = exchange(send, "seq", blocks)
    rows = blocks * SLOT
    restored, mean, inverse, shifted = run(
        functools.partial(forward_kernel, blocks, steps),
        [((rows, LANES), f32)] * 4,
        count=5,
        cost=brief,
    )(owned, mine, ahead, const["from_modes"], const["earlier"])
    there = exchange(restored, "seq", blocks)
    tiles, rest, each, rest_rows, misc_rows, extra = pieces(channels, devices)
    share = up(tiles * each + extra, 8)
    slot = share + up(own // 2, 8)
    part, misc = run(
        functools.partial(backward_kernel, own, blocks, steps),
        [((rows, LANES), f32), ((up(misc_rows, 8), LANES), f32)],
        scalars=1,
        count=14,
        cost=busy,
    )(
        place,
        owned,
        mine,
        mean,
        inverse,
        shifted,
        back,
        kernel,
        small,
        const["turn"],
        const["to_modes"],
        const["weights_t"],
        const["earlier"],
        const["later"],
        cot_sum,
    )
    layer_out, send = run(
        functools.partial(mix_kernel, own, devices),
        [((1, channels, steps), f32), ((devices * slot, LANES), f32)],
        [((padded, LANES), f32), ((up(extra * devices, 8), LANES), f32)],
        count=7,
        cost=brief,
    )(there, base, masked, same, cot3, misc, part)
    shares = exchange(send, ("seq", "rep"), devices)
    half = own // 2 * blocks
    send, kept, given = run(
        functools.partial(sum_kernel, own, devices, share),
        [((devices * share, LANES), f32), ((half, LANES), f32), ((half, LANES), f32)],
        scalars=1,
        count=1,
        cost=brief,
    )(core, shares)
    sums = exchange(send, ("seq", "rep"), devices)
    given = lax.ppermute(given, "rep", [(0, 1), (1, 0)])
    (series_grad,) = run(
        functools.partial(series_kernel, own),
        [((1, channels, steps), f32)],
        scalars=1,
        count=3,
        cost=brief,
    )(core, cotangent, kept, given)
    outs = run(
        functools.partial(spread_kernel, devices),
        [
            ((1, channels), f32),
            ((1, channels), f32),
            ((ORDER, RANK), f32),
            ((ORDER, RANK), f32),
            ((RANK, MODES), f32),
            ((RANK, MODES), f32),
            ((channels, channels), f32),
            ((1, channels), f32),
        ],
        [((up(extra * devices, 8), LANES), f32), ((LANES, ORDER), f32)],
        count=2,
        cost=brief,
    )(sums, const["endpoint"])
    return (
        layer_out,
        series_grad,
        outs[0].reshape(channels),
        outs[1].reshape(channels),
        outs[2],
        outs[3],
        outs[4],
        outs[5],
        outs[6],
        outs[7].reshape(channels),
    )


def solution(mesh):
    time_split = P("rep", None, "seq")
    in_specs = (time_split,) + (P(),) * 9 + (time_split,)
    out_specs = (time_split, time_split) + (P(),) * 8
    return jax.shard_map(body, mesh=mesh, in_specs=in_specs, out_specs=out_specs, check_vma=False)
```

```python
import functools
import math

import jax
import jax.numpy as jnp
import ml_dtypes
import numpy as np
from jax import lax
from jax.experimental import pallas as pl
from jax.experimental.pallas import tpu as pltpu
from jax.sharding import PartitionSpec as P

ORDER = 256
MODES = 32
RANK = 4
WINDOW = 720
EPSILON = 1e-05

LANES = 128
SLOT = 16
SEND = 24
f32 = jnp.float32
bf16 = jnp.bfloat16


def up(value, multiple):
    return -(-value // multiple) * multiple


def legendre_table():
    one, two = np.float32(1.0), np.float32(2.0)
    lags = np.arange(WINDOW).astype(np.float32)
    points = one - (two * (lags + np.float32(0.5))) * np.float32(1.0 / WINDOW)
    lower, this = np.zeros_like(points), np.ones_like(points)
    rows = []
    for degree in np.arange(ORDER).astype(np.float32):
        rows.append(this)
        upper = ((two * degree + one) * points * this - degree * lower) / (degree + one)
        lower, this = this, upper
    return np.stack(rows)


def in_blocks(values, steps):
    blocks = WINDOW // steps
    framed = np.zeros(values.shape[:-1] + (blocks, LANES))
    framed[..., :steps] = values.reshape(values.shape[:-1] + (blocks, steps))
    return framed.reshape(values.shape[:-1] + (blocks * LANES,))


def halves(values):
    high = values.astype(np.float32).astype(ml_dtypes.bfloat16)
    low = (values - high.astype(np.float64)).astype(ml_dtypes.bfloat16)
    return high, low


def constants(steps):
    legendre = legendre_table()
    degree = np.arange(ORDER).astype(np.float32)
    weights = legendre * ((np.float32(2.0) * degree + np.float32(1.0)) / np.float32(WINDOW))[:, None]
    flipped = in_blocks(weights[:, ::-1], steps)
    high, low = halves(flipped)
    table = {}
    table["weights"] = np.concatenate([high, low], 1)
    table["weights_t"] = np.concatenate([high.T, low.T], 1)
    table["endpoint"] = legendre[:, 0][None, :].astype(np.float32)
    mode = np.arange(MODES)[:, None]
    step = np.arange(WINDOW)[None, :]
    angle = 2.0 * math.pi / WINDOW * (mode * step % WINDOW)
    cosine, sine = np.cos(angle), np.sin(angle)
    back = 2.0 * math.pi / WINDOW * (mode * (WINDOW - 1 - step) % WINDOW)
    table["turn"] = np.concatenate(
        [in_blocks(v, steps) for v in (cosine, sine, np.cos(back), np.sin(back))]
    ).astype(np.float32)
    scale = np.where(np.arange(MODES) == 0, 1.0, 2.0) / WINDOW
    table["scale"] = np.tile(scale, 4)[None, :].astype(np.float32)
    high, low = halves(in_blocks(np.concatenate([cosine, -sine]), steps))
    table["to_modes"] = np.concatenate([high.T, low.T], 1)
    wave = in_blocks(np.concatenate([scale[:, None] * cosine, -scale[:, None] * sine]), steps)
    table["from_modes"] = np.concatenate(halves(wave), 1)
    lane = np.arange(LANES)
    upper = (lane[:, None] <= lane[None, :]).astype(np.float32)
    ones = np.ones((LANES, LANES), np.float32)
    for name, part in (("earlier", upper), ("later", upper.T)):
        both = np.concatenate([part, ones], 1)
        table[name] = np.concatenate([both, both]).astype(ml_dtypes.bfloat16)
    return table


def split(value):
    high = value.astype(bf16)
    return high, (value - high.astype(f32)).astype(bf16)


def dot(a, b):
    return lax.dot_general(a, b, (((1,), (0,)), ((), ())), preferred_element_type=f32)


def dot_nt(a, b):
    return lax.dot_general(a, b, (((1,), (1,)), ((), ())), preferred_element_type=f32)


def stacked_dot(value, table):
    rows, width = value.shape[0], table.shape[1] // 2
    high, low = split(value)
    out = dot(jnp.concatenate([high, low], 0), table)
    return out[:rows, :width] + out[:rows, width:] + out[rows:, :width]


def scan_lanes(value, table):
    high, low = split(value)
    out = dot(jnp.concatenate([high, low], 1), table)
    return out[:, :LANES], out[:, LANES:]


def row_of(i, kind):
    return 8 * kind + i if i < 8 else 16 + (i - 8) + 2 * kind


def order_mask(blocks):
    return blocks * 11 // 16


def to_wide(blocks, windows):
    per = len(blocks) // windows
    return jnp.concatenate(
        [jnp.concatenate(blocks[w * per : (w + 1) * per], 1) for w in range(windows)], 0
    )


def to_blocks(wide, windows):
    per = wide.shape[1] // LANES
    return [
        wide[w * SLOT : (w + 1) * SLOT, b * LANES : (b + 1) * LANES]
        for w in range(windows)
        for b in range(per)
    ]


def fetch(pairs, sems):
    copies = [pltpu.make_async_copy(a, b, sems.at[k]) for k, (a, b) in enumerate(pairs)]
    for copy in copies:
        copy.start()

    def ready(*which):
        for k in which:
            copies[k].wait()

    return ready


def blocks_of(value):
    return [value[k * SLOT : (k + 1) * SLOT] for k in range(value.shape[0] // SLOT)]


def same_rows(groups_ref, start, rows):
    channels = groups_ref.shape[1]
    ids = groups_ref[...].astype(f32)
    row = lax.broadcasted_iota(jnp.int32, (rows, channels), 0) + start
    lane = lax.broadcasted_iota(jnp.int32, (rows, channels), 1)
    column = jnp.sum(jnp.where(row == lane, ids, 0.0), axis=1, keepdims=True)
    return column == ids


def own_lanes(place, width, count, blocks):
    row = lax.broadcasted_iota(jnp.int32, (SLOT, width), 0)
    lane = lax.broadcasted_iota(jnp.int32, (SLOT, width), 1)
    return (lane == row * blocks + place) & (row < count)


def send_kernel(
    own,
    series_hbm,
    cot_hbm,
    mixing_hbm,
    groups_hbm,
    send_ref,
    grad_ref,
    series_ref,
    cot_ref,
    mixing_ref,
    groups_ref,
    pad_ref,
    sems,
):
    channels, steps = cot_ref.shape[1:]
    blocks = channels // own
    ready = fetch(
        [
            (groups_hbm, groups_ref),
            (mixing_hbm, mixing_ref),
            (cot_hbm, cot_ref),
            (series_hbm, series_ref),
        ],
        sems,
    )
    zero = jnp.zeros((blocks, LANES), f32)
    for r in range(row_of(own - 1, 1) + 1, SEND):
        send_ref[pl.ds(r, blocks, stride=SEND), :] = zero
    pad_ref[...] = jnp.zeros_like(pad_ref)
    ready(0, 1, 2)
    pad_ref[:, :steps] = cot_ref[0]
    chunk = channels if channels <= 512 else 256
    total = None
    for start in range(0, channels, chunk):
        same = same_rows(groups_ref, start, chunk)
        masked = jnp.where(same, mixing_ref[start : start + chunk, :], 0.0)
        high, low = split(masked.T)
        both = jnp.concatenate(split(pad_ref[start : start + chunk, :]), 1)
        out = dot(jnp.concatenate([high, low], 0), both)
        part = out[:channels, :LANES] + out[:channels, LANES:] + out[channels:, :LANES]
        total = part if total is None else total + part
    grad_ref[...] = total
    ready(3)
    pad_ref[:, :steps] = series_ref[0]
    for i in range(own):
        at = slice(blocks * i, blocks * (i + 1))
        send_ref[pl.ds(row_of(i, 0), blocks, stride=SEND), :] = pad_ref[at, :]
        send_ref[pl.ds(row_of(i, 1), blocks, stride=SEND), :] = grad_ref[at, :]


def table_kernel(
    own,
    block_ref,
    cot_hbm,
    mixing_hbm,
    groups_hbm,
    gain_hbm,
    bias_hbm,
    out_bias_hbm,
    mode_in_hbm,
    mode_out_hbm,
    mode_re_hbm,
    mode_im_hbm,
    weights_hbm,
    endpoint_hbm,
    turn_hbm,
    scale_hbm,
    later_hbm,
    ahead_ref,
    lines_ref,
    own_ref,
    columns_ref,
    masked_ref,
    same_ref,
    cot3_ref,
    cot_sum_ref,
    cot_ref,
    mixing_ref,
    groups_ref,
    gain_ref,
    bias_ref,
    out_bias_ref,
    mode_in_ref,
    mode_out_ref,
    mode_re_ref,
    mode_im_ref,
    weights_ref,
    endpoint_ref,
    turn_ref,
    scale_ref,
    later_ref,
    pad_ref,
    turned_ref,
    sems,
):
    ready = fetch(
        [
            (mode_in_hbm, mode_in_ref),
            (mode_out_hbm, mode_out_ref),
            (endpoint_hbm, endpoint_ref),
            (weights_hbm, weights_ref),
            (mode_re_hbm, mode_re_ref),
            (mode_im_hbm, mode_im_ref),
            (scale_hbm, scale_ref),
            (turn_hbm, turn_ref),
            (later_hbm, later_ref),
            (groups_hbm, groups_ref),
            (mixing_hbm, mixing_ref),
            (cot_hbm, cot_ref),
            (gain_hbm, gain_ref),
            (bias_hbm, bias_ref),
            (out_bias_hbm, out_bias_ref),
        ],
        sems,
    )
    channels, steps = cot_ref.shape[1:]
    width = ahead_ref.shape[0]
    per = width // LANES
    blocks = channels // own
    count = 2 * MODES
    lines_ref[...] = jnp.zeros_like(lines_ref)
    turned_ref[...] = jnp.zeros_like(turned_ref)
    pad_ref[...] = jnp.zeros_like(pad_ref)
    ready(0, 1, 2, 3)
    high, low = split(mode_in_ref[...])
    out = dot(jnp.concatenate([high, low], 0), weights_ref[...])
    kernel = out[:RANK, :width] + out[:RANK, width:] + out[RANK:, :width]
    lines_ref[0:RANK, :] = kernel
    mix = jnp.sum(mode_out_ref[...] * endpoint_ref[...], axis=1, keepdims=True)
    ready(4, 5, 6)
    scale = scale_ref[:, 0:count]
    gain_re, gain_im = mode_re_ref[...], mode_im_ref[...]
    signed = jnp.concatenate([gain_re, -gain_im], 1) * scale
    sign = jnp.where(lax.broadcasted_iota(jnp.int32, (RANK, count), 1) < MODES, 1.0, -1.0)
    lines_ref[8 : 8 + RANK, 0:count] = signed * mix
    lines_ref[16 : 16 + RANK, 0:count] = sign * scale * mix
    lines_ref[24 : 24 + RANK, 0:count] = signed
    lines_ref[28:29, 0:LANES] = scale_ref[...]
    turned_ref[0:RANK, 0:count] = jnp.concatenate([gain_re, gain_im], 1) * mix
    columns = turned_ref[...].T[0:count]
    response = None
    for r in range(RANK):
        term = columns[:, r : r + 1] * kernel[r : r + 1, :]
        response = term if response is None else response + term
    ready(7, 8)
    real, imag = response[:MODES], response[MODES:]
    cosine, sine = turn_ref[0:MODES], turn_ref[MODES : 2 * MODES]
    cos_b, sin_b = turn_ref[2 * MODES : 3 * MODES], turn_ref[3 * MODES : 4 * MODES]
    turned = jnp.concatenate([real * cos_b + imag * sin_b, imag * cos_b - real * sin_b], 0)
    rows = jnp.concatenate([turned[:, b * LANES : (b + 1) * LANES] for b in range(per)], 0)
    local, total = scan_lanes(rows, later_ref[...])
    run = jnp.zeros((count, LANES), f32)
    suffix = [None] * per
    for b in reversed(range(per)):
        suffix[b] = local[b * count : (b + 1) * count] + run
        run = run + total[b * count : (b + 1) * count]
    for b in range(per):
        at = slice(b * LANES, (b + 1) * LANES)
        c, s = cosine[:, at], sine[:, at]
        parts = []
        for value in (suffix[b], run - suffix[b]):
            re, im = value[:MODES], value[MODES:]
            parts += [re * c + im * s, im * c - re * s]
        high, low = split(jnp.concatenate(parts, 0).T)
        ahead_ref[at, 0:LANES] = high
        ahead_ref[at, LANES : 2 * LANES] = low
    ready(9, 10, 11, 12, 13, 14)
    chunk = channels if channels <= 512 else 256
    for start in range(0, channels, chunk):
        at = slice(start, start + chunk)
        same = same_rows(groups_ref, start, chunk)
        high, low = split(jnp.where(same, mixing_ref[at, :], 0.0))
        masked_ref[0, at, :] = high
        masked_ref[1, at, :] = low
        same_ref[at, 0:channels] = jnp.where(same, 1.0, 0.0)
        row = lax.broadcasted_iota(jnp.int32, (chunk, channels), 0) + start
        lane = lax.broadcasted_iota(jnp.int32, (chunk, channels), 1)
        for k, ref in enumerate((gain_ref, bias_ref, out_bias_ref)):
            columns_ref[at, k : k + 1] = jnp.sum(
                jnp.where(row == lane, ref[...], 0.0), axis=1, keepdims=True
            )
    mine = own_lanes(block_ref[0] ^ order_mask(blocks), channels, own, blocks)
    gain = jnp.sum(jnp.where(mine, gain_ref[...], 0.0), axis=1, keepdims=True)
    gain = jnp.where(lax.broadcasted_iota(jnp.int32, (SLOT, 1), 0) < own, gain, 1.0)
    bias = jnp.sum(jnp.where(mine, bias_ref[...], 0.0), axis=1, keepdims=True)
    own_ref[0:SLOT, :] = jnp.broadcast_to(gain, (SLOT, LANES))
    own_ref[SLOT : 2 * SLOT, :] = jnp.broadcast_to(bias, (SLOT, LANES))
    own_ref[2 * SLOT : 3 * SLOT, :] = jnp.broadcast_to(1.0 / gain, (SLOT, LANES))
    pad_ref[0:channels, :steps] = cot_ref[0]
    high, low = split(pad_ref[...])
    cot3_ref[...] = jnp.concatenate([high, high, low], 1)
    cot_sum_ref[...] = dot_nt(
        jnp.ones((8, 2 * LANES), bf16), jnp.concatenate([high, low], 1)
    )


def normalized(x, blocks, steps, earlier):
    rows = x.shape[0]
    local, total = scan_lanes(jnp.concatenate([x, x * x], 0), earlier)
    first, second = blocks_of(local[:rows]), blocks_of(local[rows:])
    first_all, second_all = blocks_of(total[:rows]), blocks_of(total[rows:])
    run_one = jnp.zeros((SLOT, LANES), f32)
    run_two = jnp.zeros((SLOT, LANES), f32)
    lane = lax.broadcasted_iota(jnp.int32, (SLOT, LANES), 1)
    found = []
    for k in range(blocks):
        inverse = 1.0 / (lane + (k * steps + 1 + WINDOW)).astype(f32)
        mean = (first[k] + run_one) * inverse
        variance = (second[k] + run_two + WINDOW) * inverse - mean * mean + EPSILON
        found.append((mean, variance, run_one, run_two))
        run_one = run_one + first_all[k]
        run_two = run_two + second_all[k]
    return found


def owned(recv_ref, blocks):
    got = recv_ref[...].reshape(blocks, SEND, LANES)
    tail = pltpu.roll(got[:, 16:24], 6, 1)
    x = jnp.concatenate([got[:, 0:8], got[:, 16:24]], 1)
    grad = jnp.concatenate([got[:, 8:16], tail], 1)
    mask = order_mask(blocks)
    return [x[b ^ mask] for b in range(blocks)], [grad[b ^ mask] for b in range(blocks)]


def forward_kernel(
    own,
    blocks,
    steps,
    recv_ref,
    own_ref,
    ahead_ref,
    from_modes_ref,
    to_modes_ref,
    earlier_ref,
    send_ref,
    mean_ref,
    inverse_ref,
    shifted_ref,
    waves_ref,
):
    windows = blocks * steps // WINDOW
    width = ahead_ref.shape[0]
    x, grad = owned(recv_ref, blocks)
    found = normalized(jnp.concatenate(x, 0), blocks, steps, earlier_ref[...])
    gain, bias, over = own_ref[0:SLOT], own_ref[SLOT : 2 * SLOT], own_ref[2 * SLOT : 3 * SLOT]
    row = lax.broadcasted_iota(jnp.int32, (SLOT, LANES), 0)
    lane = lax.broadcasted_iota(jnp.int32, (SLOT, LANES), 1)
    held = (row < own) & (lane < steps)
    normal, spreads, recon_grad = [], [], []
    for k in range(blocks):
        at = slice(k * SLOT, (k + 1) * SLOT)
        mean, variance = found[k][:2]
        inverse = lax.rsqrt(variance)
        spread = variance * inverse
        normal.append(gain * ((x[k] - mean) * inverse) + bias)
        spreads.append(spread)
        recon_grad.append(jnp.where(held, grad[k] * spread * over, 0.0))
        mean_ref[at, :] = mean
        inverse_ref[at, :] = inverse
    spectra = stacked_dot(to_wide(normal, windows), ahead_ref[...])
    waves = stacked_dot(to_wide(recon_grad, windows), to_modes_ref[...])
    count = 2 * MODES
    current, before = spectra[:, :count], spectra[:, count:]
    zero = jnp.zeros((SLOT, count), f32)
    after = zero
    if windows > 1:
        current = current + jnp.concatenate([zero, before[:-SLOT]], 0)
        after = jnp.concatenate([waves[SLOT:], zero], 0)
    recon = stacked_dot(current, from_modes_ref[...])
    waves = jnp.concatenate([waves, after], 1)
    waves_ref[...] = waves
    recon = to_blocks(recon, windows)
    row = row[0:8]
    per = blocks // windows
    for b in range(blocks):
        at = slice(b * SLOT, (b + 1) * SLOT)
        mean, variance, run_one, run_two = found[b]
        shifted = (recon[b] - bias) * over
        shifted_ref[at, :] = shifted
        back = shifted * spreads[b] + mean
        back = jnp.where(lane == steps, run_one, jnp.where(lane == steps + 1, run_two, back))
        wave = waves[b // per * SLOT : (b // per + 1) * SLOT]
        slot = (b ^ order_mask(blocks)) * SEND
        send_ref[slot : slot + 8, :] = back[0:8]
        send_ref[slot + 8 : slot + 16, :] = wave[0:8]
        send_ref[slot + 16 : slot + 24, :] = jnp.where(
            row < 2, back[8:16], pltpu.roll(wave[8:16], 2, 0)
        )


def backward_kernel(
    own,
    blocks,
    steps,
    block_ref,
    recv_ref,
    own_ref,
    mean_ref,
    inverse_ref,
    shifted_ref,
    waves_ref,
    ahead_ref,
    lines_ref,
    cot_sum_ref,
    turn_hbm,
    weights_t_hbm,
    earlier_hbm,
    misc_ref,
    starts_ref,
    turn_ref,
    weights_t_ref,
    earlier_ref,
    sems,
):
    ready = fetch(
        [(turn_hbm, turn_ref), (earlier_hbm, earlier_ref), (weights_t_hbm, weights_t_ref)], sems
    )
    windows = blocks * steps // WINDOW
    wide = cot_sum_ref.shape[1]
    count = 2 * MODES
    x, grad = owned(recv_ref, blocks)
    mean, inverse = blocks_of(mean_ref[...]), blocks_of(inverse_ref[...])
    shifted = blocks_of(shifted_ref[...])
    gain, bias, over = own_ref[0:SLOT], own_ref[SLOT : 2 * SLOT], own_ref[2 * SLOT : 3 * SLOT]
    row = lax.broadcasted_iota(jnp.int32, (SLOT, LANES), 0)
    lane = lax.broadcasted_iota(jnp.int32, (SLOT, LANES), 1)
    held = (row < own) & (lane < steps)
    waves = waves_ref[...]
    normal_grad = to_blocks(convolved_back(waves * lines_ref[28:29, 0:LANES], ahead_ref[...]), windows)
    gain_sum = jnp.zeros((SLOT, LANES), f32)
    bias_sum = jnp.zeros((SLOT, LANES), f32)
    normal, ones, twos = [], [], []
    for k in range(blocks):
        over_q = 1.0 / (lane + (k * steps + 1 + WINDOW)).astype(f32)
        centered = (x[k] - mean[k]) * inverse[k]
        normal.append(jnp.where(held, gain * centered + bias, 0.0))
        recon_grad = grad[k] / inverse[k] * over
        gain_sum = gain_sum + normal_grad[k] * centered - recon_grad * shifted[k]
        bias_sum = bias_sum + normal_grad[k] - recon_grad
        first, second, unused = statistics(
            grad[k], shifted[k], normal_grad[k] * gain * inverse[k], centered, mean[k], inverse[k], over_q
        )
        ones.append(jnp.where(held, first, 0.0))
        twos.append(jnp.where(held, second, 0.0))
    gain_sum, bias_sum = jnp.where(held, gain_sum, 0.0), jnp.where(held, bias_sum, 0.0)
    run_one = jnp.zeros((SLOT, LANES), f32)
    run_two = jnp.zeros((SLOT, LANES), f32)
    spots = (lane == row) & (row < own)
    for k in reversed(range(blocks)):
        both = jnp.where(spots, jnp.sum(run_one, 1, keepdims=True), 0.0)
        both = both + pltpu.roll(
            jnp.where(spots, jnp.sum(run_two, 1, keepdims=True), 0.0), SLOT, 1
        )
        starts_ref[k : k + 1, :] = jnp.sum(both, 0, keepdims=True)
        run_one = run_one + ones[k]
        run_two = run_two + twos[k]
    signal = to_wide(normal, windows)
    high, low = split(signal)
    w_high, w_low = split(waves.T)
    pairs = dot(
        jnp.concatenate([w_high, w_high, w_low], 1), jnp.concatenate([high, low, high], 0)
    )
    ready(0)
    cosine, sine = turn_ref[0:MODES], turn_ref[MODES : 2 * MODES]
    cos_b, sin_b = turn_ref[2 * MODES : 3 * MODES], turn_ref[3 * MODES : 4 * MODES]

    def turned(value):
        re, im = value[:MODES], value[MODES:]
        return jnp.concatenate([re * cosine - im * sine, -(re * sine + im * cosine)], 0)

    per = pairs.shape[1] // LANES
    after = turned(pairs[count:])
    left = turned(pairs[:count]) - after
    after = sum(after[:, b * LANES : (b + 1) * LANES] for b in range(per))
    ready(1)
    local, total = scan_lanes(
        jnp.concatenate([left[:, b * LANES : (b + 1) * LANES] for b in range(per)], 0),
        earlier_ref[...],
    )
    run = jnp.broadcast_to(jnp.sum(after, 1, keepdims=True), (count, LANES))
    sums = []
    for b in range(per):
        sums.append(local[b * count : (b + 1) * count] + run)
        run = run + total[b * count : (b + 1) * count]
    sums = jnp.concatenate(sums, 1)
    re, im = sums[:MODES], sums[MODES:]
    crossed = jnp.concatenate([re * cos_b + im * sin_b, im * cos_b - re * sin_b], 0)
    high, low = split(crossed)
    s_high, s_low = split(lines_ref[8:16, 0:count])
    kernel_grad = dot(
        jnp.concatenate([s_high, s_high, s_low], 1), jnp.concatenate([high, low, high], 0)
    )
    k_high, k_low = split(lines_ref[0:8, :])
    overlap = dot_nt(
        jnp.concatenate([k_high, k_high, k_low], 1), jnp.concatenate([high, low, high], 1)
    )
    modes = overlap * lines_ref[16:24, 0:count]
    mix_grad = jnp.sum(overlap * lines_ref[24:32, 0:count], axis=1, keepdims=True)
    ready(2)
    mode_in_grad = stacked_dot(kernel_grad, weights_t_ref[...])
    misc_ref[...] = jnp.zeros_like(misc_ref)
    misc_ref[0:RANK, :] = mode_in_grad[0:RANK, :LANES]
    misc_ref[RANK : 2 * RANK, :] = mode_in_grad[0:RANK, LANES:]
    misc_ref[8 : 8 + RANK, 0:count] = modes[0:RANK]
    misc_ref[8 : 8 + RANK, count : 2 * count] = jnp.broadcast_to(mix_grad, (8, count))[0:RANK]
    mine = own_lanes(block_ref[0] ^ order_mask(blocks), wide, own, blocks)
    at = 12
    gain_row = jnp.sum(
        jnp.where(mine, jnp.sum(gain_sum, 1, keepdims=True), 0.0), axis=0, keepdims=True
    )
    bias_row = jnp.sum(
        jnp.where(mine, jnp.sum(bias_sum, 1, keepdims=True), 0.0), axis=0, keepdims=True
    )
    for value in (gain_row, bias_row, cot_sum_ref[0:1, :]):
        for j in range(wide // LANES):
            misc_ref[at : at + 1, :] = value[:, j * LANES : (j + 1) * LANES]
            at += 1


def convolved_back(waves, ahead):
    rows = waves.shape[0]
    high, low = split(waves)
    out = dot_nt(jnp.concatenate([high, low], 0), ahead[:, :LANES])
    return out[:rows] + out[rows:] + dot_nt(high, ahead[:, LANES:])


def statistics(grad, shifted, scaled, centered, mean, inverse, over_q):
    variance_grad = (grad * shifted - scaled * centered) * (0.5 * inverse)
    first = (grad - scaled - 2.0 * mean * variance_grad) * over_q
    return first, variance_grad * over_q, scaled


def pieces(channels, devices):
    tiles, rest = channels // LANES, channels % LANES
    each = channels // devices
    rest_rows = channels * rest // LANES
    misc_rows = 12 + 3 * (up(channels, LANES) // LANES)
    extra = up(rest_rows + misc_rows, devices) // devices
    return tiles, rest, each, rest_rows, misc_rows, extra


def gathered(recv_ref, kind, own, blocks, dense_ref):
    for i in range(own):
        dense_ref[blocks * i : blocks * (i + 1), :] = recv_ref[
            pl.ds(row_of(i, kind), blocks, stride=SEND), :
        ]


def mix_kernel(
    own,
    devices,
    recv_ref,
    same_ref,
    cot3_ref,
    misc_ref,
    starts_ref,
    send_ref,
    dense_ref,
    misc_all_ref,
):
    channels = same_ref.shape[0]
    blocks = channels // own
    tiles, rest, each, rest_rows, misc_rows, extra = pieces(channels, devices)
    slot = send_ref.shape[0] // devices
    if dense_ref.shape[0] > channels:
        dense_ref[channels:, :] = jnp.zeros((dense_ref.shape[0] - channels, LANES), f32)
    gathered(recv_ref, 0, own, blocks, dense_ref)
    high, low = split(dense_ref[...])
    three = jnp.concatenate([high, low, high], 1)
    chunk = channels if channels <= 512 else devices
    for start in range(0, channels, chunk):
        at = slice(start, start + chunk)
        grad = dot_nt(cot3_ref[at, :], three)
        for j in range(tiles):
            lanes = slice(j * LANES, (j + 1) * LANES)
            tile = grad[:, lanes] * same_ref[at, lanes]
            for i in range(chunk // devices):
                send_ref[pl.ds(j * each + start // devices + i, devices, stride=slot), :] = tile[
                    devices * i : devices * (i + 1)
                ]
        if rest:
            lanes = slice(tiles * LANES, tiles * LANES + LANES)
            last = grad[:, lanes] * same_ref[at, lanes]
            folded = last[0:rest_rows]
            for g in range(1, LANES // rest):
                folded = folded + pltpu.roll(
                    last[g * rest_rows : (g + 1) * rest_rows], g * rest, 1
                )
            misc_all_ref[0:rest_rows, :] = folded
    end = rest_rows + misc_rows
    misc_all_ref[rest_rows:end, :] = misc_ref[0:misc_rows, :]
    if misc_all_ref.shape[0] > end:
        misc_all_ref[end:, :] = jnp.zeros((misc_all_ref.shape[0] - end, LANES), f32)
    for k in range(extra):
        send_ref[pl.ds(tiles * each + k, devices, stride=slot), :] = misc_all_ref[
            devices * k : devices * (k + 1), :
        ]
    for k in range(tiles * each + extra, slot - 1):
        send_ref[pl.ds(k, devices, stride=slot), :] = jnp.zeros((devices, LANES), f32)
    for r in range(2):
        send_ref[pl.ds(r * slot + slot - 1, blocks, stride=2 * slot), :] = starts_ref[...]


def steps_kernel(
    own,
    block_ref,
    recv_ref,
    grad_ref,
    ahead_ref,
    lines_ref,
    columns_ref,
    masked_ref,
    series_hbm,
    cot_hbm,
    earlier_hbm,
    later_hbm,
    out_ref,
    part_ref,
    series_ref,
    cot_ref,
    earlier_ref,
    later_ref,
    dense_ref,
    waves_ref,
    pad_ref,
    sems,
):
    ready = fetch(
        [
            (series_hbm, series_ref),
            (cot_hbm, cot_ref),
            (earlier_hbm, earlier_ref),
            (later_hbm, later_ref),
        ],
        sems,
    )
    channels, steps = series_ref.shape[1:]
    blocks = channels // own
    per = ahead_ref.shape[0] // LANES
    block = block_ref[0]
    gathered(recv_ref, 0, own, blocks, dense_ref)
    gathered(recv_ref, 1, own, blocks, waves_ref)
    pad_ref[...] = jnp.zeros_like(pad_ref)
    gain, bias, shift = (columns_ref[:, k : k + 1] for k in range(3))
    restored = dense_ref[...]
    both = jnp.concatenate(split(restored), 1)
    at = pl.ds(pl.multiple_of(block % per * LANES, LANES), LANES)
    normal_grad = convolved_back(waves_ref[...] * lines_ref[28:29, 0:LANES], ahead_ref[at, :])
    ready(0)
    pad_ref[:, :steps] = series_ref[0]
    chunk = channels if channels <= 512 else 256
    for start in range(0, channels, chunk):
        at = slice(start, start + chunk)
        out = dot(jnp.concatenate([masked_ref[0, at, :], masked_ref[1, at, :]], 0), both)
        mixed = out[:chunk, :LANES] + out[:chunk, LANES:] + out[chunk:, :LANES]
        out_ref[0, at, :] = (pad_ref[at, :] + mixed + shift[at])[:, :steps]
    x = pad_ref[...]
    ready(2)
    local, unused = scan_lanes(jnp.concatenate([x, x * x], 0), earlier_ref[...])
    lane = lax.broadcasted_iota(jnp.int32, (channels, LANES), 1)
    over_q = 1.0 / (lane + (block * steps + 1 + WINDOW)).astype(f32)
    mean = (local[:channels] + restored[:, steps : steps + 1]) * over_q
    variance = (local[channels:] + restored[:, steps + 1 : steps + 2] + WINDOW) * over_q
    inverse = lax.rsqrt(variance - mean * mean + EPSILON)
    centered = (x - mean) * inverse
    first, second, scaled = statistics(
        grad_ref[...],
        (restored - mean) * inverse,
        normal_grad * gain * inverse,
        centered,
        mean,
        inverse,
        over_q,
    )
    held = lane < steps
    ready(3)
    local, unused = scan_lanes(
        jnp.concatenate([jnp.where(held, first, 0.0), jnp.where(held, second, 0.0)], 0),
        later_ref[...],
    )
    part = scaled + local[:channels] + 2.0 * x * local[channels:]
    ready(1)
    part_ref[...] = cot_ref[0] + part[:, :steps]


def sum_kernel(devices, recv_ref, send_ref):
    slot = recv_ref.shape[0] // devices
    total = recv_ref[0:slot, :]
    for s in range(1, devices):
        total = total + recv_ref[s * slot : (s + 1) * slot, :]
    for s in range(devices):
        send_ref[s * slot : (s + 1) * slot, :] = total


def series_kernel(own, devices, core_ref, recv_ref, part_ref, series_hbm, out_ref, series_ref, sems):
    ready = fetch([(series_hbm, series_ref)], sems)
    channels, steps = part_ref.shape
    blocks = channels // own
    slot = recv_ref.shape[0] // devices
    mask = order_mask(blocks)
    first = core_ref[0] == 0
    rows = []
    for s in range(blocks):
        at = (s ^ mask) * 2 * slot + slot - 1
        rows.append(
            jnp.where(first, recv_ref[at : at + 1, :], recv_ref[at + slot : at + slot + 1, :])
        )
    sums = jnp.concatenate(rows, 0)
    ready(0)
    for i in range(own):
        at = slice(blocks * i, blocks * (i + 1))
        out_ref[0, at, :] = part_ref[at, :] + (
            sums[:, i : i + 1] + 2.0 * series_ref[0, at, :] * sums[:, SLOT + i : SLOT + i + 1]
        )


def spread_kernel(
    devices,
    recv_ref,
    endpoint_ref,
    gain_ref,
    bias_ref,
    mode_in_ref,
    mode_out_ref,
    mode_re_ref,
    mode_im_ref,
    mixing_ref,
    out_bias_ref,
    misc_ref,
):
    channels = mixing_ref.shape[0]
    tiles, rest, each, rest_rows, misc_rows, extra = pieces(channels, devices)
    slot = recv_ref.shape[0] // devices
    for j in range(tiles):
        for i in range(each):
            mixing_ref[devices * i : devices * (i + 1), j * LANES : (j + 1) * LANES] = recv_ref[
                pl.ds(j * each + i, devices, stride=slot), :
            ]
    for k in range(extra):
        misc_ref[devices * k : devices * (k + 1), :] = recv_ref[
            pl.ds(tiles * each + k, devices, stride=slot), :
        ]
    if rest:
        folded = misc_ref[0:rest_rows, :]
        for g in range(LANES // rest):
            piece = folded if g == 0 else pltpu.roll(folded, LANES - g * rest, 1)
            mixing_ref[g * rest_rows : (g + 1) * rest_rows, tiles * LANES :] = piece[:, :rest]
    at = rest_rows
    mode_in_ref[:, 0:LANES] = misc_ref[at : at + RANK, :]
    mode_in_ref[:, LANES : 2 * LANES] = misc_ref[at + RANK : at + 2 * RANK, :]
    modes = misc_ref[at + 8 : at + 8 + RANK, :]
    mode_re_ref[...] = modes[:, 0:MODES]
    mode_im_ref[...] = modes[:, MODES : 2 * MODES]
    mode_out_ref[...] = modes[:, 2 * MODES : 2 * MODES + 1] * endpoint_ref[...]
    at += 12
    for ref in (gain_ref, bias_ref, out_bias_ref):
        for start in range(0, channels, LANES):
            size = min(LANES, channels - start)
            ref[:, start : start + size] = misc_ref[at : at + 1, 0:size]
            at += 1


def call(kernel, outs, smem=(), vmem=(), hbm=(), scratch=(), cost=None, limit=None):
    in_vmem = pl.BlockSpec(memory_space=pltpu.VMEM)
    in_smem = pl.BlockSpec(memory_space=pltpu.SMEM)
    in_hbm = pl.BlockSpec(memory_space=pltpu.HBM)
    held = [pltpu.VMEM(a.shape, a.dtype) for a in hbm] + list(scratch)
    if hbm:
        held.append(pltpu.SemaphoreType.DMA((len(hbm),)))
    hbm = [pltpu.with_memory_space_constraint(a, pltpu.HBM) for a in hbm]
    return pl.pallas_call(
        kernel,
        out_shape=tuple(jax.ShapeDtypeStruct(shape, kind) for shape, kind in outs),
        in_specs=[in_smem] * len(smem) + [in_vmem] * len(vmem) + [in_hbm] * len(hbm),
        out_specs=tuple(in_vmem for unused in outs),
        scratch_shapes=held,
        compiler_params=pltpu.CompilerParams(vmem_limit_bytes=limit),
        cost_estimate=cost,
    )(*smem, *vmem, *hbm)


def exchange(value, axis, count, order=None):
    rows = value.shape[0] // count
    out = lax.all_to_all(
        value.reshape(count, rows, value.shape[1]),
        axis,
        split_axis=0,
        concat_axis=0,
        axis_index_groups=order,
    )
    return out.reshape(value.shape)


def body(
    series,
    group_ids,
    rev_gain,
    rev_bias,
    mode_in,
    mode_out,
    mode_re,
    mode_im,
    mixing,
    out_bias,
    cotangent,
):
    samples, channels, steps = series.shape
    blocks = lax.axis_size("seq")
    devices = blocks * lax.axis_size("rep")
    own = channels // blocks
    width = WINDOW // steps * LANES
    padded = up(channels, LANES)
    block = lax.axis_index("seq").astype(jnp.int32).reshape(1)
    core = lax.axis_index("rep").astype(jnp.int32).reshape(1)
    const = {name: jnp.asarray(value) for name, value in constants(steps).items()}
    groups = group_ids.reshape(1, channels)
    order = [[k ^ order_mask(blocks) for k in range(blocks)]]
    limit = (16 if channels <= 512 else 56) * 2**20
    run = functools.partial(call, limit=limit)
    busy = pl.CostEstimate(flops=4_000_000_000, bytes_accessed=8_000_000, transcendentals=0)
    brief = pl.CostEstimate(flops=100_000_000, bytes_accessed=1_000_000, transcendentals=0)

    send, restored_grad = run(
        functools.partial(send_kernel, own),
        [((blocks * SEND, LANES), f32), ((channels, LANES), f32)],
        hbm=(series, cotangent, mixing, groups),
        scratch=[pltpu.VMEM((channels, LANES), f32)],
        cost=brief,
    )
    ahead, lines, mine, columns, masked, same, cot3, cot_sum = run(
        functools.partial(table_kernel, own),
        [
            ((width, 2 * LANES), bf16),
            ((32, width), f32),
            ((3 * SLOT, LANES), f32),
            ((channels, LANES), f32),
            ((2, channels, channels), bf16),
            ((channels, padded), f32),
            ((padded, 3 * LANES), bf16),
            ((8, padded), f32),
        ],
        smem=(block,),
        hbm=(
            cotangent,
            mixing,
            groups,
            rev_gain.reshape(1, channels),
            rev_bias.reshape(1, channels),
            out_bias.reshape(1, channels),
            mode_in.T,
            mode_out.T,
            mode_re,
            mode_im,
            const["weights"],
            const["endpoint"],
            const["turn"],
            const["scale"],
            const["later"],
        ),
        scratch=[pltpu.VMEM((padded, LANES), f32), pltpu.VMEM((LANES, LANES), f32)],
        cost=busy,
    )
    owned_rows = exchange(send, "seq", blocks, order)
    rows = blocks * SLOT
    windows = blocks * steps // WINDOW
    send, mean, inverse, shifted, waves = run(
        functools.partial(forward_kernel, own, blocks, steps),
        [((blocks * SEND, LANES), f32)]
        + [((rows, LANES), f32)] * 3
        + [((windows * SLOT, LANES), f32)],
        vmem=(
            owned_rows,
            mine,
            ahead,
            const["from_modes"],
            const["to_modes"],
            const["earlier"],
        ),
        cost=brief,
    )
    there = exchange(send, "seq", blocks, order)
    tiles, rest, each, rest_rows, misc_rows, extra = pieces(channels, devices)
    slot = up(tiles * each + extra + 1, 8)
    misc, starts = run(
        functools.partial(backward_kernel, own, blocks, steps),
        [((up(misc_rows, 8), LANES), f32), ((blocks, LANES), f32)],
        smem=(block,),
        vmem=(owned_rows, mine, mean, inverse, shifted, waves, ahead, lines, cot_sum),
        hbm=(const["turn"], const["weights_t"], const["earlier"]),
        cost=busy,
    )
    (send,) = run(
        functools.partial(mix_kernel, own, devices),
        [((devices * slot, LANES), f32)],
        vmem=(there, same, cot3, misc, starts),
        scratch=[
            pltpu.VMEM((padded, LANES), f32),
            pltpu.VMEM((up(extra * devices, 8), LANES), f32),
        ],
        cost=brief,
    )
    shares = exchange(send, ("seq", "rep"), devices)
    layer_out, part = run(
        functools.partial(steps_kernel, own),
        [((1, channels, steps), f32), ((channels, steps), f32)],
        smem=(block,),
        vmem=(there, restored_grad, ahead, lines, columns, masked),
        hbm=(series, cotangent, const["earlier"], const["later"]),
        scratch=[pltpu.VMEM((channels, LANES), f32)] * 3,
        cost=busy,
    )
    (send,) = run(
        functools.partial(sum_kernel, devices),
        [((devices * slot, LANES), f32)],
        vmem=(shares,),
        cost=brief,
    )
    sums = exchange(send, ("seq", "rep"), devices)
    (series_grad,) = run(
        functools.partial(series_kernel, own, devices),
        [((1, channels, steps), f32)],
        smem=(core,),
        vmem=(shares, part),
        hbm=(series,),
        cost=busy,
    )
    outs = run(
        functools.partial(spread_kernel, devices),
        [
            ((1, channels), f32),
            ((1, channels), f32),
            ((RANK, ORDER), f32),
            ((RANK, ORDER), f32),
            ((RANK, MODES), f32),
            ((RANK, MODES), f32),
            ((channels, channels), f32),
            ((1, channels), f32),
        ],
        vmem=(sums, const["endpoint"]),
        scratch=[pltpu.VMEM((up(extra * devices, 8), LANES), f32)],
        cost=brief,
    )
    return (
        layer_out,
        series_grad,
        outs[0].reshape(channels),
        outs[1].reshape(channels),
        outs[2].T,
        outs[3].T,
        outs[4],
        outs[5],
        outs[6],
        outs[7].reshape(channels),
    )


def solution(mesh):
    time_split = P("rep", None, "seq")
    in_specs = (time_split,) + (P(),) * 9 + (time_split,)
    out_specs = (time_split, time_split) + (P(),) * 8
    return jax.shard_map(body, mesh=mesh, in_specs=in_specs, out_specs=out_specs, check_vma=False)
```

```python
import functools
import math

import jax
import jax.numpy as jnp
import ml_dtypes
import numpy as np
from jax import lax
from jax.experimental import pallas as pl
from jax.experimental.pallas import tpu as pltpu
from jax.sharding import PartitionSpec as P

ORDER = 256
MODES = 32
RANK = 4
WINDOW = 720
EPSILON = 1e-05

LANES = 128
CORES = 2
SLOT = 16
SEND = 16
EXTRA = 36
f32 = jnp.float32
bf16 = jnp.bfloat16


def up(value, multiple):
    return -(-value // multiple) * multiple


def legendre_table():
    one, two = np.float32(1.0), np.float32(2.0)
    lags = np.arange(WINDOW).astype(np.float32)
    points = one - (two * (lags + np.float32(0.5))) * np.float32(1.0 / WINDOW)
    lower, this = np.zeros_like(points), np.ones_like(points)
    rows = []
    for degree in np.arange(ORDER).astype(np.float32):
        rows.append(this)
        upper = ((two * degree + one) * points * this - degree * lower) / (degree + one)
        lower, this = this, upper
    return np.stack(rows)


def in_blocks(values, steps):
    blocks = WINDOW // steps
    framed = np.zeros(values.shape[:-1] + (blocks, LANES))
    framed[..., :steps] = values.reshape(values.shape[:-1] + (blocks, steps))
    return framed.reshape(values.shape[:-1] + (blocks * LANES,))


def halves(values):
    high = values.astype(np.float32).astype(ml_dtypes.bfloat16)
    low = (values - high.astype(np.float64)).astype(ml_dtypes.bfloat16)
    return high, low


def constants(steps):
    legendre = legendre_table()
    degree = np.arange(ORDER).astype(np.float32)
    weights = legendre * ((np.float32(2.0) * degree + np.float32(1.0)) / np.float32(WINDOW))[:, None]
    flipped = in_blocks(weights[:, ::-1], steps)
    high, low = halves(flipped)
    table = {}
    table["weights"] = np.concatenate([high, low], 1)
    table["weights_t"] = np.concatenate([high.T, low.T], 1)
    table["endpoint"] = legendre[:, 0][None, :].astype(np.float32)
    mode = np.arange(MODES)[:, None]
    step = np.arange(WINDOW)[None, :]
    angle = 2.0 * math.pi / WINDOW * (mode * step % WINDOW)
    cosine, sine = np.cos(angle), np.sin(angle)
    back = 2.0 * math.pi / WINDOW * (mode * (WINDOW - 1 - step) % WINDOW)
    table["turn"] = np.concatenate(
        [in_blocks(v, steps) for v in (cosine, sine, np.cos(back), np.sin(back))]
    ).astype(np.float32)
    scale = np.where(np.arange(MODES) == 0, 1.0, 2.0) / WINDOW
    table["scale"] = np.tile(scale, 4)[None, :].astype(np.float32)
    high, low = halves(in_blocks(np.concatenate([cosine, -sine]), steps))
    table["to_modes"] = np.concatenate([high.T, low.T], 1)
    wave = in_blocks(np.concatenate([scale[:, None] * cosine, -scale[:, None] * sine]), steps)
    table["from_modes"] = np.concatenate(halves(wave), 1)
    lane = np.arange(LANES)
    upper = (lane[:, None] <= lane[None, :]).astype(np.float32)
    ones = np.ones((LANES, LANES), np.float32)
    for name, part in (("earlier", upper), ("later", upper.T)):
        both = np.concatenate([part, ones], 1)
        table[name] = np.concatenate([both, both]).astype(ml_dtypes.bfloat16)
    return table


def split(value):
    high = value.astype(bf16)
    return high, (value - high.astype(f32)).astype(bf16)


def dot(a, b):
    return lax.dot_general(a, b, (((1,), (0,)), ((), ())), preferred_element_type=f32)


def dot_nt(a, b):
    return lax.dot_general(a, b, (((1,), (1,)), ((), ())), preferred_element_type=f32)


def stacked_dot(value, table):
    rows, width = value.shape[0], table.shape[1] // 2
    high, low = split(value)
    out = dot(jnp.concatenate([high, low], 0), table)
    return out[:rows, :width] + out[:rows, width:] + out[rows:, :width]


def scan_lanes(value, table):
    high, low = split(value)
    out = dot(jnp.concatenate([high, low], 1), table)
    return out[:, :LANES], out[:, LANES:]


def unpacked(ref, i, kind, blocks, steps):
    if i < 8:
        return ref[pl.ds(8 * kind + i, blocks, stride=SEND), :]
    lane = lax.broadcasted_iota(jnp.int32, (blocks, LANES), 1)
    value = None
    for p in reversed(range(3)):
        row = ref[pl.ds(8 * kind + 4 * (i - 8) + p, blocks, stride=SEND), :]
        row = pltpu.roll(row, LANES - steps + EXTRA * p, 1)
        value = row if value is None else jnp.where(lane < EXTRA * (p + 1), row, value)
    return value


def pack_extra(ref, value, i, kind, blocks, steps):
    lane = lax.broadcasted_iota(jnp.int32, (blocks, LANES), 1)
    behind = (lane >= steps) & (lane < steps + EXTRA)
    for p in range(3):
        at = pl.ds(8 * kind + 4 * (i - 8) + p, blocks, stride=SEND)
        ref[at, :] = jnp.where(behind, pltpu.roll(value, steps - EXTRA * p, 1), ref[at, :])


def order_mask(blocks):
    return blocks * 11 // 16


def to_wide(blocks, windows):
    per = len(blocks) // windows
    return jnp.concatenate(
        [jnp.concatenate(blocks[w * per : (w + 1) * per], 1) for w in range(windows)], 0
    )


def to_blocks(wide, windows):
    per = wide.shape[1] // LANES
    return [
        wide[w * SLOT : (w + 1) * SLOT, b * LANES : (b + 1) * LANES]
        for w in range(windows)
        for b in range(per)
    ]


def fetch(pairs, sems):
    copies = [pltpu.make_async_copy(a, b, sems.at[k]) for k, (a, b) in enumerate(pairs)]
    for copy in copies:
        copy.start()

    def ready(*which):
        for k in which:
            copies[k].wait()

    return ready


def blocks_of(value):
    return [value[k * SLOT : (k + 1) * SLOT] for k in range(value.shape[0] // SLOT)]


def same_rows(groups_ref, start, rows):
    channels = groups_ref.shape[1]
    ids = groups_ref[...].astype(f32)
    row = lax.broadcasted_iota(jnp.int32, (rows, channels), 0) + start
    lane = lax.broadcasted_iota(jnp.int32, (rows, channels), 1)
    column = jnp.sum(jnp.where(row == lane, ids, 0.0), axis=1, keepdims=True)
    return column == ids


def own_lanes(place, width, count, blocks):
    row = lax.broadcasted_iota(jnp.int32, (SLOT, width), 0)
    lane = lax.broadcasted_iota(jnp.int32, (SLOT, width), 1)
    return (lane == row * blocks + place) & (row < count)


def send_kernel(
    own,
    series_hbm,
    cot_hbm,
    mixing_hbm,
    groups_hbm,
    send_ref,
    grad_ref,
    series_ref,
    cot_ref,
    mixing_ref,
    groups_ref,
    pad_ref,
    sems,
):
    channels, steps = cot_ref.shape[1:]
    blocks = channels // own
    ready = fetch(
        [
            (groups_hbm, groups_ref),
            (mixing_hbm, mixing_ref),
            (cot_hbm, cot_ref),
            (series_hbm, series_ref),
        ],
        sems,
    )
    pad_ref[...] = jnp.zeros_like(pad_ref)
    ready(0, 1, 2)
    pad_ref[:, :steps] = cot_ref[0]
    chunk = channels if channels <= 512 else 256
    total = None
    for start in range(0, channels, chunk):
        same = same_rows(groups_ref, start, chunk)
        masked = jnp.where(same, mixing_ref[start : start + chunk, :], 0.0)
        high, low = split(masked.T)
        both = jnp.concatenate(split(pad_ref[start : start + chunk, :]), 1)
        out = dot(jnp.concatenate([high, low], 0), both)
        part = out[:channels, :LANES] + out[:channels, LANES:] + out[channels:, :LANES]
        total = part if total is None else total + part
    grad_ref[...] = total
    ready(3)
    pad_ref[:, :steps] = series_ref[0]
    for kind, ref in enumerate((pad_ref, grad_ref)):
        for i in range(own):
            value = ref[blocks * i : blocks * (i + 1), :]
            if i < 8:
                send_ref[pl.ds(8 * kind + i, blocks, stride=SEND), :] = value
            else:
                pack_extra(send_ref, value, i, kind, blocks, steps)


def table_kernel(
    own,
    place_ref,
    cot_hbm,
    mixing_hbm,
    groups_hbm,
    gain_hbm,
    bias_hbm,
    out_bias_hbm,
    mode_in_hbm,
    mode_out_hbm,
    mode_re_hbm,
    mode_im_hbm,
    weights_hbm,
    endpoint_hbm,
    turn_hbm,
    scale_hbm,
    later_hbm,
    ahead_ref,
    lines_ref,
    own_ref,
    columns_ref,
    masked_ref,
    same_ref,
    cot3_ref,
    cot_sum_ref,
    cot_ref,
    mixing_ref,
    groups_ref,
    gain_ref,
    bias_ref,
    out_bias_ref,
    mode_in_ref,
    mode_out_ref,
    mode_re_ref,
    mode_im_ref,
    weights_ref,
    endpoint_ref,
    turn_ref,
    scale_ref,
    later_ref,
    pad_ref,
    turned_ref,
    sems,
):
    ready = fetch(
        [
            (mode_in_hbm, mode_in_ref),
            (mode_out_hbm, mode_out_ref),
            (endpoint_hbm, endpoint_ref),
            (weights_hbm, weights_ref),
            (mode_re_hbm, mode_re_ref),
            (mode_im_hbm, mode_im_ref),
            (scale_hbm, scale_ref),
            (turn_hbm, turn_ref),
            (later_hbm, later_ref),
            (groups_hbm, groups_ref),
            (mixing_hbm, mixing_ref),
            (cot_hbm, cot_ref),
            (gain_hbm, gain_ref),
            (bias_hbm, bias_ref),
            (out_bias_hbm, out_bias_ref),
        ],
        sems,
    )
    channels, steps = cot_ref.shape[1:]
    width = ahead_ref.shape[0]
    per = width // LANES
    blocks = channels // own
    count = 2 * MODES
    lines_ref[...] = jnp.zeros_like(lines_ref)
    turned_ref[...] = jnp.zeros_like(turned_ref)
    pad_ref[...] = jnp.zeros_like(pad_ref)
    ready(0, 1, 2, 3)
    high, low = split(mode_in_ref[...])
    out = dot(jnp.concatenate([high, low], 0), weights_ref[...])
    kernel = out[:RANK, :width] + out[:RANK, width:] + out[RANK:, :width]
    lines_ref[0:RANK, :] = kernel
    mix = jnp.sum(mode_out_ref[...] * endpoint_ref[...], axis=1, keepdims=True)
    ready(4, 5, 6)
    scale = scale_ref[:, 0:count]
    gain_re, gain_im = mode_re_ref[...], mode_im_ref[...]
    signed = jnp.concatenate([gain_re, -gain_im], 1) * scale
    sign = jnp.where(lax.broadcasted_iota(jnp.int32, (RANK, count), 1) < MODES, 1.0, -1.0)
    lines_ref[8 : 8 + RANK, 0:count] = signed * mix
    lines_ref[16 : 16 + RANK, 0:count] = sign * scale * mix
    lines_ref[24 : 24 + RANK, 0:count] = signed
    turned_ref[0:RANK, 0:count] = jnp.concatenate([gain_re, gain_im], 1) * mix
    columns = turned_ref[...].T[0:count]
    response = None
    for r in range(RANK):
        term = columns[:, r : r + 1] * kernel[r : r + 1, :]
        response = term if response is None else response + term
    ready(7, 8)
    real, imag = response[:MODES], response[MODES:]
    cosine, sine = turn_ref[0:MODES], turn_ref[MODES : 2 * MODES]
    cos_b, sin_b = turn_ref[2 * MODES : 3 * MODES], turn_ref[3 * MODES : 4 * MODES]
    turned = jnp.concatenate([real * cos_b + imag * sin_b, imag * cos_b - real * sin_b], 0)
    rows = jnp.concatenate([turned[:, b * LANES : (b + 1) * LANES] for b in range(per)], 0)
    local, total = scan_lanes(rows, later_ref[...])
    run = jnp.zeros((count, LANES), f32)
    suffix = [None] * per
    for b in reversed(range(per)):
        suffix[b] = local[b * count : (b + 1) * count] + run
        run = run + total[b * count : (b + 1) * count]
    for b in range(per):
        at = slice(b * LANES, (b + 1) * LANES)
        c, s = cosine[:, at], sine[:, at]
        parts = []
        for value in (suffix[b], run - suffix[b]):
            re, im = value[:MODES], value[MODES:]
            parts += [re * c + im * s, im * c - re * s]
        high, low = split(jnp.concatenate(parts, 0).T)
        ahead_ref[at, 0:LANES] = high
        ahead_ref[at, LANES : 2 * LANES] = low
    ready(9, 10, 11, 12, 13, 14)
    chunk = channels if channels <= 512 else 256
    for start in range(0, channels, chunk):
        at = slice(start, start + chunk)
        same = same_rows(groups_ref, start, chunk)
        high, low = split(jnp.where(same, mixing_ref[at, :], 0.0))
        masked_ref[0, at, :] = high
        masked_ref[1, at, :] = low
        same_ref[at, 0:channels] = jnp.where(same, 1.0, 0.0)
        row = lax.broadcasted_iota(jnp.int32, (chunk, channels), 0) + start
        lane = lax.broadcasted_iota(jnp.int32, (chunk, channels), 1)
        for k, ref in enumerate((gain_ref, bias_ref, out_bias_ref)):
            columns_ref[at, k : k + 1] = jnp.sum(
                jnp.where(row == lane, ref[...], 0.0), axis=1, keepdims=True
            )
    mine = own_lanes(place_ref[0] // CORES ^ order_mask(blocks), channels, own, blocks)
    gain = jnp.sum(jnp.where(mine, gain_ref[...], 0.0), axis=1, keepdims=True)
    gain = jnp.where(lax.broadcasted_iota(jnp.int32, (SLOT, 1), 0) < own, gain, 1.0)
    bias = jnp.sum(jnp.where(mine, bias_ref[...], 0.0), axis=1, keepdims=True)
    own_ref[0:SLOT, :] = jnp.broadcast_to(gain, (SLOT, LANES))
    own_ref[SLOT : 2 * SLOT, :] = jnp.broadcast_to(bias, (SLOT, LANES))
    own_ref[2 * SLOT : 3 * SLOT, :] = jnp.broadcast_to(1.0 / gain, (SLOT, LANES))
    own_ref[3 * SLOT :, :] = jnp.broadcast_to(scale_ref[...], (8, LANES))
    pad_ref[0:channels, :steps] = cot_ref[0]
    high, low = split(pad_ref[...])
    cot3_ref[...] = jnp.concatenate([high, high, low], 1)
    cot_sum_ref[...] = dot_nt(
        jnp.ones((8, 2 * LANES), bf16), jnp.concatenate([high, low], 1)
    )


def normalized(x, blocks, steps, earlier):
    rows = x.shape[0]
    local, total = scan_lanes(jnp.concatenate([x, x * x], 0), earlier)
    first, second = blocks_of(local[:rows]), blocks_of(local[rows:])
    first_all, second_all = blocks_of(total[:rows]), blocks_of(total[rows:])
    run_one = jnp.zeros((SLOT, LANES), f32)
    run_two = jnp.zeros((SLOT, LANES), f32)
    lane = lax.broadcasted_iota(jnp.int32, (SLOT, LANES), 1)
    found = []
    for k in range(blocks):
        inverse = 1.0 / (lane + (k * steps + 1 + WINDOW)).astype(f32)
        mean = (first[k] + run_one) * inverse
        variance = (second[k] + run_two + WINDOW) * inverse - mean * mean + EPSILON
        found.append((mean, variance, run_one, run_two))
        run_one = run_one + first_all[k]
        run_two = run_two + second_all[k]
    return found


def owned(recv_ref, tail_ref, own, blocks, steps):
    lane = lax.broadcasted_iota(jnp.int32, (blocks, LANES), 1)
    tail_ref[...] = jnp.zeros_like(tail_ref)
    for kind in range(2):
        for i in range(8, own):
            tail_ref[pl.ds(8 * kind + i - 8, blocks, stride=SLOT), :] = jnp.where(
                lane < steps, unpacked(recv_ref, i, kind, blocks, steps), 0.0
            )
    got = recv_ref[...].reshape(blocks, SEND, LANES)
    got = jnp.where(lax.broadcasted_iota(jnp.int32, got.shape, 2) < steps, got, 0.0)
    tail = tail_ref[...].reshape(blocks, SLOT, LANES)
    x = jnp.concatenate([got[:, 0:8], tail[:, 0:8]], 1)
    grad = jnp.concatenate([got[:, 8:16], tail[:, 8:16]], 1)
    mask = order_mask(blocks)
    return [x[b ^ mask] for b in range(blocks)], [grad[b ^ mask] for b in range(blocks)]


def forward_kernel(
    own,
    blocks,
    steps,
    recv_ref,
    own_ref,
    ahead_ref,
    from_modes_ref,
    to_modes_ref,
    earlier_ref,
    send_ref,
    mean_ref,
    inverse_ref,
    centered_ref,
    shifted_ref,
    grad_ref,
    normal_grad_ref,
    waves_ref,
    tail_ref,
):
    windows = blocks * steps // WINDOW
    x, grad = owned(recv_ref, tail_ref, own, blocks, steps)
    found = normalized(jnp.concatenate(x, 0), blocks, steps, earlier_ref[...])
    gain, bias, over = own_ref[0:SLOT], own_ref[SLOT : 2 * SLOT], own_ref[2 * SLOT : 3 * SLOT]
    row = lax.broadcasted_iota(jnp.int32, (SLOT, LANES), 0)
    lane = lax.broadcasted_iota(jnp.int32, (SLOT, LANES), 1)
    held = (row < own) & (lane < steps)
    normal, spreads, recon_grad = [], [], []
    for k in range(blocks):
        at = slice(k * SLOT, (k + 1) * SLOT)
        mean, variance = found[k][:2]
        inverse = lax.rsqrt(variance)
        spread = variance * inverse
        centered = (x[k] - mean) * inverse
        normal.append(gain * centered + bias)
        spreads.append(spread)
        recon_grad.append(jnp.where(held, grad[k] * spread * over, 0.0))
        mean_ref[at, :] = mean
        inverse_ref[at, :] = inverse
        centered_ref[at, :] = centered
        grad_ref[at, :] = grad[k]
    spectra = stacked_dot(to_wide(normal, windows), ahead_ref[...])
    waves = stacked_dot(to_wide(recon_grad, windows), to_modes_ref[...])
    count = 2 * MODES
    current, before = spectra[:, :count], spectra[:, count:]
    zero = jnp.zeros((SLOT, count), f32)
    after = zero
    if windows > 1:
        current = current + jnp.concatenate([zero, before[:-SLOT]], 0)
        after = jnp.concatenate([waves[SLOT:], zero], 0)
    recon = stacked_dot(current, from_modes_ref[...])
    waves = jnp.concatenate([waves, after], 1)
    waves_ref[...] = waves
    recon = to_blocks(recon, windows)
    normal_grad = to_blocks(convolved_back(waves * own_ref[3 * SLOT : 3 * SLOT + 1], ahead_ref[...]), windows)
    for b in range(blocks):
        at = slice(b * SLOT, (b + 1) * SLOT)
        mean, variance, run_one, run_two = found[b]
        shifted = (recon[b] - bias) * over
        shifted_ref[at, :] = shifted
        normal_grad_ref[at, :] = normal_grad[b]
        back = shifted * spreads[b] + mean
        one, two = lane[0:8] == LANES - 2, lane[0:8] == LANES - 1
        slot = (b ^ order_mask(blocks)) * SEND
        send_ref[slot : slot + 8, :] = jnp.where(
            one, run_one[0:8], jnp.where(two, run_two[0:8], back[0:8])
        )
        send_ref[slot + 8 : slot + 16, :] = jnp.where(
            one, run_one[8:16], jnp.where(two, run_two[8:16], normal_grad[b][0:8])
        )
        tail_ref[slot : slot + 8, :] = back[8:16]
        tail_ref[slot + 8 : slot + 16, :] = normal_grad[b][8:16]
    for kind in range(2):
        for i in range(8, own):
            value = tail_ref[pl.ds(8 * kind + i - 8, blocks, stride=SLOT), :]
            pack_extra(send_ref, value, i, kind, blocks, steps)


def backward_kernel(
    own,
    blocks,
    steps,
    place_ref,
    own_ref,
    mean_ref,
    inverse_ref,
    centered_ref,
    shifted_ref,
    grad_ref,
    normal_grad_ref,
    waves_ref,
    lines_ref,
    cot_sum_ref,
    turn_hbm,
    weights_t_hbm,
    earlier_hbm,
    misc_ref,
    starts_ref,
    turn_ref,
    weights_t_ref,
    earlier_ref,
    sems,
):
    ready = fetch(
        [(turn_hbm, turn_ref), (earlier_hbm, earlier_ref), (weights_t_hbm, weights_t_ref)], sems
    )
    windows = blocks * steps // WINDOW
    wide = cot_sum_ref.shape[1]
    count = 2 * MODES
    mean, inverse, centered, shifted, grad, normal_grad = (
        blocks_of(ref[...])
        for ref in (
            mean_ref,
            inverse_ref,
            centered_ref,
            shifted_ref,
            grad_ref,
            normal_grad_ref,
        )
    )
    gain, bias, over = own_ref[0:SLOT], own_ref[SLOT : 2 * SLOT], own_ref[2 * SLOT : 3 * SLOT]
    row = lax.broadcasted_iota(jnp.int32, (SLOT, LANES), 0)
    lane = lax.broadcasted_iota(jnp.int32, (SLOT, LANES), 1)
    held = (row < own) & (lane < steps)
    waves = waves_ref[...]
    gain_sum = jnp.zeros((SLOT, LANES), f32)
    bias_sum = jnp.zeros((SLOT, LANES), f32)
    normal, ones, twos = [], [], []
    for k in range(blocks):
        over_q = 1.0 / (lane + (k * steps + 1 + WINDOW)).astype(f32)
        normal.append(jnp.where(held, gain * centered[k] + bias, 0.0))
        recon_grad = grad[k] / inverse[k] * over
        gain_sum = gain_sum + normal_grad[k] * centered[k] - recon_grad * shifted[k]
        bias_sum = bias_sum + normal_grad[k] - recon_grad
        first, second = statistics(
            grad[k],
            shifted[k],
            normal_grad[k] * gain * inverse[k],
            centered[k],
            mean[k],
            inverse[k],
            over_q,
        )
        ones.append(jnp.where(held, first, 0.0))
        twos.append(jnp.where(held, second, 0.0))
    gain_sum, bias_sum = jnp.where(held, gain_sum, 0.0), jnp.where(held, bias_sum, 0.0)
    run_one = jnp.zeros((SLOT, LANES), f32)
    run_two = jnp.zeros((SLOT, LANES), f32)
    spots = (lane == row) & (row < own)
    for k in reversed(range(blocks)):
        both = jnp.where(spots, jnp.sum(run_one, 1, keepdims=True), 0.0)
        both = both + pltpu.roll(
            jnp.where(spots, jnp.sum(run_two, 1, keepdims=True), 0.0), SLOT, 1
        )
        starts_ref[k : k + 1, :] = jnp.sum(both, 0, keepdims=True)
        run_one = run_one + ones[k]
        run_two = run_two + twos[k]
    signal = to_wide(normal, windows)
    high, low = split(signal)
    w_high, w_low = split(waves.T)
    pairs = dot(
        jnp.concatenate([w_high, w_high, w_low], 1), jnp.concatenate([high, low, high], 0)
    )
    ready(0)
    cosine, sine = turn_ref[0:MODES], turn_ref[MODES : 2 * MODES]
    cos_b, sin_b = turn_ref[2 * MODES : 3 * MODES], turn_ref[3 * MODES : 4 * MODES]

    def turned(value):
        re, im = value[:MODES], value[MODES:]
        return jnp.concatenate([re * cosine - im * sine, -(re * sine + im * cosine)], 0)

    per = pairs.shape[1] // LANES
    after = turned(pairs[count:])
    left = turned(pairs[:count]) - after
    after = sum(after[:, b * LANES : (b + 1) * LANES] for b in range(per))
    ready(1)
    local, total = scan_lanes(
        jnp.concatenate([left[:, b * LANES : (b + 1) * LANES] for b in range(per)], 0),
        earlier_ref[...],
    )
    run = jnp.broadcast_to(jnp.sum(after, 1, keepdims=True), (count, LANES))
    sums = []
    for b in range(per):
        sums.append(local[b * count : (b + 1) * count] + run)
        run = run + total[b * count : (b + 1) * count]
    sums = jnp.concatenate(sums, 1)
    re, im = sums[:MODES], sums[MODES:]
    crossed = jnp.concatenate([re * cos_b + im * sin_b, im * cos_b - re * sin_b], 0)
    high, low = split(crossed)
    s_high, s_low = split(lines_ref[8:16, 0:count])
    kernel_grad = dot(
        jnp.concatenate([s_high, s_high, s_low], 1), jnp.concatenate([high, low, high], 0)
    )
    k_high, k_low = split(lines_ref[0:8, :])
    overlap = dot_nt(
        jnp.concatenate([k_high, k_high, k_low], 1), jnp.concatenate([high, low, high], 1)
    )
    modes = overlap * lines_ref[16:24, 0:count]
    mix_grad = jnp.sum(overlap * lines_ref[24:32, 0:count], axis=1, keepdims=True)
    ready(2)
    mode_in_grad = stacked_dot(kernel_grad, weights_t_ref[...])
    misc_ref[...] = jnp.zeros_like(misc_ref)
    misc_ref[0:RANK, :] = mode_in_grad[0:RANK, :LANES]
    misc_ref[RANK : 2 * RANK, :] = mode_in_grad[0:RANK, LANES:]
    misc_ref[8 : 8 + RANK, 0:count] = modes[0:RANK]
    misc_ref[8 : 8 + RANK, count : 2 * count] = jnp.broadcast_to(mix_grad, (8, count))[0:RANK]
    mine = own_lanes(place_ref[0] // CORES ^ order_mask(blocks), wide, own, blocks)
    at = 12
    gain_row = jnp.sum(
        jnp.where(mine, jnp.sum(gain_sum, 1, keepdims=True), 0.0), axis=0, keepdims=True
    )
    bias_row = jnp.sum(
        jnp.where(mine, jnp.sum(bias_sum, 1, keepdims=True), 0.0), axis=0, keepdims=True
    )
    for value in (gain_row, bias_row, cot_sum_ref[0:1, :]):
        for j in range(wide // LANES):
            misc_ref[at : at + 1, :] = value[:, j * LANES : (j + 1) * LANES]
            at += 1


def convolved_back(waves, ahead):
    rows = waves.shape[0]
    high, low = split(waves)
    out = dot_nt(jnp.concatenate([high, low], 0), ahead[:, :LANES])
    return out[:rows] + out[rows:] + dot_nt(high, ahead[:, LANES:])


def statistics(grad, shifted, scaled, centered, mean, inverse, over_q):
    variance_grad = (grad * shifted - scaled * centered) * (0.5 * inverse)
    first = (grad - scaled - 2.0 * mean * variance_grad) * over_q
    return first, variance_grad * over_q


def pieces(channels, devices):
    tiles, rest = channels // LANES, channels % LANES
    each = channels // devices
    rest_rows = channels * rest // LANES
    misc_rows = 12 + 3 * (up(channels, LANES) // LANES)
    extra = up(rest_rows + misc_rows, devices) // devices
    return tiles, rest, each, rest_rows, misc_rows, extra


def gathered(recv_ref, kind, own, blocks, steps, dense_ref):
    for i in range(own):
        dense_ref[blocks * i : blocks * (i + 1), :] = unpacked(recv_ref, i, kind, blocks, steps)


def mix_kernel(
    own,
    devices,
    steps,
    recv_ref,
    same_ref,
    cot3_ref,
    misc_ref,
    starts_ref,
    send_ref,
    dense_ref,
    misc_all_ref,
):
    channels = same_ref.shape[0]
    blocks = channels // own
    tiles, rest, each, rest_rows, misc_rows, extra = pieces(channels, devices)
    slot = send_ref.shape[0] // devices
    if dense_ref.shape[0] > channels:
        dense_ref[channels:, :] = jnp.zeros((dense_ref.shape[0] - channels, LANES), f32)
    gathered(recv_ref, 0, own, blocks, steps, dense_ref)
    high, low = split(dense_ref[...])
    three = jnp.concatenate([high, low, high], 1)
    chunk = channels if channels <= 512 else devices
    for start in range(0, channels, chunk):
        at = slice(start, start + chunk)
        grad = dot_nt(cot3_ref[at, :], three)
        for j in range(tiles):
            lanes = slice(j * LANES, (j + 1) * LANES)
            tile = grad[:, lanes] * same_ref[at, lanes]
            for i in range(chunk // devices):
                send_ref[pl.ds(j * each + start // devices + i, devices, stride=slot), :] = tile[
                    devices * i : devices * (i + 1)
                ]
        if rest:
            lanes = slice(tiles * LANES, tiles * LANES + LANES)
            last = grad[:, lanes] * same_ref[at, lanes]
            folded = last[0:rest_rows]
            for g in range(1, LANES // rest):
                folded = folded + pltpu.roll(
                    last[g * rest_rows : (g + 1) * rest_rows], g * rest, 1
                )
            misc_all_ref[0:rest_rows, :] = folded
    end = rest_rows + misc_rows
    misc_all_ref[rest_rows:end, :] = misc_ref[0:misc_rows, :]
    if misc_all_ref.shape[0] > end:
        misc_all_ref[end:, :] = jnp.zeros((misc_all_ref.shape[0] - end, LANES), f32)
    for k in range(extra):
        send_ref[pl.ds(tiles * each + k, devices, stride=slot), :] = misc_all_ref[
            devices * k : devices * (k + 1), :
        ]
    for k in range(tiles * each + extra, slot - 1):
        send_ref[pl.ds(k, devices, stride=slot), :] = jnp.zeros((devices, LANES), f32)
    for r in range(2):
        send_ref[pl.ds(r * slot + slot - 1, blocks, stride=2 * slot), :] = starts_ref[...]


def steps_kernel(
    own,
    devices,
    place_ref,
    recv_ref,
    shares_ref,
    grad_ref,
    columns_ref,
    masked_ref,
    series_hbm,
    cot_hbm,
    earlier_hbm,
    later_hbm,
    out_ref,
    series_grad_ref,
    series_ref,
    cot_ref,
    earlier_ref,
    later_ref,
    dense_ref,
    back_ref,
    sums_ref,
    pad_ref,
    sems,
):
    ready = fetch(
        [
            (series_hbm, series_ref),
            (cot_hbm, cot_ref),
            (earlier_hbm, earlier_ref),
            (later_hbm, later_ref),
        ],
        sems,
    )
    channels, steps = series_ref.shape[1:]
    blocks = channels // own
    block = place_ref[0] // CORES
    gathered(recv_ref, 0, own, blocks, steps, dense_ref)
    gathered(recv_ref, 1, own, blocks, steps, back_ref)
    for i in range(own):
        sums_ref[blocks * i : blocks * (i + 1), :] = recv_ref[pl.ds(i, blocks, stride=SEND), :]
    pad_ref[...] = jnp.zeros_like(pad_ref)
    gain, bias, shift = (columns_ref[:, k : k + 1] for k in range(3))
    restored = dense_ref[...]
    both = jnp.concatenate(split(restored), 1)
    ready(0)
    pad_ref[:, :steps] = series_ref[0]
    chunk = channels if channels <= 512 else 256
    for start in range(0, channels, chunk):
        at = slice(start, start + chunk)
        out = dot(jnp.concatenate([masked_ref[0, at, :], masked_ref[1, at, :]], 0), both)
        mixed = out[:chunk, :LANES] + out[:chunk, LANES:] + out[chunk:, :LANES]
        out_ref[0, at, :] = (pad_ref[at, :] + mixed + shift[at])[:, :steps]
    x = pad_ref[...]
    ready(2)
    local, unused = scan_lanes(jnp.concatenate([x, x * x], 0), earlier_ref[...])
    lane = lax.broadcasted_iota(jnp.int32, (channels, LANES), 1)
    over_q = 1.0 / (lane + (block * steps + 1 + WINDOW)).astype(f32)
    mean = (local[:channels] + sums_ref[:, LANES - 2 : LANES - 1]) * over_q
    variance = (local[channels:] + sums_ref[:, LANES - 1 : LANES] + WINDOW) * over_q
    inverse = lax.rsqrt(variance - mean * mean + EPSILON)
    centered = (x - mean) * inverse
    scaled = back_ref[...] * gain * inverse
    first, second = statistics(
        grad_ref[...], (restored - mean) * inverse, scaled, centered, mean, inverse, over_q
    )
    held = lane < steps
    ready(3)
    local, unused = scan_lanes(
        jnp.concatenate([jnp.where(held, first, 0.0), jnp.where(held, second, 0.0)], 0),
        later_ref[...],
    )
    slot = shares_ref.shape[0] // devices
    first_core = place_ref[0] % CORES == 0
    rows = []
    for s in range(blocks):
        at = (s ^ order_mask(blocks)) * 2 * slot + slot - 1
        rows.append(
            jnp.where(
                first_core, shares_ref[at : at + 1, :], shares_ref[at + slot : at + slot + 1, :]
            )
        )
    later = jnp.concatenate(rows, 0)
    part = scaled + local[:channels] + 2.0 * x * local[channels:]
    ready(1)
    for i in range(own):
        at = slice(blocks * i, blocks * (i + 1))
        sums = later[:, i : i + 1] + 2.0 * x[at] * later[:, SLOT + i : SLOT + i + 1]
        series_grad_ref[0, at, :] = cot_ref[0, at, :] + (part[at] + sums)[:, :steps]


def sum_kernel(devices, recv_ref, send_ref):
    slot = recv_ref.shape[0] // devices
    total = recv_ref[0:slot, :]
    for s in range(1, devices):
        total = total + recv_ref[s * slot : (s + 1) * slot, :]
    for s in range(devices):
        send_ref[s * slot : (s + 1) * slot, :] = total


def spread_kernel(
    devices,
    recv_ref,
    endpoint_ref,
    gain_ref,
    bias_ref,
    mode_in_ref,
    mode_out_ref,
    mode_re_ref,
    mode_im_ref,
    mixing_ref,
    out_bias_ref,
    misc_ref,
):
    channels = mixing_ref.shape[0]
    tiles, rest, each, rest_rows, misc_rows, extra = pieces(channels, devices)
    slot = recv_ref.shape[0] // devices
    for j in range(tiles):
        for i in range(each):
            mixing_ref[devices * i : devices * (i + 1), j * LANES : (j + 1) * LANES] = recv_ref[
                pl.ds(j * each + i, devices, stride=slot), :
            ]
    for k in range(extra):
        misc_ref[devices * k : devices * (k + 1), :] = recv_ref[
            pl.ds(tiles * each + k, devices, stride=slot), :
        ]
    if rest:
        folded = misc_ref[0:rest_rows, :]
        for g in range(LANES // rest):
            piece = folded if g == 0 else pltpu.roll(folded, LANES - g * rest, 1)
            mixing_ref[g * rest_rows : (g + 1) * rest_rows, tiles * LANES :] = piece[:, :rest]
    at = rest_rows
    mode_in_ref[:, 0:LANES] = misc_ref[at : at + RANK, :]
    mode_in_ref[:, LANES : 2 * LANES] = misc_ref[at + RANK : at + 2 * RANK, :]
    modes = misc_ref[at + 8 : at + 8 + RANK, :]
    mode_re_ref[...] = modes[:, 0:MODES]
    mode_im_ref[...] = modes[:, MODES : 2 * MODES]
    mode_out_ref[...] = modes[:, 2 * MODES : 2 * MODES + 1] * endpoint_ref[...]
    at += 12
    for ref in (gain_ref, bias_ref, out_bias_ref):
        for start in range(0, channels, LANES):
            size = min(LANES, channels - start)
            ref[:, start : start + size] = misc_ref[at : at + 1, 0:size]
            at += 1


def call(kernel, outs, smem=(), vmem=(), hbm=(), scratch=(), cost=None, limit=None):
    in_vmem = pl.BlockSpec(memory_space=pltpu.VMEM)
    in_smem = pl.BlockSpec(memory_space=pltpu.SMEM)
    in_hbm = pl.BlockSpec(memory_space=pltpu.HBM)
    held = [pltpu.VMEM(a.shape, a.dtype) for a in hbm] + list(scratch)
    if hbm:
        held.append(pltpu.SemaphoreType.DMA((len(hbm),)))
    hbm = [pltpu.with_memory_space_constraint(a, pltpu.HBM) for a in hbm]
    return pl.pallas_call(
        kernel,
        out_shape=tuple(jax.ShapeDtypeStruct(shape, kind) for shape, kind in outs),
        in_specs=[in_smem] * len(smem) + [in_vmem] * len(vmem) + [in_hbm] * len(hbm),
        out_specs=tuple(in_vmem for unused in outs),
        scratch_shapes=held,
        compiler_params=pltpu.CompilerParams(vmem_limit_bytes=limit),
        cost_estimate=cost,
    )(*smem, *vmem, *hbm)


def exchange(value, axis, count, order=None):
    rows = value.shape[0] // count
    out = lax.all_to_all(
        value.reshape(count, rows, value.shape[1]),
        axis,
        split_axis=0,
        concat_axis=0,
        axis_index_groups=order,
    )
    return out.reshape(value.shape)


def body(
    series,
    group_ids,
    rev_gain,
    rev_bias,
    mode_in,
    mode_out,
    mode_re,
    mode_im,
    mixing,
    out_bias,
    cotangent,
):
    samples, channels, steps = series.shape
    blocks = lax.axis_size("seq")
    devices = blocks * lax.axis_size("rep")
    own = channels // blocks
    width = WINDOW // steps * LANES
    padded = up(channels, LANES)
    place = lax.axis_index(("seq", "rep")).astype(jnp.int32).reshape(1)
    const = {name: jnp.asarray(value) for name, value in constants(steps).items()}
    groups = group_ids.reshape(1, channels)
    order = [[k ^ order_mask(blocks) for k in range(blocks)]]
    limit = (16 if channels <= 512 else 56) * 2**20
    run = functools.partial(call, limit=limit)
    busy = pl.CostEstimate(flops=4_000_000_000, bytes_accessed=8_000_000, transcendentals=0)
    brief = pl.CostEstimate(flops=100_000_000, bytes_accessed=1_000_000, transcendentals=0)

    send, restored_grad = run(
        functools.partial(send_kernel, own),
        [((blocks * SEND, LANES), f32), ((channels, LANES), f32)],
        hbm=(series, cotangent, mixing, groups),
        scratch=[pltpu.VMEM((channels, LANES), f32)],
        cost=brief,
    )
    ahead, lines, mine, columns, masked, same, cot3, cot_sum = run(
        functools.partial(table_kernel, own),
        [
            ((width, 2 * LANES), bf16),
            ((32, width), f32),
            ((3 * SLOT + 8, LANES), f32),
            ((channels, LANES), f32),
            ((2, channels, channels), bf16),
            ((channels, padded), f32),
            ((padded, 3 * LANES), bf16),
            ((8, padded), f32),
        ],
        smem=(place,),
        hbm=(
            cotangent,
            mixing,
            groups,
            rev_gain.reshape(1, channels),
            rev_bias.reshape(1, channels),
            out_bias.reshape(1, channels),
            mode_in.T,
            mode_out.T,
            mode_re,
            mode_im,
            const["weights"],
            const["endpoint"],
            const["turn"],
            const["scale"],
            const["later"],
        ),
        scratch=[pltpu.VMEM((padded, LANES), f32), pltpu.VMEM((LANES, LANES), f32)],
        cost=busy,
    )
    owned_rows = exchange(send, "seq", blocks, order)
    rows = blocks * SLOT
    windows = blocks * steps // WINDOW
    send, *kept = run(
        functools.partial(forward_kernel, own, blocks, steps),
        [((blocks * SEND, LANES), f32)]
        + [((rows, LANES), f32)] * 6
        + [((windows * SLOT, LANES), f32)],
        vmem=(
            owned_rows,
            mine,
            ahead,
            const["from_modes"],
            const["to_modes"],
            const["earlier"],
        ),
        scratch=[pltpu.VMEM((rows, LANES), f32)],
        cost=brief,
    )
    there = exchange(send, "seq", blocks, order)
    tiles, rest, each, rest_rows, misc_rows, extra = pieces(channels, devices)
    slot = up(tiles * each + extra + 1, 8)
    misc, starts = run(
        functools.partial(backward_kernel, own, blocks, steps),
        [((up(misc_rows, 8), LANES), f32), ((blocks, LANES), f32)],
        smem=(place,),
        vmem=(mine, *kept, lines, cot_sum),
        hbm=(const["turn"], const["weights_t"], const["earlier"]),
        cost=busy,
    )
    (send,) = run(
        functools.partial(mix_kernel, own, devices, steps),
        [((devices * slot, LANES), f32)],
        vmem=(there, same, cot3, misc, starts),
        scratch=[
            pltpu.VMEM((padded, LANES), f32),
            pltpu.VMEM((up(extra * devices, 8), LANES), f32),
        ],
        cost=brief,
    )
    shares = exchange(send, ("seq", "rep"), devices)
    (send,) = run(
        functools.partial(sum_kernel, devices),
        [((devices * slot, LANES), f32)],
        vmem=(shares,),
        cost=brief,
    )
    sums = exchange(send, ("seq", "rep"), devices)
    layer_out, series_grad = run(
        functools.partial(steps_kernel, own, devices),
        [((1, channels, steps), f32), ((1, channels, steps), f32)],
        smem=(place,),
        vmem=(there, shares, restored_grad, columns, masked),
        hbm=(series, cotangent, const["earlier"], const["later"]),
        scratch=[pltpu.VMEM((channels, LANES), f32)] * 4,
        cost=busy,
    )
    outs = run(
        functools.partial(spread_kernel, devices),
        [
            ((1, channels), f32),
            ((1, channels), f32),
            ((RANK, ORDER), f32),
            ((RANK, ORDER), f32),
            ((RANK, MODES), f32),
            ((RANK, MODES), f32),
            ((channels, channels), f32),
            ((1, channels), f32),
        ],
        vmem=(sums, const["endpoint"]),
        scratch=[pltpu.VMEM((up(extra * devices, 8), LANES), f32)],
        cost=brief,
    )
    return (
        layer_out,
        series_grad,
        outs[0].reshape(channels),
        outs[1].reshape(channels),
        outs[2].T,
        outs[3].T,
        outs[4],
        outs[5],
        outs[6],
        outs[7].reshape(channels),
    )


def solution(mesh):
    time_split = P("rep", None, "seq")
    in_specs = (time_split,) + (P(),) * 9 + (time_split,)
    out_specs = (time_split, time_split) + (P(),) * 8
    return jax.shard_map(body, mesh=mesh, in_specs=in_specs, out_specs=out_specs, check_vma=False)
```

```python
import functools
import math

import jax
import jax.numpy as jnp
import ml_dtypes
import numpy as np
from jax import lax
from jax.experimental import pallas as pl
from jax.experimental.pallas import tpu as pltpu
from jax.sharding import PartitionSpec as P

ORDER = 256
MODES = 32
RANK = 4
WINDOW = 720
EPSILON = 1e-05

LANES = 128
CORES = 2
HALVES = 2
SLOT = 24
KIND = 16
EXTRA = 36
f32 = jnp.float32
bf16 = jnp.bfloat16


def up(value, multiple):
    return -(-value // multiple) * multiple


def legendre_table():
    one, two = np.float32(1.0), np.float32(2.0)
    lags = np.arange(WINDOW).astype(np.float32)
    points = one - (two * (lags + np.float32(0.5))) * np.float32(1.0 / WINDOW)
    lower, this = np.zeros_like(points), np.ones_like(points)
    rows = []
    for degree in np.arange(ORDER).astype(np.float32):
        rows.append(this)
        upper = ((two * degree + one) * points * this - degree * lower) / (degree + one)
        lower, this = this, upper
    return np.stack(rows)


def in_blocks(values, steps):
    blocks = WINDOW // steps
    framed = np.zeros(values.shape[:-1] + (blocks, LANES))
    framed[..., :steps] = values.reshape(values.shape[:-1] + (blocks, steps))
    return framed.reshape(values.shape[:-1] + (blocks * LANES,))


def halves(values):
    high = values.astype(np.float32).astype(ml_dtypes.bfloat16)
    low = (values - high.astype(np.float64)).astype(ml_dtypes.bfloat16)
    return high, low


def constants(steps):
    legendre = legendre_table()
    degree = np.arange(ORDER).astype(np.float32)
    weights = legendre * ((np.float32(2.0) * degree + np.float32(1.0)) / np.float32(WINDOW))[:, None]
    flipped = in_blocks(weights[:, ::-1], steps)
    high, low = halves(flipped)
    table = {}
    table["weights"] = flipped.astype(np.float32)
    table["weights_t"] = np.concatenate([high.T, low.T], 1)
    table["endpoint"] = legendre[:, 0][None, :].astype(np.float32)
    mode = np.arange(MODES)[:, None]
    step = np.arange(WINDOW)[None, :]
    angle = 2.0 * math.pi / WINDOW * (mode * step % WINDOW)
    cosine, sine = np.cos(angle), np.sin(angle)
    back = 2.0 * math.pi / WINDOW * (mode * (WINDOW - 1 - step) % WINDOW)
    table["turn"] = np.concatenate(
        [in_blocks(v, steps) for v in (cosine, sine, np.cos(back), np.sin(back))]
    ).astype(np.float32)
    scale = np.where(np.arange(MODES) == 0, 1.0, 2.0) / WINDOW
    table["scale"] = np.tile(scale, 4)[None, :].astype(np.float32)
    high, low = halves(in_blocks(np.concatenate([cosine, -sine]), steps))
    table["to_modes"] = np.concatenate([high.T, low.T], 1)
    wave = in_blocks(np.concatenate([scale[:, None] * cosine, -scale[:, None] * sine]), steps)
    table["from_modes"] = np.concatenate(halves(wave), 1)
    lane = np.arange(LANES)
    upper = (lane[:, None] <= lane[None, :]).astype(np.float32)
    ones = np.ones((LANES, LANES), np.float32)
    for name, part in (("earlier", upper), ("later", upper.T)):
        both = np.concatenate([part, ones], 1)
        table[name] = np.concatenate([both, both]).astype(ml_dtypes.bfloat16)
    return table


def split(value):
    high = value.astype(bf16)
    return high, (value - high.astype(f32)).astype(bf16)


def dot(a, b):
    return lax.dot_general(a, b, (((1,), (0,)), ((), ())), preferred_element_type=f32)


def dot_nt(a, b):
    return lax.dot_general(a, b, (((1,), (1,)), ((), ())), preferred_element_type=f32)


def stacked_dot(value, table):
    rows, width = value.shape[0], table.shape[1] // 2
    high, low = split(value)
    out = dot(jnp.concatenate([high, low], 0), table)
    return out[:rows, :width] + out[:rows, width:] + out[rows:, :width]


def scan_lanes(value, table):
    high, low = split(value)
    out = dot(jnp.concatenate([high, low], 1), table)
    return out[:, :LANES], out[:, LANES:]


def scan_lanes_exactly(value, table):
    high, low = split(value)
    last = (value - high.astype(f32) - low.astype(f32)).astype(bf16)
    out = dot(jnp.concatenate([high, low], 1), table) + dot(last, table[:LANES])
    return out[:, :LANES], out[:, LANES:]


def unpacked(ref, i, kind, count, steps):
    rows = ref.shape[0] // count
    if i < KIND:
        return ref[pl.ds(KIND * kind + i, count, stride=rows), :]
    lane = lax.broadcasted_iota(jnp.int32, (count, LANES), 1)
    value = None
    for p in reversed(range(3)):
        row = ref[pl.ds(KIND * kind + 4 * (i - KIND) + p, count, stride=rows), :]
        row = pltpu.roll(row, LANES - steps + EXTRA * p, 1)
        value = row if value is None else jnp.where(lane < EXTRA * (p + 1), row, value)
    return value


def pack_extra(ref, value, i, kind, rows, steps):
    count = value.shape[0]
    lane = lax.broadcasted_iota(jnp.int32, (count, LANES), 1)
    behind = (lane >= steps) & (lane < steps + EXTRA)
    for p in range(3):
        at = pl.ds(KIND * kind + 4 * (i - KIND) + p, count, stride=rows)
        ref[at, :] = jnp.where(behind, pltpu.roll(value, steps - EXTRA * p, 1), ref[at, :])


def owner_order(half):
    return [k ^ 1 for k in range(half)]


def owner_orders(blocks):
    half = blocks // HALVES
    return [[h * half + k for k in owner_order(half)] for h in range(HALVES)]


def first_order(blocks):
    return sum(owner_orders(blocks)[::-1], [])


def share_order(devices):
    sharing = devices // HALVES
    if sharing == 16:
        return [15, 1, 12, 14, 8, 4, 7, 3, 2, 11, 5, 6, 10, 0, 9, 13]
    return [int(k) for k in np.random.default_rng(0).permutation(sharing)]


def places(place_ref, blocks):
    block, core = place_ref[0] // CORES, place_ref[0] % CORES
    half = blocks // HALVES
    place = jnp.int32(0)
    for k, member in enumerate(owner_order(half)):
        place = jnp.where(block % half == member, k, place)
    return block, core, block // half, place


def to_wide(blocks, windows):
    per = len(blocks) // windows
    return jnp.concatenate(
        [jnp.concatenate(blocks[w * per : (w + 1) * per], 1) for w in range(windows)], 0
    )


def to_blocks(wide, windows):
    per = wide.shape[1] // LANES
    return [
        wide[w * SLOT : (w + 1) * SLOT, b * LANES : (b + 1) * LANES]
        for w in range(windows)
        for b in range(per)
    ]


def fetch(pairs, sems):
    copies = [pltpu.make_async_copy(a, b, sems.at[k]) for k, (a, b) in enumerate(pairs)]
    for copy in copies:
        copy.start()

    def ready(*which):
        for k in which:
            copies[k].wait()

    return ready


def blocks_of(value):
    return [value[k * SLOT : (k + 1) * SLOT] for k in range(value.shape[0] // SLOT)]


def same_rows(groups_ref, start, rows):
    channels = groups_ref.shape[1]
    ids = groups_ref[...].astype(f32)
    row = lax.broadcasted_iota(jnp.int32, (rows, channels), 0) + start
    lane = lax.broadcasted_iota(jnp.int32, (rows, channels), 1)
    column = jnp.sum(jnp.where(row == lane, ids, 0.0), axis=1, keepdims=True)
    return column == ids


def own_lanes(place, width, count, blocks):
    row = lax.broadcasted_iota(jnp.int32, (SLOT, width), 0)
    lane = lax.broadcasted_iota(jnp.int32, (SLOT, width), 1)
    return (lane == row * blocks + place) & (row < count)


def send_kernel(
    own,
    series_hbm,
    cot_hbm,
    mixing_hbm,
    groups_hbm,
    send_ref,
    grad_ref,
    series_ref,
    cot_ref,
    mixing_ref,
    groups_ref,
    pad_ref,
    sems,
):
    channels, steps = cot_ref.shape[1:]
    sets = channels // own
    ready = fetch(
        [
            (groups_hbm, groups_ref),
            (mixing_hbm, mixing_ref),
            (cot_hbm, cot_ref),
            (series_hbm, series_ref),
        ],
        sems,
    )
    rows = 2 * KIND
    pad_ref[...] = jnp.zeros_like(pad_ref)
    ready(2)
    pad_ref[:, :steps] = cot_ref[0]
    ready(0, 1)
    chunk = channels if channels <= 512 else 256
    total = None
    for start in range(0, channels, chunk):
        same = same_rows(groups_ref, start, chunk)
        masked = jnp.where(same, mixing_ref[start : start + chunk, :], 0.0)
        high, low = split(masked.T)
        both = jnp.concatenate(split(pad_ref[start : start + chunk, :]), 1)
        out = dot(jnp.concatenate([high, low], 0), both)
        part = out[:channels, :LANES] + out[:channels, LANES:] + out[channels:, :LANES]
        total = part if total is None else total + part
    spot = lax.broadcasted_iota(jnp.int32, (channels, LANES), 1) == LANES - 2
    sums = jnp.sum(pad_ref[...], axis=1, keepdims=True)
    grad_ref[...] = total
    ready(3)
    pad_ref[:, :steps] = series_ref[0]
    pad_ref[...] = jnp.where(spot, sums, pad_ref[...])
    for kind, ref in enumerate((pad_ref, grad_ref)):
        for i in range(own):
            value = ref[sets * i : sets * (i + 1), :]
            if kind and i < own - KIND:
                there = sets * (KIND + i)
                value = jnp.where(spot[:sets], sums[there : there + sets], value)
            if i < KIND:
                send_ref[pl.ds(KIND * kind + i, sets, stride=rows), :] = value
            else:
                pack_extra(send_ref, value, i, kind, rows, steps)
    for half in range(1, HALVES):
        send_ref[half * sets * rows : (half + 1) * sets * rows, :] = send_ref[0 : sets * rows, :]


def table_kernel(
    own,
    place_ref,
    cot_hbm,
    mixing_hbm,
    groups_hbm,
    gain_hbm,
    bias_hbm,
    out_bias_hbm,
    mode_in_hbm,
    mode_out_hbm,
    mode_re_hbm,
    mode_im_hbm,
    weights_hbm,
    endpoint_hbm,
    turn_hbm,
    scale_hbm,
    later_hbm,
    ahead_ref,
    lines_ref,
    own_ref,
    columns_ref,
    masked_ref,
    same_ref,
    cot_pad_ref,
    cot_send_ref,
    cot_ref,
    mixing_ref,
    groups_ref,
    gain_ref,
    bias_ref,
    out_bias_ref,
    mode_in_ref,
    mode_out_ref,
    mode_re_ref,
    mode_im_ref,
    weights_ref,
    endpoint_ref,
    turn_ref,
    scale_ref,
    later_ref,
    turned_ref,
    sems,
):
    ready = fetch(
        [
            (mode_in_hbm, mode_in_ref),
            (mode_out_hbm, mode_out_ref),
            (endpoint_hbm, endpoint_ref),
            (weights_hbm, weights_ref),
            (mode_re_hbm, mode_re_ref),
            (mode_im_hbm, mode_im_ref),
            (scale_hbm, scale_ref),
            (turn_hbm, turn_ref),
            (later_hbm, later_ref),
            (groups_hbm, groups_ref),
            (mixing_hbm, mixing_ref),
            (cot_hbm, cot_ref),
            (gain_hbm, gain_ref),
            (bias_hbm, bias_ref),
            (out_bias_hbm, out_bias_ref),
        ],
        sems,
    )
    channels, steps = cot_ref.shape[1:]
    width = ahead_ref.shape[0]
    per = width // LANES
    sets = channels // own
    count = 2 * MODES
    lines_ref[...] = jnp.zeros_like(lines_ref)
    turned_ref[...] = jnp.zeros_like(turned_ref)
    cot_pad_ref[...] = jnp.zeros_like(cot_pad_ref)
    ready(0, 1, 2, 3)
    kernel = lax.dot_general(
        mode_in_ref[...],
        weights_ref[...],
        (((1,), (0,)), ((), ())),
        precision=lax.Precision.HIGHEST,
        preferred_element_type=f32,
    )
    lines_ref[0:RANK, :] = kernel
    mix = jnp.sum(mode_out_ref[...] * endpoint_ref[...], axis=1, keepdims=True)
    ready(4, 5, 6)
    scale = scale_ref[:, 0:count]
    gain_re, gain_im = mode_re_ref[...], mode_im_ref[...]
    signed = jnp.concatenate([gain_re, -gain_im], 1) * scale
    sign = jnp.where(lax.broadcasted_iota(jnp.int32, (RANK, count), 1) < MODES, 1.0, -1.0)
    lines_ref[8 : 8 + RANK, 0:count] = signed * mix
    lines_ref[16 : 16 + RANK, 0:count] = sign * scale * mix
    lines_ref[24 : 24 + RANK, 0:count] = signed
    turned_ref[0:RANK, 0:count] = jnp.concatenate([gain_re, gain_im], 1) * mix
    columns = turned_ref[...].T[0:count]
    response = None
    for r in range(RANK):
        term = columns[:, r : r + 1] * kernel[r : r + 1, :]
        response = term if response is None else response + term
    ready(7, 8)
    real, imag = response[:MODES], response[MODES:]
    cosine, sine = turn_ref[0:MODES], turn_ref[MODES : 2 * MODES]
    cos_b, sin_b = turn_ref[2 * MODES : 3 * MODES], turn_ref[3 * MODES : 4 * MODES]
    turned = jnp.concatenate([real * cos_b + imag * sin_b, imag * cos_b - real * sin_b], 0)
    rows = jnp.concatenate([turned[:, b * LANES : (b + 1) * LANES] for b in range(per)], 0)
    local, total = scan_lanes_exactly(rows, later_ref[...])
    run = jnp.zeros((count, LANES), f32)
    suffix = [None] * per
    for b in reversed(range(per)):
        suffix[b] = local[b * count : (b + 1) * count] + run
        run = run + total[b * count : (b + 1) * count]
    for b in range(per):
        at = slice(b * LANES, (b + 1) * LANES)
        c, s = cosine[:, at], sine[:, at]
        parts = []
        for value in (suffix[b], run - suffix[b]):
            re, im = value[:MODES], value[MODES:]
            parts += [re * c + im * s, im * c - re * s]
        high, low = split(jnp.concatenate(parts, 0).T)
        ahead_ref[at, 0:LANES] = high
        ahead_ref[at, LANES : 2 * LANES] = low
    ready(9, 10, 11, 12, 13, 14)
    chunk = channels if channels <= 512 else 256
    for start in range(0, channels, chunk):
        at = slice(start, start + chunk)
        same = same_rows(groups_ref, start, chunk)
        high, low = split(jnp.where(same, mixing_ref[at, :], 0.0))
        masked_ref[0, at, :] = high
        masked_ref[1, at, :] = low
        same_ref[at, 0:channels] = jnp.where(same, 1.0, 0.0)
        row = lax.broadcasted_iota(jnp.int32, (chunk, channels), 0) + start
        lane = lax.broadcasted_iota(jnp.int32, (chunk, channels), 1)
        for k, ref in enumerate((gain_ref, bias_ref, out_bias_ref)):
            columns_ref[at, k : k + 1] = jnp.sum(
                jnp.where(row == lane, ref[...], 0.0), axis=1, keepdims=True
            )
    unused, unused, unused, place = places(place_ref, sets * HALVES)
    mine = own_lanes(place, channels, own, sets)
    gain = jnp.sum(jnp.where(mine, gain_ref[...], 0.0), axis=1, keepdims=True)
    gain = jnp.where(lax.broadcasted_iota(jnp.int32, (SLOT, 1), 0) < own, gain, 1.0)
    bias = jnp.sum(jnp.where(mine, bias_ref[...], 0.0), axis=1, keepdims=True)
    own_ref[0:SLOT, :] = jnp.broadcast_to(gain, (SLOT, LANES))
    own_ref[SLOT : 2 * SLOT, :] = jnp.broadcast_to(bias, (SLOT, LANES))
    own_ref[2 * SLOT : 3 * SLOT, :] = jnp.broadcast_to(1.0 / gain, (SLOT, LANES))
    own_ref[3 * SLOT :, :] = jnp.broadcast_to(scale_ref[...], (8, LANES))
    cot_pad_ref[:, :steps] = cot_ref[0]
    most = cot_send_ref.shape[0]
    lane = lax.broadcasted_iota(jnp.int32, (channels - most, LANES), 1)
    behind = (lane >= steps) & (lane < steps + EXTRA)
    cot_send_ref[...] = cot_pad_ref[0:most, :]
    for p in range(3):
        at = pl.ds(p, channels - most, stride=3)
        moved = pltpu.roll(cot_pad_ref[most:, :], steps - EXTRA * p, 1)
        cot_send_ref[at, :] = jnp.where(behind, moved, cot_send_ref[at, :])


def normalized(x, blocks, steps, earlier):
    rows = x.shape[0]
    local, total = scan_lanes(jnp.concatenate([x, x * x], 0), earlier)
    first, second = blocks_of(local[:rows]), blocks_of(local[rows:])
    first_all, second_all = blocks_of(total[:rows]), blocks_of(total[rows:])
    run_one = jnp.zeros((SLOT, LANES), f32)
    run_two = jnp.zeros((SLOT, LANES), f32)
    lane = lax.broadcasted_iota(jnp.int32, (SLOT, LANES), 1)
    found = []
    for k in range(blocks):
        inverse = 1.0 / (lane + (k * steps + 1 + WINDOW)).astype(f32)
        mean = (first[k] + run_one) * inverse
        variance = (second[k] + run_two + WINDOW) * inverse - mean * mean + EPSILON
        found.append((mean, variance, run_one, run_two))
        run_one = run_one + first_all[k]
        run_two = run_two + second_all[k]
    return found


def owned(recv_ref, tail_ref, own, blocks, steps):
    lane = lax.broadcasted_iota(jnp.int32, (blocks, LANES), 1)
    tail_ref[...] = jnp.zeros_like(tail_ref)
    for kind in range(2):
        for i in range(KIND, own):
            tail_ref[pl.ds(8 * kind + i - KIND, blocks, stride=16), :] = jnp.where(
                lane < steps, unpacked(recv_ref, i, kind, blocks, steps), 0.0
            )
    got = recv_ref[...].reshape(blocks, 2 * KIND, LANES)
    got = jnp.where(lax.broadcasted_iota(jnp.int32, got.shape, 2) < steps, got, 0.0)
    tail = tail_ref[...].reshape(blocks, 16, LANES)
    x = jnp.concatenate([got[:, 0:KIND], tail[:, 0:8]], 1)
    grad = jnp.concatenate([got[:, KIND : 2 * KIND], tail[:, 8:16]], 1)
    order = first_order(blocks)
    slots = [order.index(b) for b in range(blocks)]
    return [x[k] for k in slots], [grad[k] for k in slots]


def forward_kernel(
    own,
    blocks,
    steps,
    place_ref,
    recv_ref,
    own_ref,
    ahead_ref,
    from_modes_ref,
    to_modes_ref,
    earlier_ref,
    send_ref,
    mean_ref,
    inverse_ref,
    centered_ref,
    shifted_ref,
    grad_ref,
    normal_grad_ref,
    waves_ref,
    tail_ref,
    back_tail_ref,
):
    windows = blocks * steps // WINDOW
    x, grad = owned(recv_ref, tail_ref, own, blocks, steps)
    found = normalized(jnp.concatenate(x, 0), blocks, steps, earlier_ref[...])
    gain, bias, over = own_ref[0:SLOT], own_ref[SLOT : 2 * SLOT], own_ref[2 * SLOT : 3 * SLOT]
    row = lax.broadcasted_iota(jnp.int32, (SLOT, LANES), 0)
    lane = lax.broadcasted_iota(jnp.int32, (SLOT, LANES), 1)
    held = (row < own) & (lane < steps)
    normal, spreads, recon_grad = [], [], []
    for k in range(blocks):
        at = slice(k * SLOT, (k + 1) * SLOT)
        mean, variance = found[k][:2]
        inverse = lax.rsqrt(variance)
        spread = variance * inverse
        centered = (x[k] - mean) * inverse
        normal.append(gain * centered + bias)
        spreads.append(spread)
        recon_grad.append(jnp.where(held, grad[k] * spread * over, 0.0))
        mean_ref[at, :] = mean
        inverse_ref[at, :] = inverse
        centered_ref[at, :] = centered
        grad_ref[at, :] = grad[k]
    spectra = stacked_dot(to_wide(normal, windows), ahead_ref[...])
    waves = stacked_dot(to_wide(recon_grad, windows), to_modes_ref[...])
    count = 2 * MODES
    current, before = spectra[:, :count], spectra[:, count:]
    zero = jnp.zeros((SLOT, count), f32)
    after = zero
    if windows > 1:
        current = current + jnp.concatenate([zero, before[:-SLOT]], 0)
        after = jnp.concatenate([waves[SLOT:], zero], 0)
    recon = stacked_dot(current, from_modes_ref[...])
    waves = jnp.concatenate([waves, after], 1)
    waves_ref[...] = waves
    recon = to_blocks(recon, windows)
    normal_grad = to_blocks(convolved_back(waves * own_ref[3 * SLOT : 3 * SLOT + 1], ahead_ref[...]), windows)
    backs = []
    for b in range(blocks):
        at = slice(b * SLOT, (b + 1) * SLOT)
        shifted = (recon[b] - bias) * over
        shifted_ref[at, :] = shifted
        normal_grad_ref[at, :] = normal_grad[b]
        backs.append(shifted * spreads[b] + found[b][0])
    unused, unused, half, unused = places(place_ref, blocks)
    first = half == 0
    sets = blocks // HALVES
    count = 3 * KIND
    one, two = lane == LANES - 2, lane == LANES - 1
    for k, b in enumerate(owner_orders(blocks)[0]):
        c = b + sets
        arrays = [
            jnp.where(first, backs[b], backs[c]),
            jnp.where(first, backs[c], backs[b]),
            jnp.where(first, normal_grad[b], normal_grad[c]),
        ]
        run_one = jnp.where(first, found[b][2], found[c][2])
        run_two = jnp.where(first, found[b][3], found[c][3])
        arrays[0] = jnp.where(one, run_one, jnp.where(two, run_two, arrays[0]))
        send_ref[k * count : k * count + KIND, :] = arrays[0][:KIND]
        tail = jnp.where(one[:8], run_one[KIND:], jnp.where(two[:8], run_two[KIND:], arrays[1][:8]))
        send_ref[k * count + KIND : k * count + KIND + 8, :] = tail
        send_ref[k * count + KIND + 8 : k * count + 2 * KIND, :] = arrays[1][8:KIND]
        send_ref[k * count + 2 * KIND : k * count + 3 * KIND, :] = arrays[2][:KIND]
        for kind in range(3):
            back_tail_ref[(3 * k + kind) * 8 : (3 * k + kind + 1) * 8, :] = arrays[kind][KIND:]
    for kind in range(3):
        for i in range(KIND, own):
            value = back_tail_ref[pl.ds(8 * kind + i - KIND, sets, stride=24), :]
            pack_extra(send_ref, value, i, kind, count, steps)


def backward_kernel(
    own,
    blocks,
    steps,
    wide,
    place_ref,
    recv_ref,
    own_ref,
    mean_ref,
    inverse_ref,
    centered_ref,
    shifted_ref,
    grad_ref,
    normal_grad_ref,
    waves_ref,
    lines_ref,
    turn_hbm,
    weights_t_hbm,
    earlier_hbm,
    misc_ref,
    starts_ref,
    turn_ref,
    weights_t_ref,
    earlier_ref,
    sems,
):
    ready = fetch(
        [(turn_hbm, turn_ref), (earlier_hbm, earlier_ref), (weights_t_hbm, weights_t_ref)], sems
    )
    windows = blocks * steps // WINDOW
    count = 2 * MODES
    mean, inverse, centered, shifted, grad, normal_grad = (
        blocks_of(ref[...])
        for ref in (
            mean_ref,
            inverse_ref,
            centered_ref,
            shifted_ref,
            grad_ref,
            normal_grad_ref,
        )
    )
    gain, bias, over = own_ref[0:SLOT], own_ref[SLOT : 2 * SLOT], own_ref[2 * SLOT : 3 * SLOT]
    row = lax.broadcasted_iota(jnp.int32, (SLOT, LANES), 0)
    lane = lax.broadcasted_iota(jnp.int32, (SLOT, LANES), 1)
    held = (row < own) & (lane < steps)
    waves = waves_ref[...]
    gain_sum = jnp.zeros((SLOT, LANES), f32)
    bias_sum = jnp.zeros((SLOT, LANES), f32)
    normal, ones, twos = [], [], []
    for k in range(blocks):
        over_q = 1.0 / (lane + (k * steps + 1 + WINDOW)).astype(f32)
        normal.append(jnp.where(held, gain * centered[k] + bias, 0.0))
        recon_grad = grad[k] / inverse[k] * over
        gain_sum = gain_sum + normal_grad[k] * centered[k] - recon_grad * shifted[k]
        bias_sum = bias_sum + normal_grad[k] - recon_grad
        first, second = statistics(
            grad[k],
            shifted[k],
            normal_grad[k] * gain * inverse[k],
            centered[k],
            mean[k],
            inverse[k],
            over_q,
        )
        ones.append(jnp.where(held, first, 0.0))
        twos.append(jnp.where(held, second, 0.0))
    gain_sum, bias_sum = jnp.where(held, gain_sum, 0.0), jnp.where(held, bias_sum, 0.0)
    ready(1)
    high, low = split(jnp.concatenate(ones + twos, 0))
    total = blocks_of(dot(jnp.concatenate([high, low], 1), earlier_ref[:, LANES:]))
    run_one = jnp.zeros((SLOT, LANES), f32)
    run_two = jnp.zeros((SLOT, LANES), f32)
    unused, unused, half, place = places(place_ref, blocks)
    first = half == 0
    sets = blocks // HALVES
    starts = [None] * blocks
    for k in reversed(range(blocks)):
        both = jnp.where(lane == row, run_one, jnp.where(lane == row + 32, run_two, 0.0))
        starts[k] = jnp.sum(both, 0, keepdims=True)
        run_one = run_one + total[k]
        run_two = run_two + total[blocks + k]
    for at, device in enumerate(share_order(blocks * CORES)):
        k = device // CORES
        starts_ref[at : at + 1, :] = jnp.where(first, starts[k], starts[k + sets])
    signal = to_wide(normal, windows)
    high, low = split(signal)
    w_high, w_low = split(waves.T)
    pairs = dot(
        jnp.concatenate([w_high, w_high, w_low], 1), jnp.concatenate([high, low, high], 0)
    )
    ready(0)
    cosine, sine = turn_ref[0:MODES], turn_ref[MODES : 2 * MODES]
    cos_b, sin_b = turn_ref[2 * MODES : 3 * MODES], turn_ref[3 * MODES : 4 * MODES]

    def turned(value):
        re, im = value[:MODES], value[MODES:]
        return jnp.concatenate([re * cosine - im * sine, -(re * sine + im * cosine)], 0)

    per = pairs.shape[1] // LANES
    after = turned(pairs[count:])
    left = turned(pairs[:count]) - after
    after = sum(after[:, b * LANES : (b + 1) * LANES] for b in range(per))
    local, total = scan_lanes(
        jnp.concatenate([left[:, b * LANES : (b + 1) * LANES] for b in range(per)], 0),
        earlier_ref[...],
    )
    run = jnp.broadcast_to(jnp.sum(after, 1, keepdims=True), (count, LANES))
    sums = []
    for b in range(per):
        sums.append(local[b * count : (b + 1) * count] + run)
        run = run + total[b * count : (b + 1) * count]
    sums = jnp.concatenate(sums, 1)
    re, im = sums[:MODES], sums[MODES:]
    crossed = jnp.concatenate([re * cos_b + im * sin_b, im * cos_b - re * sin_b], 0)
    high, low = split(crossed)
    s_high, s_low = split(lines_ref[8:16, 0:count])
    kernel_grad = dot(
        jnp.concatenate([s_high, s_high, s_low], 1), jnp.concatenate([high, low, high], 0)
    )
    k_high, k_low = split(lines_ref[0:8, :])
    overlap = dot_nt(
        jnp.concatenate([k_high, k_high, k_low], 1), jnp.concatenate([high, low, high], 1)
    )
    modes = overlap * lines_ref[16:24, 0:count]
    mix_grad = jnp.sum(overlap * lines_ref[24:32, 0:count], axis=1, keepdims=True)
    ready(2)
    mode_in_grad = stacked_dot(kernel_grad, weights_t_ref[...])
    misc_ref[...] = jnp.zeros_like(misc_ref)
    misc_ref[0:RANK, :] = mode_in_grad[0:RANK, :LANES]
    misc_ref[RANK : 2 * RANK, :] = mode_in_grad[0:RANK, LANES:]
    misc_ref[8 : 8 + RANK, 0:count] = modes[0:RANK]
    misc_ref[8 : 8 + RANK, count : 2 * count] = jnp.broadcast_to(mix_grad, (8, count))[0:RANK]
    mine = own_lanes(place, wide, own, sets)
    at = 12
    gain_row = jnp.sum(
        jnp.where(mine, jnp.sum(gain_sum, 1, keepdims=True), 0.0), axis=0, keepdims=True
    )
    bias_row = jnp.sum(
        jnp.where(mine, jnp.sum(bias_sum, 1, keepdims=True), 0.0), axis=0, keepdims=True
    )
    cot_sum = jnp.sum(recv_ref[...].reshape(blocks, 2 * KIND, LANES), axis=0)[:SLOT]
    cot_row = jnp.sum(
        jnp.where(mine, cot_sum[:, LANES - 2 : LANES - 1], 0.0), axis=0, keepdims=True
    )
    for value in (gain_row, bias_row, cot_row):
        for j in range(wide // LANES):
            misc_ref[at : at + 1, :] = value[:, j * LANES : (j + 1) * LANES]
            at += 1


def convolved_back(waves, ahead):
    rows = waves.shape[0]
    high, low = split(waves)
    out = dot_nt(jnp.concatenate([high, low], 0), ahead[:, :LANES])
    return out[:rows] + out[rows:] + dot_nt(high, ahead[:, LANES:])


def statistics(grad, shifted, scaled, centered, mean, inverse, over_q):
    variance_grad = (grad * shifted - scaled * centered) * (0.5 * inverse)
    first = (grad - scaled - 2.0 * mean * variance_grad) * over_q
    return first, variance_grad * over_q


def pieces(channels, devices):
    tiles, rest = channels // LANES, channels % LANES
    each = channels // devices
    rest_rows = channels * rest // LANES
    misc_rows = 12 + 3 * (up(channels, LANES) // LANES)
    extra = up(rest_rows + misc_rows, devices) // devices
    return tiles, rest, each, rest_rows, misc_rows, extra


def gathered(recv_ref, kind, own, steps, dense_ref):
    sets = recv_ref.shape[0] // (3 * KIND)
    for i in range(own):
        dense_ref[sets * i : sets * (i + 1), :] = unpacked(recv_ref, i, kind, sets, steps)


def mix_kernel(
    own,
    devices,
    steps,
    recv_ref,
    same_ref,
    cot_ref,
    cot_partner_ref,
    misc_ref,
    starts_ref,
    send_ref,
    dense_ref,
    partner_ref,
    cot_all_ref,
    misc_all_ref,
):
    channels = same_ref.shape[0]
    tiles, rest, each, rest_rows, misc_rows, extra = pieces(channels, devices)
    slot = send_ref.shape[0] // devices
    most = cot_partner_ref.shape[0]
    cot = cot_partner_ref[...]
    cot_all_ref[0:most, :] = jnp.where(
        lax.broadcasted_iota(jnp.int32, cot.shape, 1) < steps, cot, 0.0
    )
    lane = lax.broadcasted_iota(jnp.int32, (channels - most, LANES), 1)
    cot = jnp.zeros((channels - most, LANES), f32)
    for p in reversed(range(3)):
        row = cot_partner_ref[pl.ds(p, channels - most, stride=3), :]
        row = pltpu.roll(row, LANES - steps + EXTRA * p, 1)
        cot = jnp.where(lane < min(EXTRA * (p + 1), steps), row, cot)
    cot_all_ref[most:, :] = cot
    three = []
    for kind, ref in enumerate((dense_ref, partner_ref)):
        if ref.shape[0] > channels:
            ref[channels:, :] = jnp.zeros((ref.shape[0] - channels, LANES), f32)
        gathered(recv_ref, kind, own, steps, ref)
        high, low = split(ref[...])
        three += [high, low, high]
    three = jnp.concatenate(three, 1)
    chunk = channels if channels <= 512 else devices
    for start in range(0, channels, chunk):
        at = slice(start, start + chunk)
        six = []
        for ref in (cot_ref, cot_all_ref):
            high, low = split(ref[at, :])
            six += [high, high, low]
        grad = dot_nt(jnp.concatenate(six, 1), three)
        for j in range(tiles):
            lanes = slice(j * LANES, (j + 1) * LANES)
            tile = grad[:, lanes] * same_ref[at, lanes]
            for i in range(chunk // devices):
                send_ref[pl.ds(j * each + start // devices + i, devices, stride=slot), :] = tile[
                    devices * i : devices * (i + 1)
                ]
        if rest:
            lanes = slice(tiles * LANES, tiles * LANES + LANES)
            last = grad[:, lanes] * same_ref[at, lanes]
            folded = last[0:rest_rows]
            for g in range(1, LANES // rest):
                folded = folded + pltpu.roll(
                    last[g * rest_rows : (g + 1) * rest_rows], g * rest, 1
                )
            misc_all_ref[0:rest_rows, :] = folded
    end = rest_rows + misc_rows
    misc_all_ref[rest_rows:end, :] = misc_ref[0:misc_rows, :]
    if misc_all_ref.shape[0] > end:
        misc_all_ref[end:, :] = jnp.zeros((misc_all_ref.shape[0] - end, LANES), f32)
    for k in range(extra):
        send_ref[pl.ds(tiles * each + k, devices, stride=slot), :] = misc_all_ref[
            devices * k : devices * (k + 1), :
        ]
    for k in range(tiles * each + extra, slot - 1):
        send_ref[pl.ds(k, devices, stride=slot), :] = jnp.zeros((devices, LANES), f32)
    send_ref[pl.ds(slot - 1, devices, stride=slot), :] = starts_ref[...]


def steps_kernel(
    own,
    devices,
    place_ref,
    recv_ref,
    shares_ref,
    grad_ref,
    columns_ref,
    masked_ref,
    series_hbm,
    cot_hbm,
    earlier_hbm,
    later_hbm,
    out_ref,
    series_grad_ref,
    series_ref,
    cot_ref,
    earlier_ref,
    later_ref,
    dense_ref,
    back_ref,
    sums_ref,
    pad_ref,
    sems,
):
    ready = fetch(
        [
            (series_hbm, series_ref),
            (cot_hbm, cot_ref),
            (earlier_hbm, earlier_ref),
            (later_hbm, later_ref),
        ],
        sems,
    )
    channels, steps = series_ref.shape[1:]
    sets = channels // own
    block, core, unused, unused = places(place_ref, sets * HALVES)
    gathered(recv_ref, 0, own, steps, dense_ref)
    gathered(recv_ref, 2, own, steps, back_ref)
    for i in range(own):
        sums_ref[sets * i : sets * (i + 1), :] = recv_ref[pl.ds(i, sets, stride=3 * KIND), :]
    pad_ref[...] = jnp.zeros_like(pad_ref)
    gain, bias, shift = (columns_ref[:, k : k + 1] for k in range(3))
    restored = dense_ref[...]
    both = jnp.concatenate(split(restored), 1)
    ready(0)
    pad_ref[:, :steps] = series_ref[0]
    chunk = channels if channels <= 512 else 256
    for start in range(0, channels, chunk):
        at = slice(start, start + chunk)
        out = dot(jnp.concatenate([masked_ref[0, at, :], masked_ref[1, at, :]], 0), both)
        mixed = out[:chunk, :LANES] + out[:chunk, LANES:] + out[chunk:, :LANES]
        out_ref[0, at, :] = (pad_ref[at, :] + mixed + shift[at])[:, :steps]
    x = pad_ref[...]
    ready(2)
    local, unused = scan_lanes(jnp.concatenate([x, x * x], 0), earlier_ref[...])
    lane = lax.broadcasted_iota(jnp.int32, (channels, LANES), 1)
    over_q = 1.0 / (lane + (block * steps + 1 + WINDOW)).astype(f32)
    mean = (local[:channels] + sums_ref[:, LANES - 2 : LANES - 1]) * over_q
    variance = (local[channels:] + sums_ref[:, LANES - 1 : LANES] + WINDOW) * over_q
    inverse = lax.rsqrt(variance - mean * mean + EPSILON)
    centered = (x - mean) * inverse
    scaled = back_ref[...] * gain * inverse
    first, second = statistics(
        grad_ref[...], (restored - mean) * inverse, scaled, centered, mean, inverse, over_q
    )
    held = lane < steps
    ready(3)
    local, unused = scan_lanes(
        jnp.concatenate([jnp.where(held, first, 0.0), jnp.where(held, second, 0.0)], 0),
        later_ref[...],
    )
    slot = shares_ref.shape[0] // devices
    rows = []
    order = share_order(devices * HALVES)
    for owner in owner_orders(sets * HALVES)[0]:
        even, odd = (order.index(owner * CORES + r) * slot + slot - 1 for r in range(CORES))
        rows.append(
            jnp.where(core == 0, shares_ref[even : even + 1, :], shares_ref[odd : odd + 1, :])
        )
    later = jnp.concatenate(rows, 0)
    part = scaled + local[:channels] + 2.0 * x * local[channels:]
    ready(1)
    for i in range(own):
        at = slice(sets * i, sets * (i + 1))
        sums = later[:, i : i + 1] + 2.0 * x[at] * later[:, 32 + i : 33 + i]
        series_grad_ref[0, at, :] = cot_ref[0, at, :] + (part[at] + sums)[:, :steps]


def sum_kernel(devices, recv_ref, send_ref):
    slot = recv_ref.shape[0] // devices
    total = recv_ref[0:slot, :]
    for s in range(1, devices):
        total = total + recv_ref[s * slot : (s + 1) * slot, :]
    for s in range(devices):
        send_ref[s * slot : (s + 1) * slot, :] = total


def spread_kernel(
    devices,
    recv_ref,
    endpoint_ref,
    gain_ref,
    bias_ref,
    mode_in_ref,
    mode_out_ref,
    mode_re_ref,
    mode_im_ref,
    mixing_ref,
    out_bias_ref,
    misc_ref,
):
    channels = mixing_ref.shape[0]
    tiles, rest, each, rest_rows, misc_rows, extra = pieces(channels, devices)
    slot = recv_ref.shape[0] // devices
    for j in range(tiles):
        for i in range(each):
            mixing_ref[devices * i : devices * (i + 1), j * LANES : (j + 1) * LANES] = recv_ref[
                pl.ds(j * each + i, devices, stride=slot), :
            ]
    for k in range(extra):
        misc_ref[devices * k : devices * (k + 1), :] = recv_ref[
            pl.ds(tiles * each + k, devices, stride=slot), :
        ]
    if rest:
        folded = misc_ref[0:rest_rows, :]
        for g in range(LANES // rest):
            piece = folded if g == 0 else pltpu.roll(folded, LANES - g * rest, 1)
            mixing_ref[g * rest_rows : (g + 1) * rest_rows, tiles * LANES :] = piece[:, :rest]
    at = rest_rows
    mode_in_ref[:, 0:LANES] = misc_ref[at : at + RANK, :]
    mode_in_ref[:, LANES : 2 * LANES] = misc_ref[at + RANK : at + 2 * RANK, :]
    modes = misc_ref[at + 8 : at + 8 + RANK, :]
    mode_re_ref[...] = modes[:, 0:MODES]
    mode_im_ref[...] = modes[:, MODES : 2 * MODES]
    mode_out_ref[...] = modes[:, 2 * MODES : 2 * MODES + 1] * endpoint_ref[...]
    at += 12
    for ref in (gain_ref, bias_ref, out_bias_ref):
        for start in range(0, channels, LANES):
            size = min(LANES, channels - start)
            ref[:, start : start + size] = misc_ref[at : at + 1, 0:size]
            at += 1


def call(kernel, outs, smem=(), vmem=(), hbm=(), scratch=(), cost=None, limit=None):
    in_vmem = pl.BlockSpec(memory_space=pltpu.VMEM)
    in_smem = pl.BlockSpec(memory_space=pltpu.SMEM)
    in_hbm = pl.BlockSpec(memory_space=pltpu.HBM)
    held = [pltpu.VMEM(a.shape, a.dtype) for a in hbm] + list(scratch)
    if hbm:
        held.append(pltpu.SemaphoreType.DMA((len(hbm),)))
    hbm = [pltpu.with_memory_space_constraint(a, pltpu.HBM) for a in hbm]
    return pl.pallas_call(
        kernel,
        out_shape=tuple(jax.ShapeDtypeStruct(shape, kind) for shape, kind in outs),
        in_specs=[in_smem] * len(smem) + [in_vmem] * len(vmem) + [in_hbm] * len(hbm),
        out_specs=tuple(in_vmem for unused in outs),
        scratch_shapes=held,
        compiler_params=pltpu.CompilerParams(vmem_limit_bytes=limit),
        cost_estimate=cost,
    )(*smem, *vmem, *hbm)


def exchange(value, axis, orders):
    count = len(orders[0])
    out = lax.all_to_all(
        value.reshape(count, value.shape[0] // count, value.shape[1]),
        axis,
        split_axis=0,
        concat_axis=0,
        axis_index_groups=orders,
    )
    return out.reshape(value.shape)


def body(
    series,
    group_ids,
    rev_gain,
    rev_bias,
    mode_in,
    mode_out,
    mode_re,
    mode_im,
    mixing,
    out_bias,
    cotangent,
):
    samples, channels, steps = series.shape
    blocks = lax.axis_size("seq")
    sets = blocks // HALVES
    devices = blocks * lax.axis_size("rep")
    sharing = devices // HALVES
    own = channels // sets
    width = WINDOW // steps * LANES
    padded = up(channels, LANES)
    place = lax.axis_index(("seq", "rep")).astype(jnp.int32).reshape(1)
    halves_of = owner_orders(blocks)
    all_of = [first_order(blocks)]
    shares_of = [[h * sharing + k for k in share_order(devices)] for h in range(HALVES)]
    const = {name: jnp.asarray(value) for name, value in constants(steps).items()}
    groups = group_ids.reshape(1, channels)
    limit = (16 if channels <= 512 else 56) * 2**20
    run = functools.partial(call, limit=limit)
    busy = pl.CostEstimate(flops=4_000_000_000, bytes_accessed=8_000_000, transcendentals=0)
    brief = pl.CostEstimate(flops=100_000_000, bytes_accessed=1_000_000, transcendentals=0)

    send, restored_grad = run(
        functools.partial(send_kernel, own),
        [((blocks * 2 * KIND, LANES), f32), ((channels, LANES), f32)],
        hbm=(series, cotangent, mixing, groups),
        scratch=[pltpu.VMEM((channels, LANES), f32)],
        cost=brief,
    )
    ahead, lines, mine, columns, masked, same, cot, cot_send = run(
        functools.partial(table_kernel, own),
        [
            ((width, 2 * LANES), bf16),
            ((32, width), f32),
            ((3 * SLOT + 8, LANES), f32),
            ((channels, LANES), f32),
            ((2, channels, channels), bf16),
            ((channels, padded), f32),
            ((channels, LANES), f32),
            ((channels * 3 // 4, LANES), f32),
        ],
        smem=(place,),
        hbm=(
            cotangent,
            mixing,
            groups,
            rev_gain.reshape(1, channels),
            rev_bias.reshape(1, channels),
            out_bias.reshape(1, channels),
            mode_in.T,
            mode_out.T,
            mode_re,
            mode_im,
            const["weights"],
            const["endpoint"],
            const["turn"],
            const["scale"],
            const["later"],
        ),
        scratch=[pltpu.VMEM((LANES, LANES), f32)],
        cost=busy,
    )
    owned_rows = exchange(send, "seq", all_of)
    rows = blocks * SLOT
    windows = blocks * steps // WINDOW
    send, *kept = run(
        functools.partial(forward_kernel, own, blocks, steps),
        [((sets * 3 * KIND, LANES), f32)]
        + [((rows, LANES), f32)] * 6
        + [((windows * SLOT, LANES), f32)],
        smem=(place,),
        vmem=(
            owned_rows,
            mine,
            ahead,
            const["from_modes"],
            const["to_modes"],
            const["earlier"],
        ),
        scratch=[pltpu.VMEM((blocks * 16, LANES), f32), pltpu.VMEM((sets * 24, LANES), f32)],
        cost=brief,
    )
    there = exchange(send, "seq", halves_of)
    cot_send, kept[0] = lax.optimization_barrier((cot_send, kept[0]))
    cot_partner = lax.ppermute(cot_send, "seq", [(k, (k + sets) % blocks) for k in range(blocks)])
    tiles, rest, each, rest_rows, misc_rows, extra = pieces(channels, sharing)
    slot = up(tiles * each + extra + 1, 8)
    misc, starts = run(
        functools.partial(backward_kernel, own, blocks, steps, padded),
        [
            ((up(misc_rows, 8), LANES), f32),
            ((sharing, LANES), f32),
        ],
        smem=(place,),
        vmem=(owned_rows, mine, *kept, lines),
        hbm=(const["turn"], const["weights_t"], const["earlier"]),
        cost=busy,
    )
    (send,) = run(
        functools.partial(mix_kernel, own, sharing, steps),
        [((sharing * slot, LANES), f32)],
        vmem=(there, same, cot, cot_partner, misc, starts),
        scratch=[
            pltpu.VMEM((padded, LANES), f32),
            pltpu.VMEM((padded, LANES), f32),
            pltpu.VMEM((channels, LANES), f32),
            pltpu.VMEM((up(extra * sharing, 8), LANES), f32),
        ],
        cost=brief,
    )
    shares = exchange(send, ("seq", "rep"), shares_of)
    (send,) = run(
        functools.partial(sum_kernel, sharing),
        [((sharing * slot, LANES), f32)],
        vmem=(shares,),
        cost=brief,
    )
    sums = exchange(send, ("seq", "rep"), shares_of)
    layer_out, series_grad = run(
        functools.partial(steps_kernel, own, sharing),
        [((1, channels, steps), f32), ((1, channels, steps), f32)],
        smem=(place,),
        vmem=(there, shares, restored_grad, columns, masked),
        hbm=(series, cotangent, const["earlier"], const["later"]),
        scratch=[pltpu.VMEM((channels, LANES), f32)] * 4,
        cost=busy,
    )
    outs = run(
        functools.partial(spread_kernel, sharing),
        [
            ((1, channels), f32),
            ((1, channels), f32),
            ((RANK, ORDER), f32),
            ((RANK, ORDER), f32),
            ((RANK, MODES), f32),
            ((RANK, MODES), f32),
            ((channels, channels), f32),
            ((1, channels), f32),
        ],
        vmem=(sums, const["endpoint"]),
        scratch=[pltpu.VMEM((up(extra * sharing, 8), LANES), f32)],
        cost=brief,
    )
    return (
        layer_out,
        series_grad,
        outs[0].reshape(channels),
        outs[1].reshape(channels),
        outs[2].T,
        outs[3].T,
        outs[4],
        outs[5],
        outs[6],
        outs[7].reshape(channels),
    )


def solution(mesh):
    time_split = P("rep", None, "seq")
    in_specs = (time_split,) + (P(),) * 9 + (time_split,)
    out_specs = (time_split, time_split) + (P(),) * 8
    return jax.shard_map(body, mesh=mesh, in_specs=in_specs, out_specs=out_specs, check_vma=False)
```

```python
import functools
import math

import jax
import jax.numpy as jnp
import ml_dtypes
import numpy as np
from jax import lax
from jax.experimental import pallas as pl
from jax.experimental.pallas import tpu as pltpu
from jax.sharding import PartitionSpec as P

ORDER = 256
MODES = 32
RANK = 4
WINDOW = 720
EPSILON = 1e-05

LANES = 128
CORES = 2
HALVES = 2
SLOT = 24
KIND = 16
EXTRA = 36
f32 = jnp.float32
bf16 = jnp.bfloat16


def up(value, multiple):
    return -(-value // multiple) * multiple


def legendre_table():
    one, two = np.float32(1.0), np.float32(2.0)
    lags = np.arange(WINDOW).astype(np.float32)
    points = one - (two * (lags + np.float32(0.5))) * np.float32(1.0 / WINDOW)
    lower, this = np.zeros_like(points), np.ones_like(points)
    rows = []
    for degree in np.arange(ORDER).astype(np.float32):
        rows.append(this)
        upper = ((two * degree + one) * points * this - degree * lower) / (degree + one)
        lower, this = this, upper
    return np.stack(rows)


def in_blocks(values, steps):
    blocks = WINDOW // steps
    framed = np.zeros(values.shape[:-1] + (blocks, LANES))
    framed[..., :steps] = values.reshape(values.shape[:-1] + (blocks, steps))
    return framed.reshape(values.shape[:-1] + (blocks * LANES,))


def halves(values):
    high = values.astype(np.float32).astype(ml_dtypes.bfloat16)
    low = (values - high.astype(np.float64)).astype(ml_dtypes.bfloat16)
    return high, low


def constants(steps):
    legendre = legendre_table()
    degree = np.arange(ORDER).astype(np.float32)
    weights = legendre * ((np.float32(2.0) * degree + np.float32(1.0)) / np.float32(WINDOW))[:, None]
    flipped = in_blocks(weights[:, ::-1], steps)
    high, low = halves(flipped)
    table = {}
    table["weights"] = flipped.astype(np.float32)
    table["weights_t"] = np.concatenate([high.T, low.T], 1)
    table["endpoint"] = legendre[:, 0][None, :].astype(np.float32)
    mode = np.arange(MODES)[:, None]
    step = np.arange(WINDOW)[None, :]
    angle = 2.0 * math.pi / WINDOW * (mode * step % WINDOW)
    cosine, sine = np.cos(angle), np.sin(angle)
    back = 2.0 * math.pi / WINDOW * (mode * (WINDOW - 1 - step) % WINDOW)
    table["turn"] = np.concatenate(
        [in_blocks(v, steps) for v in (cosine, sine, np.cos(back), np.sin(back))]
    ).astype(np.float32)
    scale = np.where(np.arange(MODES) == 0, 1.0, 2.0) / WINDOW
    table["scale"] = np.tile(scale, 4)[None, :].astype(np.float32)
    high, low = halves(in_blocks(np.concatenate([cosine, -sine]), steps))
    table["to_modes"] = np.concatenate([high.T, low.T], 1)
    wave = in_blocks(np.concatenate([scale[:, None] * cosine, -scale[:, None] * sine]), steps)
    table["from_modes"] = np.concatenate(halves(wave), 1)
    lane = np.arange(LANES)
    upper = (lane[:, None] <= lane[None, :]).astype(np.float32)
    ones = np.ones((LANES, LANES), np.float32)
    for name, part in (("earlier", upper), ("later", upper.T)):
        both = np.concatenate([part, ones], 1)
        table[name] = np.concatenate([both, both]).astype(ml_dtypes.bfloat16)
    return table


def split(value):
    high = value.astype(bf16)
    return high, (value - high.astype(f32)).astype(bf16)


def dot(a, b):
    return lax.dot_general(a, b, (((1,), (0,)), ((), ())), preferred_element_type=f32)


def dot_nt(a, b):
    return lax.dot_general(a, b, (((1,), (1,)), ((), ())), preferred_element_type=f32)


def stacked_dot(value, table):
    rows, width = value.shape[0], table.shape[1] // 2
    high, low = split(value)
    out = dot(jnp.concatenate([high, low], 0), table)
    return out[:rows, :width] + out[:rows, width:] + out[rows:, :width]


def scan_lanes(value, table):
    high, low = split(value)
    out = dot(jnp.concatenate([high, low], 1), table)
    return out[:, :LANES], out[:, LANES:]


def scan_lanes_exactly(value, table):
    high, low = split(value)
    last = (value - high.astype(f32) - low.astype(f32)).astype(bf16)
    out = dot(jnp.concatenate([high, low], 1), table) + dot(last, table[:LANES])
    return out[:, :LANES], out[:, LANES:]


def unpacked(ref, i, kind, count, steps):
    rows = ref.shape[0] // count
    if i < KIND:
        return ref[pl.ds(KIND * kind + i, count, stride=rows), :]
    lane = lax.broadcasted_iota(jnp.int32, (count, LANES), 1)
    value = None
    for p in reversed(range(3)):
        row = ref[pl.ds(KIND * kind + 4 * (i - KIND) + p, count, stride=rows), :]
        row = pltpu.roll(row, LANES - steps + EXTRA * p, 1)
        value = row if value is None else jnp.where(lane < EXTRA * (p + 1), row, value)
    return value


def pack_extra(ref, value, i, kind, rows, steps):
    count = value.shape[0]
    lane = lax.broadcasted_iota(jnp.int32, (count, LANES), 1)
    behind = (lane >= steps) & (lane < steps + EXTRA)
    for p in range(3):
        at = pl.ds(KIND * kind + 4 * (i - KIND) + p, count, stride=rows)
        ref[at, :] = jnp.where(behind, pltpu.roll(value, steps - EXTRA * p, 1), ref[at, :])


def owner_order(half):
    return [k ^ 1 for k in range(half)]


def owner_orders(blocks):
    half = blocks // HALVES
    return [[h * half + k for k in owner_order(half)] for h in range(HALVES)]


def first_order(blocks):
    return sum(owner_orders(blocks)[::-1], [])


def share_order(devices):
    sharing = devices // HALVES
    if sharing == 16:
        return [15, 1, 12, 8, 14, 4, 7, 3, 2, 11, 5, 6, 0, 10, 9, 13]
    return [int(k) for k in np.random.default_rng(0).permutation(sharing)]


def places(place_ref, blocks):
    block, core = place_ref[0] // CORES, place_ref[0] % CORES
    half = blocks // HALVES
    place = jnp.int32(0)
    for k, member in enumerate(owner_order(half)):
        place = jnp.where(block % half == member, k, place)
    return block, core, block // half, place


def to_wide(blocks, windows):
    per = len(blocks) // windows
    return jnp.concatenate(
        [jnp.concatenate(blocks[w * per : (w + 1) * per], 1) for w in range(windows)], 0
    )


def to_blocks(wide, windows):
    per = wide.shape[1] // LANES
    return [
        wide[w * SLOT : (w + 1) * SLOT, b * LANES : (b + 1) * LANES]
        for w in range(windows)
        for b in range(per)
    ]


def fetch(pairs, sems):
    copies = [pltpu.make_async_copy(a, b, sems.at[k]) for k, (a, b) in enumerate(pairs)]
    for copy in copies:
        copy.start()

    def ready(*which):
        for k in which:
            copies[k].wait()

    return ready


def blocks_of(value):
    return [value[k * SLOT : (k + 1) * SLOT] for k in range(value.shape[0] // SLOT)]


def same_rows(groups_ref, start, rows):
    channels = groups_ref.shape[1]
    ids = groups_ref[...].astype(f32)
    row = lax.broadcasted_iota(jnp.int32, (rows, channels), 0) + start
    lane = lax.broadcasted_iota(jnp.int32, (rows, channels), 1)
    column = jnp.sum(jnp.where(row == lane, ids, 0.0), axis=1, keepdims=True)
    return column == ids


def own_lanes(place, width, count, blocks):
    row = lax.broadcasted_iota(jnp.int32, (SLOT, width), 0)
    lane = lax.broadcasted_iota(jnp.int32, (SLOT, width), 1)
    return (lane == row * blocks + place) & (row < count)


def send_kernel(
    own,
    series_hbm,
    cot_hbm,
    mixing_hbm,
    groups_hbm,
    send_ref,
    grad_ref,
    series_ref,
    cot_ref,
    mixing_ref,
    groups_ref,
    pad_ref,
    sems,
):
    channels, steps = cot_ref.shape[1:]
    sets = channels // own
    ready = fetch(
        [
            (groups_hbm, groups_ref),
            (mixing_hbm, mixing_ref),
            (cot_hbm, cot_ref),
            (series_hbm, series_ref),
        ],
        sems,
    )
    rows = 2 * KIND
    pad_ref[...] = jnp.zeros_like(pad_ref)
    ready(2)
    pad_ref[:, :steps] = cot_ref[0]
    ready(0, 1)
    chunk = channels if channels <= 512 else 256
    total = None
    for start in range(0, channels, chunk):
        same = same_rows(groups_ref, start, chunk)
        masked = jnp.where(same, mixing_ref[start : start + chunk, :], 0.0)
        high, low = split(masked.T)
        both = jnp.concatenate(split(pad_ref[start : start + chunk, :]), 1)
        out = dot(jnp.concatenate([high, low], 0), both)
        part = out[:channels, :LANES] + out[:channels, LANES:] + out[channels:, :LANES]
        total = part if total is None else total + part
    lane = lax.broadcasted_iota(jnp.int32, (channels, LANES), 1)
    spot = lane == LANES - 2
    behind = (lane[:sets] >= steps) & (lane[:sets] < steps + EXTRA)
    sums = jnp.sum(pad_ref[...], axis=1, keepdims=True)
    grad_ref[...] = total
    ready(3)
    pad_ref[:, :steps] = series_ref[0]
    pad_ref[...] = jnp.where(spot, sums, pad_ref[...])
    for kind, ref in enumerate((pad_ref, grad_ref)):
        for i in range(KIND):
            value = ref[sets * i : sets * (i + 1), :]
            if kind and i < own - KIND:
                there = sets * (KIND + i)
                value = jnp.where(spot[:sets], sums[there : there + sets], value)
            there, p = sets * (KIND + i // 4), i % 4
            if there < channels and p < 3:
                extra = pltpu.roll(ref[there : there + sets, :], steps - EXTRA * p, 1)
                value = jnp.where(behind, extra, value)
            send_ref[pl.ds(KIND * kind + i, sets, stride=rows), :] = value
    for half in range(1, HALVES):
        send_ref[half * sets * rows : (half + 1) * sets * rows, :] = send_ref[0 : sets * rows, :]


def table_kernel(
    own,
    place_ref,
    cot_hbm,
    mixing_hbm,
    groups_hbm,
    gain_hbm,
    bias_hbm,
    out_bias_hbm,
    mode_in_hbm,
    mode_out_hbm,
    mode_re_hbm,
    mode_im_hbm,
    weights_hbm,
    endpoint_hbm,
    turn_hbm,
    scale_hbm,
    later_hbm,
    ahead_ref,
    lines_ref,
    own_ref,
    columns_ref,
    masked_ref,
    same_ref,
    cot_pad_ref,
    cot_send_ref,
    cot_ref,
    mixing_ref,
    groups_ref,
    gain_ref,
    bias_ref,
    out_bias_ref,
    mode_in_ref,
    mode_out_ref,
    mode_re_ref,
    mode_im_ref,
    weights_ref,
    endpoint_ref,
    turn_ref,
    scale_ref,
    later_ref,
    turned_ref,
    sems,
):
    ready = fetch(
        [
            (mode_in_hbm, mode_in_ref),
            (mode_out_hbm, mode_out_ref),
            (endpoint_hbm, endpoint_ref),
            (weights_hbm, weights_ref),
            (mode_re_hbm, mode_re_ref),
            (mode_im_hbm, mode_im_ref),
            (scale_hbm, scale_ref),
            (turn_hbm, turn_ref),
            (later_hbm, later_ref),
            (groups_hbm, groups_ref),
            (mixing_hbm, mixing_ref),
            (cot_hbm, cot_ref),
            (gain_hbm, gain_ref),
            (bias_hbm, bias_ref),
            (out_bias_hbm, out_bias_ref),
        ],
        sems,
    )
    channels, steps = cot_ref.shape[1:]
    width = ahead_ref.shape[0]
    per = width // LANES
    sets = channels // own
    count = 2 * MODES
    lines_ref[...] = jnp.zeros_like(lines_ref)
    turned_ref[...] = jnp.zeros_like(turned_ref)
    cot_pad_ref[...] = jnp.zeros_like(cot_pad_ref)
    same_ref[...] = jnp.zeros_like(same_ref)
    ready(0, 1, 2, 3)
    kernel = lax.dot_general(
        mode_in_ref[...],
        weights_ref[...],
        (((1,), (0,)), ((), ())),
        precision=lax.Precision.HIGHEST,
        preferred_element_type=f32,
    )
    lines_ref[0:RANK, :] = kernel
    mix = jnp.sum(mode_out_ref[...] * endpoint_ref[...], axis=1, keepdims=True)
    ready(4, 5, 6)
    scale = scale_ref[:, 0:count]
    gain_re, gain_im = mode_re_ref[...], mode_im_ref[...]
    signed = jnp.concatenate([gain_re, -gain_im], 1) * scale
    sign = jnp.where(lax.broadcasted_iota(jnp.int32, (RANK, count), 1) < MODES, 1.0, -1.0)
    lines_ref[8 : 8 + RANK, 0:count] = signed * mix
    lines_ref[16 : 16 + RANK, 0:count] = sign * scale * mix
    lines_ref[24 : 24 + RANK, 0:count] = signed
    turned_ref[0:RANK, 0:count] = jnp.concatenate([gain_re, gain_im], 1) * mix
    columns = turned_ref[...].T[0:count]
    response = None
    for r in range(RANK):
        term = columns[:, r : r + 1] * kernel[r : r + 1, :]
        response = term if response is None else response + term
    ready(7, 8)
    real, imag = response[:MODES], response[MODES:]
    cosine, sine = turn_ref[0:MODES], turn_ref[MODES : 2 * MODES]
    cos_b, sin_b = turn_ref[2 * MODES : 3 * MODES], turn_ref[3 * MODES : 4 * MODES]
    turned = jnp.concatenate([real * cos_b + imag * sin_b, imag * cos_b - real * sin_b], 0)
    rows = jnp.concatenate([turned[:, b * LANES : (b + 1) * LANES] for b in range(per)], 0)
    local, total = scan_lanes_exactly(rows, later_ref[...])
    run = jnp.zeros((count, LANES), f32)
    suffix = [None] * per
    for b in reversed(range(per)):
        suffix[b] = local[b * count : (b + 1) * count] + run
        run = run + total[b * count : (b + 1) * count]
    for b in range(per):
        at = slice(b * LANES, (b + 1) * LANES)
        c, s = cosine[:, at], sine[:, at]
        parts = []
        for value in (suffix[b], run - suffix[b]):
            re, im = value[:MODES], value[MODES:]
            parts += [re * c + im * s, im * c - re * s]
        high, low = split(jnp.concatenate(parts, 0).T)
        ahead_ref[at, 0:LANES] = high
        ahead_ref[at, LANES : 2 * LANES] = low
    ready(9, 10, 11, 12, 13, 14)
    chunk = channels if channels <= 512 else 256
    for start in range(0, channels, chunk):
        at = slice(start, start + chunk)
        same = same_rows(groups_ref, start, chunk)
        high, low = split(jnp.where(same, mixing_ref[at, :], 0.0))
        masked_ref[0, at, :] = high
        masked_ref[1, at, :] = low
        same_ref[at, 0:channels] = jnp.where(same, 1.0, 0.0)
        row = lax.broadcasted_iota(jnp.int32, (chunk, channels), 0) + start
        lane = lax.broadcasted_iota(jnp.int32, (chunk, channels), 1)
        for k, ref in enumerate((gain_ref, bias_ref, out_bias_ref)):
            columns_ref[at, k : k + 1] = jnp.sum(
                jnp.where(row == lane, ref[...], 0.0), axis=1, keepdims=True
            )
    unused, unused, unused, place = places(place_ref, sets * HALVES)
    mine = own_lanes(place, channels, own, sets)
    gain = jnp.sum(jnp.where(mine, gain_ref[...], 0.0), axis=1, keepdims=True)
    gain = jnp.where(lax.broadcasted_iota(jnp.int32, (SLOT, 1), 0) < own, gain, 1.0)
    bias = jnp.sum(jnp.where(mine, bias_ref[...], 0.0), axis=1, keepdims=True)
    own_ref[0:SLOT, :] = jnp.broadcast_to(gain, (SLOT, LANES))
    own_ref[SLOT : 2 * SLOT, :] = jnp.broadcast_to(bias, (SLOT, LANES))
    own_ref[2 * SLOT : 3 * SLOT, :] = jnp.broadcast_to(1.0 / gain, (SLOT, LANES))
    own_ref[3 * SLOT :, :] = jnp.broadcast_to(scale_ref[...], (8, LANES))
    cot_pad_ref[:, :steps] = cot_ref[0]
    most = cot_send_ref.shape[0]
    lane = lax.broadcasted_iota(jnp.int32, (channels - most, LANES), 1)
    behind = (lane >= steps) & (lane < steps + EXTRA)
    cot_send_ref[...] = cot_pad_ref[0:most, :]
    for p in range(3):
        at = pl.ds(p, channels - most, stride=3)
        moved = pltpu.roll(cot_pad_ref[most:, :], steps - EXTRA * p, 1)
        cot_send_ref[at, :] = jnp.where(behind, moved, cot_send_ref[at, :])


def normalized(x, blocks, steps, earlier):
    rows = x.shape[0]
    local, total = scan_lanes(jnp.concatenate([x, x * x], 0), earlier)
    first, second = blocks_of(local[:rows]), blocks_of(local[rows:])
    first_all, second_all = blocks_of(total[:rows]), blocks_of(total[rows:])
    run_one = jnp.zeros((SLOT, LANES), f32)
    run_two = jnp.zeros((SLOT, LANES), f32)
    lane = lax.broadcasted_iota(jnp.int32, (SLOT, LANES), 1)
    found = []
    for k in range(blocks):
        inverse = 1.0 / (lane + (k * steps + 1 + WINDOW)).astype(f32)
        mean = (first[k] + run_one) * inverse
        variance = (second[k] + run_two + WINDOW) * inverse - mean * mean + EPSILON
        found.append((mean, variance, run_one, run_two))
        run_one = run_one + first_all[k]
        run_two = run_two + second_all[k]
    return found


def owned(recv_ref, tail_ref, own, blocks, steps):
    lane = lax.broadcasted_iota(jnp.int32, (blocks, LANES), 1)
    tail_ref[...] = jnp.zeros_like(tail_ref)
    for kind in range(2):
        for i in range(KIND, own):
            tail_ref[pl.ds(8 * kind + i - KIND, blocks, stride=16), :] = jnp.where(
                lane < steps, unpacked(recv_ref, i, kind, blocks, steps), 0.0
            )
    got = recv_ref[...].reshape(blocks, 2 * KIND, LANES)
    got = jnp.where(lax.broadcasted_iota(jnp.int32, got.shape, 2) < steps, got, 0.0)
    tail = tail_ref[...].reshape(blocks, 16, LANES)
    x = jnp.concatenate([got[:, 0:KIND], tail[:, 0:8]], 1)
    grad = jnp.concatenate([got[:, KIND : 2 * KIND], tail[:, 8:16]], 1)
    order = first_order(blocks)
    slots = [order.index(b) for b in range(blocks)]
    return [x[k] for k in slots], [grad[k] for k in slots]


def forward_kernel(
    own,
    blocks,
    steps,
    place_ref,
    recv_ref,
    own_ref,
    ahead_ref,
    from_modes_ref,
    to_modes_ref,
    earlier_ref,
    send_ref,
    mean_ref,
    inverse_ref,
    centered_ref,
    shifted_ref,
    grad_ref,
    normal_grad_ref,
    waves_ref,
    tail_ref,
    back_tail_ref,
):
    windows = blocks * steps // WINDOW
    x, grad = owned(recv_ref, tail_ref, own, blocks, steps)
    found = normalized(jnp.concatenate(x, 0), blocks, steps, earlier_ref[...])
    gain, bias, over = own_ref[0:SLOT], own_ref[SLOT : 2 * SLOT], own_ref[2 * SLOT : 3 * SLOT]
    row = lax.broadcasted_iota(jnp.int32, (SLOT, LANES), 0)
    lane = lax.broadcasted_iota(jnp.int32, (SLOT, LANES), 1)
    held = (row < own) & (lane < steps)
    normal, spreads, recon_grad = [], [], []
    for k in range(blocks):
        at = slice(k * SLOT, (k + 1) * SLOT)
        mean, variance = found[k][:2]
        inverse = lax.rsqrt(variance)
        spread = variance * inverse
        centered = (x[k] - mean) * inverse
        normal.append(gain * centered + bias)
        spreads.append(spread)
        recon_grad.append(jnp.where(held, grad[k] * spread * over, 0.0))
        mean_ref[at, :] = mean
        inverse_ref[at, :] = inverse
        centered_ref[at, :] = centered
        grad_ref[at, :] = grad[k]
    spectra = stacked_dot(to_wide(normal, windows), ahead_ref[...])
    waves = stacked_dot(to_wide(recon_grad, windows), to_modes_ref[...])
    count = 2 * MODES
    current, before = spectra[:, :count], spectra[:, count:]
    zero = jnp.zeros((SLOT, count), f32)
    after = zero
    if windows > 1:
        current = current + jnp.concatenate([zero, before[:-SLOT]], 0)
        after = jnp.concatenate([waves[SLOT:], zero], 0)
    recon = stacked_dot(current, from_modes_ref[...])
    waves = jnp.concatenate([waves, after], 1)
    waves_ref[...] = waves
    recon = to_blocks(recon, windows)
    normal_grad = to_blocks(convolved_back(waves * own_ref[3 * SLOT : 3 * SLOT + 1], ahead_ref[...]), windows)
    backs = []
    for b in range(blocks):
        at = slice(b * SLOT, (b + 1) * SLOT)
        shifted = (recon[b] - bias) * over
        shifted_ref[at, :] = shifted
        normal_grad_ref[at, :] = normal_grad[b]
        backs.append(shifted * spreads[b] + found[b][0])
    unused, unused, half, unused = places(place_ref, blocks)
    first = half == 0
    sets = blocks // HALVES
    count = 3 * KIND
    one, two = lane == LANES - 2, lane == LANES - 1
    for k, b in enumerate(owner_orders(blocks)[0]):
        c = b + sets
        arrays = [
            jnp.where(first, backs[b], backs[c]),
            jnp.where(first, backs[c], backs[b]),
            jnp.where(first, normal_grad[b], normal_grad[c]),
        ]
        run_one = jnp.where(first, found[b][2], found[c][2])
        run_two = jnp.where(first, found[b][3], found[c][3])
        arrays[0] = jnp.where(one, run_one, jnp.where(two, run_two, arrays[0]))
        send_ref[k * count : k * count + KIND, :] = arrays[0][:KIND]
        tail = jnp.where(one[:8], run_one[KIND:], jnp.where(two[:8], run_two[KIND:], arrays[1][:8]))
        send_ref[k * count + KIND : k * count + KIND + 8, :] = tail
        send_ref[k * count + KIND + 8 : k * count + 2 * KIND, :] = arrays[1][8:KIND]
        send_ref[k * count + 2 * KIND : k * count + 3 * KIND, :] = arrays[2][:KIND]
        for kind in range(3):
            back_tail_ref[(3 * k + kind) * 8 : (3 * k + kind + 1) * 8, :] = arrays[kind][KIND:]
    for kind in range(3):
        for i in range(KIND, own):
            value = back_tail_ref[pl.ds(8 * kind + i - KIND, sets, stride=24), :]
            pack_extra(send_ref, value, i, kind, count, steps)


def backward_kernel(
    own,
    blocks,
    steps,
    wide,
    place_ref,
    recv_ref,
    own_ref,
    mean_ref,
    inverse_ref,
    centered_ref,
    shifted_ref,
    grad_ref,
    normal_grad_ref,
    waves_ref,
    lines_ref,
    turn_hbm,
    weights_t_hbm,
    earlier_hbm,
    misc_ref,
    starts_ref,
    turn_ref,
    weights_t_ref,
    earlier_ref,
    sems,
):
    ready = fetch(
        [(turn_hbm, turn_ref), (earlier_hbm, earlier_ref), (weights_t_hbm, weights_t_ref)], sems
    )
    windows = blocks * steps // WINDOW
    count = 2 * MODES
    mean, inverse, centered, shifted, grad, normal_grad = (
        blocks_of(ref[...])
        for ref in (
            mean_ref,
            inverse_ref,
            centered_ref,
            shifted_ref,
            grad_ref,
            normal_grad_ref,
        )
    )
    gain, bias, over = own_ref[0:SLOT], own_ref[SLOT : 2 * SLOT], own_ref[2 * SLOT : 3 * SLOT]
    row = lax.broadcasted_iota(jnp.int32, (SLOT, LANES), 0)
    lane = lax.broadcasted_iota(jnp.int32, (SLOT, LANES), 1)
    held = (row < own) & (lane < steps)
    waves = waves_ref[...]
    gain_sum = jnp.zeros((SLOT, LANES), f32)
    bias_sum = jnp.zeros((SLOT, LANES), f32)
    normal, ones, twos = [], [], []
    for k in range(blocks):
        over_q = 1.0 / (lane + (k * steps + 1 + WINDOW)).astype(f32)
        normal.append(jnp.where(held, gain * centered[k] + bias, 0.0))
        recon_grad = grad[k] / inverse[k] * over
        gain_sum = gain_sum + normal_grad[k] * centered[k] - recon_grad * shifted[k]
        bias_sum = bias_sum + normal_grad[k] - recon_grad
        first, second = statistics(
            grad[k],
            shifted[k],
            normal_grad[k] * gain * inverse[k],
            centered[k],
            mean[k],
            inverse[k],
            over_q,
        )
        ones.append(jnp.where(held, first, 0.0))
        twos.append(jnp.where(held, second, 0.0))
    gain_sum, bias_sum = jnp.where(held, gain_sum, 0.0), jnp.where(held, bias_sum, 0.0)
    ready(1)
    high, low = split(jnp.concatenate(ones + twos, 0))
    total = blocks_of(dot(jnp.concatenate([high, low], 1), earlier_ref[:, LANES:]))
    run_one = jnp.zeros((SLOT, LANES), f32)
    run_two = jnp.zeros((SLOT, LANES), f32)
    unused, unused, half, place = places(place_ref, blocks)
    first = half == 0
    sets = blocks // HALVES
    starts = [None] * blocks
    for k in reversed(range(blocks)):
        both = jnp.where(lane == row, run_one, jnp.where(lane == row + 32, run_two, 0.0))
        starts[k] = jnp.sum(both, 0, keepdims=True)
        run_one = run_one + total[k]
        run_two = run_two + total[blocks + k]
    for at, device in enumerate(share_order(blocks * CORES)):
        k = device // CORES
        starts_ref[at : at + 1, :] = jnp.where(first, starts[k], starts[k + sets])
    signal = to_wide(normal, windows)
    high, low = split(signal)
    w_high, w_low = split(waves.T)
    pairs = dot(
        jnp.concatenate([w_high, w_high, w_low], 1), jnp.concatenate([high, low, high], 0)
    )
    ready(0)
    cosine, sine = turn_ref[0:MODES], turn_ref[MODES : 2 * MODES]
    cos_b, sin_b = turn_ref[2 * MODES : 3 * MODES], turn_ref[3 * MODES : 4 * MODES]

    def turned(value):
        re, im = value[:MODES], value[MODES:]
        return jnp.concatenate([re * cosine - im * sine, -(re * sine + im * cosine)], 0)

    per = pairs.shape[1] // LANES
    after = turned(pairs[count:])
    left = turned(pairs[:count]) - after
    after = sum(after[:, b * LANES : (b + 1) * LANES] for b in range(per))
    local, total = scan_lanes(
        jnp.concatenate([left[:, b * LANES : (b + 1) * LANES] for b in range(per)], 0),
        earlier_ref[...],
    )
    run = jnp.broadcast_to(jnp.sum(after, 1, keepdims=True), (count, LANES))
    sums = []
    for b in range(per):
        sums.append(local[b * count : (b + 1) * count] + run)
        run = run + total[b * count : (b + 1) * count]
    sums = jnp.concatenate(sums, 1)
    re, im = sums[:MODES], sums[MODES:]
    crossed = jnp.concatenate([re * cos_b + im * sin_b, im * cos_b - re * sin_b], 0)
    high, low = split(crossed)
    s_high, s_low = split(lines_ref[8:16, 0:count])
    kernel_grad = dot(
        jnp.concatenate([s_high, s_high, s_low], 1), jnp.concatenate([high, low, high], 0)
    )
    k_high, k_low = split(lines_ref[0:8, :])
    overlap = dot_nt(
        jnp.concatenate([k_high, k_high, k_low], 1), jnp.concatenate([high, low, high], 1)
    )
    modes = overlap * lines_ref[16:24, 0:count]
    mix_grad = jnp.sum(overlap * lines_ref[24:32, 0:count], axis=1, keepdims=True)
    ready(2)
    mode_in_grad = stacked_dot(kernel_grad, weights_t_ref[...])
    misc_ref[...] = jnp.zeros_like(misc_ref)
    misc_ref[0:RANK, :] = mode_in_grad[0:RANK, :LANES]
    misc_ref[RANK : 2 * RANK, :] = mode_in_grad[0:RANK, LANES:]
    misc_ref[8 : 8 + RANK, 0:count] = modes[0:RANK]
    misc_ref[8 : 8 + RANK, count : 2 * count] = jnp.broadcast_to(mix_grad, (8, count))[0:RANK]
    mine = own_lanes(place, wide, own, sets)
    at = 12
    gain_row = jnp.sum(
        jnp.where(mine, jnp.sum(gain_sum, 1, keepdims=True), 0.0), axis=0, keepdims=True
    )
    bias_row = jnp.sum(
        jnp.where(mine, jnp.sum(bias_sum, 1, keepdims=True), 0.0), axis=0, keepdims=True
    )
    cot_sum = jnp.sum(recv_ref[...].reshape(blocks, 2 * KIND, LANES), axis=0)[:SLOT]
    cot_row = jnp.sum(
        jnp.where(mine, cot_sum[:, LANES - 2 : LANES - 1], 0.0), axis=0, keepdims=True
    )
    for value in (gain_row, bias_row, cot_row):
        for j in range(wide // LANES):
            misc_ref[at : at + 1, :] = value[:, j * LANES : (j + 1) * LANES]
            at += 1


def convolved_back(waves, ahead):
    rows = waves.shape[0]
    high, low = split(waves)
    out = dot_nt(jnp.concatenate([high, low], 0), ahead[:, :LANES])
    return out[:rows] + out[rows:] + dot_nt(high, ahead[:, LANES:])


def statistics(grad, shifted, scaled, centered, mean, inverse, over_q):
    variance_grad = (grad * shifted - scaled * centered) * (0.5 * inverse)
    first = (grad - scaled - 2.0 * mean * variance_grad) * over_q
    return first, variance_grad * over_q


def pieces(channels, devices):
    tiles, rest = channels // LANES, channels % LANES
    each = channels // devices
    rest_rows = channels * rest // LANES
    misc_rows = 12 + 3 * (up(channels, LANES) // LANES)
    extra = up(rest_rows + misc_rows, devices) // devices
    return tiles, rest, each, rest_rows, misc_rows, extra


def gathered(recv_ref, kind, own, steps, dense_ref):
    sets = recv_ref.shape[0] // (3 * KIND)
    for i in range(own):
        dense_ref[sets * i : sets * (i + 1), :] = unpacked(recv_ref, i, kind, sets, steps)


def mix_kernel(
    own,
    devices,
    steps,
    recv_ref,
    same_ref,
    cot_ref,
    cot_partner_ref,
    misc_ref,
    starts_ref,
    send_ref,
    dense_ref,
    partner_ref,
    cot_all_ref,
    misc_all_ref,
):
    channels = same_ref.shape[0]
    tiles, rest, each, rest_rows, misc_rows, extra = pieces(channels, devices)
    slot = send_ref.shape[0] // devices
    most = cot_partner_ref.shape[0]
    cot = cot_partner_ref[...]
    cot_all_ref[0:most, :] = jnp.where(
        lax.broadcasted_iota(jnp.int32, cot.shape, 1) < steps, cot, 0.0
    )
    lane = lax.broadcasted_iota(jnp.int32, (channels - most, LANES), 1)
    cot = jnp.zeros((channels - most, LANES), f32)
    for p in reversed(range(3)):
        row = cot_partner_ref[pl.ds(p, channels - most, stride=3), :]
        row = pltpu.roll(row, LANES - steps + EXTRA * p, 1)
        cot = jnp.where(lane < min(EXTRA * (p + 1), steps), row, cot)
    cot_all_ref[most:, :] = cot
    three = []
    for kind, ref in enumerate((dense_ref, partner_ref)):
        if ref.shape[0] > channels:
            ref[channels:, :] = jnp.zeros((ref.shape[0] - channels, LANES), f32)
        gathered(recv_ref, kind, own, steps, ref)
        high, low = split(ref[...])
        three += [high, low, high]
    three = jnp.concatenate(three, 1)
    chunk = channels if channels <= 512 else devices
    for start in range(0, channels, chunk):
        at = slice(start, start + chunk)
        six = []
        for ref in (cot_ref, cot_all_ref):
            high, low = split(ref[at, :])
            six += [high, high, low]
        grad = dot_nt(jnp.concatenate(six, 1), three)
        for j in range(tiles):
            lanes = slice(j * LANES, (j + 1) * LANES)
            tile = grad[:, lanes] * same_ref[at, lanes]
            for i in range(chunk // devices):
                send_ref[pl.ds(j * each + start // devices + i, devices, stride=slot), :] = tile[
                    devices * i : devices * (i + 1)
                ]
        if rest:
            lanes = slice(tiles * LANES, tiles * LANES + LANES)
            last = grad[:, lanes] * same_ref[at, lanes]
            folded = last[0:rest_rows]
            for g in range(1, LANES // rest):
                folded = folded + pltpu.roll(
                    last[g * rest_rows : (g + 1) * rest_rows], g * rest, 1
                )
            misc_all_ref[0:rest_rows, :] = folded
    end = rest_rows + misc_rows
    misc_all_ref[rest_rows:end, :] = misc_ref[0:misc_rows, :]
    if misc_all_ref.shape[0] > end:
        misc_all_ref[end:, :] = jnp.zeros((misc_all_ref.shape[0] - end, LANES), f32)
    for k in range(extra):
        send_ref[pl.ds(tiles * each + k, devices, stride=slot), :] = misc_all_ref[
            devices * k : devices * (k + 1), :
        ]
    for k in range(tiles * each + extra, slot - 1):
        send_ref[pl.ds(k, devices, stride=slot), :] = jnp.zeros((devices, LANES), f32)
    send_ref[pl.ds(slot - 1, devices, stride=slot), :] = starts_ref[...]


def steps_kernel(
    own,
    devices,
    place_ref,
    recv_ref,
    shares_ref,
    grad_ref,
    columns_ref,
    masked_ref,
    series_hbm,
    cot_hbm,
    earlier_hbm,
    later_hbm,
    out_ref,
    series_grad_ref,
    series_ref,
    cot_ref,
    earlier_ref,
    later_ref,
    dense_ref,
    back_ref,
    sums_ref,
    pad_ref,
    sems,
):
    ready = fetch(
        [
            (series_hbm, series_ref),
            (cot_hbm, cot_ref),
            (earlier_hbm, earlier_ref),
            (later_hbm, later_ref),
        ],
        sems,
    )
    channels, steps = series_ref.shape[1:]
    sets = channels // own
    block, core, unused, unused = places(place_ref, sets * HALVES)
    gathered(recv_ref, 0, own, steps, dense_ref)
    gathered(recv_ref, 2, own, steps, back_ref)
    for i in range(own):
        sums_ref[sets * i : sets * (i + 1), :] = recv_ref[pl.ds(i, sets, stride=3 * KIND), :]
    pad_ref[...] = jnp.zeros_like(pad_ref)
    gain, bias, shift = (columns_ref[:, k : k + 1] for k in range(3))
    restored = dense_ref[...]
    both = jnp.concatenate(split(restored), 1)
    ready(0)
    pad_ref[:, :steps] = series_ref[0]
    chunk = channels if channels <= 512 else 256
    for start in range(0, channels, chunk):
        at = slice(start, start + chunk)
        out = dot(jnp.concatenate([masked_ref[0, at, :], masked_ref[1, at, :]], 0), both)
        mixed = out[:chunk, :LANES] + out[:chunk, LANES:] + out[chunk:, :LANES]
        out_ref[0, at, :] = (pad_ref[at, :] + mixed + shift[at])[:, :steps]
    x = pad_ref[...]
    ready(2)
    local, unused = scan_lanes(jnp.concatenate([x, x * x], 0), earlier_ref[...])
    lane = lax.broadcasted_iota(jnp.int32, (channels, LANES), 1)
    over_q = 1.0 / (lane + (block * steps + 1 + WINDOW)).astype(f32)
    mean = (local[:channels] + sums_ref[:, LANES - 2 : LANES - 1]) * over_q
    variance = (local[channels:] + sums_ref[:, LANES - 1 : LANES] + WINDOW) * over_q
    inverse = lax.rsqrt(variance - mean * mean + EPSILON)
    centered = (x - mean) * inverse
    scaled = back_ref[...] * gain * inverse
    first, second = statistics(
        grad_ref[...], (restored - mean) * inverse, scaled, centered, mean, inverse, over_q
    )
    held = lane < steps
    ready(3)
    local, unused = scan_lanes(
        jnp.concatenate([jnp.where(held, first, 0.0), jnp.where(held, second, 0.0)], 0),
        later_ref[...],
    )
    slot = shares_ref.shape[0] // devices
    rows = []
    order = share_order(devices * HALVES)
    for owner in owner_orders(sets * HALVES)[0]:
        even, odd = (order.index(owner * CORES + r) * slot + slot - 1 for r in range(CORES))
        rows.append(
            jnp.where(core == 0, shares_ref[even : even + 1, :], shares_ref[odd : odd + 1, :])
        )
    later = jnp.concatenate(rows, 0)
    part = scaled + local[:channels] + 2.0 * x * local[channels:]
    ready(1)
    for i in range(own):
        at = slice(sets * i, sets * (i + 1))
        sums = later[:, i : i + 1] + 2.0 * x[at] * later[:, 32 + i : 33 + i]
        series_grad_ref[0, at, :] = cot_ref[0, at, :] + (part[at] + sums)[:, :steps]


def sum_kernel(devices, recv_ref, send_ref):
    slot = recv_ref.shape[0] // devices
    total = recv_ref[0:slot, :]
    for s in range(1, devices):
        total = total + recv_ref[s * slot : (s + 1) * slot, :]
    for s in range(devices):
        send_ref[s * slot : (s + 1) * slot, :] = total


def spread_kernel(
    devices,
    recv_ref,
    endpoint_ref,
    gain_ref,
    bias_ref,
    mode_in_ref,
    mode_out_ref,
    mode_re_ref,
    mode_im_ref,
    mixing_ref,
    out_bias_ref,
    misc_ref,
):
    channels = mixing_ref.shape[0]
    tiles, rest, each, rest_rows, misc_rows, extra = pieces(channels, devices)
    slot = recv_ref.shape[0] // devices
    for j in range(tiles):
        for i in range(each):
            mixing_ref[devices * i : devices * (i + 1), j * LANES : (j + 1) * LANES] = recv_ref[
                pl.ds(j * each + i, devices, stride=slot), :
            ]
    for k in range(extra):
        misc_ref[devices * k : devices * (k + 1), :] = recv_ref[
            pl.ds(tiles * each + k, devices, stride=slot), :
        ]
    if rest:
        folded = misc_ref[0:rest_rows, :]
        for g in range(LANES // rest):
            piece = folded if g == 0 else pltpu.roll(folded, LANES - g * rest, 1)
            mixing_ref[g * rest_rows : (g + 1) * rest_rows, tiles * LANES :] = piece[:, :rest]
    at = rest_rows
    mode_in_ref[:, 0:LANES] = misc_ref[at : at + RANK, :]
    mode_in_ref[:, LANES : 2 * LANES] = misc_ref[at + RANK : at + 2 * RANK, :]
    modes = misc_ref[at + 8 : at + 8 + RANK, :]
    mode_re_ref[...] = modes[:, 0:MODES]
    mode_im_ref[...] = modes[:, MODES : 2 * MODES]
    mode_out_ref[...] = modes[:, 2 * MODES : 2 * MODES + 1] * endpoint_ref[...]
    at += 12
    for ref in (gain_ref, bias_ref, out_bias_ref):
        for start in range(0, channels, LANES):
            size = min(LANES, channels - start)
            ref[:, start : start + size] = misc_ref[at : at + 1, 0:size]
            at += 1


def call(kernel, outs, smem=(), vmem=(), hbm=(), scratch=(), cost=None, limit=None):
    in_vmem = pl.BlockSpec(memory_space=pltpu.VMEM)
    in_smem = pl.BlockSpec(memory_space=pltpu.SMEM)
    in_hbm = pl.BlockSpec(memory_space=pltpu.HBM)
    held = [pltpu.VMEM(a.shape, a.dtype) for a in hbm] + list(scratch)
    if hbm:
        held.append(pltpu.SemaphoreType.DMA((len(hbm),)))
    hbm = [pltpu.with_memory_space_constraint(a, pltpu.HBM) for a in hbm]
    return pl.pallas_call(
        kernel,
        out_shape=tuple(jax.ShapeDtypeStruct(shape, kind) for shape, kind in outs),
        in_specs=[in_smem] * len(smem) + [in_vmem] * len(vmem) + [in_hbm] * len(hbm),
        out_specs=tuple(in_vmem for unused in outs),
        scratch_shapes=held,
        compiler_params=pltpu.CompilerParams(vmem_limit_bytes=limit),
        cost_estimate=cost,
    )(*smem, *vmem, *hbm)


def exchange(value, axis, orders):
    count = len(orders[0])
    out = lax.all_to_all(
        value.reshape(count, value.shape[0] // count, value.shape[1]),
        axis,
        split_axis=0,
        concat_axis=0,
        axis_index_groups=orders,
    )
    return out.reshape(value.shape)


def body(
    series,
    group_ids,
    rev_gain,
    rev_bias,
    mode_in,
    mode_out,
    mode_re,
    mode_im,
    mixing,
    out_bias,
    cotangent,
):
    samples, channels, steps = series.shape
    blocks = lax.axis_size("seq")
    sets = blocks // HALVES
    devices = blocks * lax.axis_size("rep")
    sharing = devices // HALVES
    own = channels // sets
    width = WINDOW // steps * LANES
    padded = up(channels, LANES)
    place = lax.axis_index(("seq", "rep")).astype(jnp.int32).reshape(1)
    halves_of = owner_orders(blocks)
    all_of = [first_order(blocks)]
    shares_of = [[h * sharing + k for k in share_order(devices)] for h in range(HALVES)]
    const = {name: jnp.asarray(value) for name, value in constants(steps).items()}
    groups = group_ids.reshape(1, channels)
    limit = (16 if channels <= 512 else 56) * 2**20
    run = functools.partial(call, limit=limit)
    busy = pl.CostEstimate(flops=4_000_000_000, bytes_accessed=8_000_000, transcendentals=0)
    brief = pl.CostEstimate(flops=100_000_000, bytes_accessed=1_000_000, transcendentals=0)

    send, restored_grad = run(
        functools.partial(send_kernel, own),
        [((blocks * 2 * KIND, LANES), f32), ((channels, LANES), f32)],
        hbm=(series, cotangent, mixing, groups),
        scratch=[pltpu.VMEM((channels, LANES), f32)],
        cost=brief,
    )
    ahead, lines, mine, columns, masked, same, cot, cot_send = run(
        functools.partial(table_kernel, own),
        [
            ((width, 2 * LANES), bf16),
            ((32, width), f32),
            ((3 * SLOT + 8, LANES), f32),
            ((channels, LANES), f32),
            ((2, channels, channels), bf16),
            ((channels, padded), f32),
            ((channels, LANES), f32),
            ((channels * 3 // 4, LANES), f32),
        ],
        smem=(place,),
        hbm=(
            cotangent,
            mixing,
            groups,
            rev_gain.reshape(1, channels),
            rev_bias.reshape(1, channels),
            out_bias.reshape(1, channels),
            mode_in.T,
            mode_out.T,
            mode_re,
            mode_im,
            const["weights"],
            const["endpoint"],
            const["turn"],
            const["scale"],
            const["later"],
        ),
        scratch=[pltpu.VMEM((LANES, LANES), f32)],
        cost=busy,
    )
    owned_rows = exchange(send, "seq", all_of)
    rows = blocks * SLOT
    windows = blocks * steps // WINDOW
    send, *kept = run(
        functools.partial(forward_kernel, own, blocks, steps),
        [((sets * 3 * KIND, LANES), f32)]
        + [((rows, LANES), f32)] * 6
        + [((windows * SLOT, LANES), f32)],
        smem=(place,),
        vmem=(
            owned_rows,
            mine,
            ahead,
            const["from_modes"],
            const["to_modes"],
            const["earlier"],
        ),
        scratch=[pltpu.VMEM((blocks * 16, LANES), f32), pltpu.VMEM((sets * 24, LANES), f32)],
        cost=brief,
    )
    there = exchange(send, "seq", halves_of)
    cot_send, kept[0] = lax.optimization_barrier((cot_send, kept[0]))
    cot_partner = lax.ppermute(cot_send, "seq", [(k, (k + sets) % blocks) for k in range(blocks)])
    tiles, rest, each, rest_rows, misc_rows, extra = pieces(channels, sharing)
    slot = up(tiles * each + extra + 1, 8)
    misc, starts = run(
        functools.partial(backward_kernel, own, blocks, steps, padded),
        [
            ((up(misc_rows, 8), LANES), f32),
            ((sharing, LANES), f32),
        ],
        smem=(place,),
        vmem=(owned_rows, mine, *kept, lines),
        hbm=(const["turn"], const["weights_t"], const["earlier"]),
        cost=busy,
    )
    (send,) = run(
        functools.partial(mix_kernel, own, sharing, steps),
        [((sharing * slot, LANES), f32)],
        vmem=(there, same, cot, cot_partner, misc, starts),
        scratch=[
            pltpu.VMEM((padded, LANES), f32),
            pltpu.VMEM((padded, LANES), f32),
            pltpu.VMEM((channels, LANES), f32),
            pltpu.VMEM((up(extra * sharing, 8), LANES), f32),
        ],
        cost=brief,
    )
    shares = exchange(send, ("seq", "rep"), shares_of)
    (send,) = run(
        functools.partial(sum_kernel, sharing),
        [((sharing * slot, LANES), f32)],
        vmem=(shares,),
        cost=brief,
    )
    sums = exchange(send, ("seq", "rep"), shares_of)
    layer_out, series_grad = run(
        functools.partial(steps_kernel, own, sharing),
        [((1, channels, steps), f32), ((1, channels, steps), f32)],
        smem=(place,),
        vmem=(there, shares, restored_grad, columns, masked),
        hbm=(series, cotangent, const["earlier"], const["later"]),
        scratch=[pltpu.VMEM((channels, LANES), f32)] * 4,
        cost=busy,
    )
    outs = run(
        functools.partial(spread_kernel, sharing),
        [
            ((1, channels), f32),
            ((1, channels), f32),
            ((RANK, ORDER), f32),
            ((RANK, ORDER), f32),
            ((RANK, MODES), f32),
            ((RANK, MODES), f32),
            ((channels, channels), f32),
            ((1, channels), f32),
        ],
        vmem=(sums, const["endpoint"]),
        scratch=[pltpu.VMEM((up(extra * sharing, 8), LANES), f32)],
        cost=brief,
    )
    return (
        layer_out,
        series_grad,
        outs[0].reshape(channels),
        outs[1].reshape(channels),
        outs[2].T,
        outs[3].T,
        outs[4],
        outs[5],
        outs[6],
        outs[7].reshape(channels),
    )


def solution(mesh):
    time_split = P("rep", None, "seq")
    in_specs = (time_split,) + (P(),) * 9 + (time_split,)
    out_specs = (time_split, time_split) + (P(),) * 8
    return jax.shard_map(body, mesh=mesh, in_specs=in_specs, out_specs=out_specs, check_vma=False)
```

```python
import functools
import math

import jax
import jax.numpy as jnp
import ml_dtypes
import numpy as np
from jax import lax
from jax.experimental import pallas as pl
from jax.experimental.pallas import tpu as pltpu
from jax.sharding import PartitionSpec as P

ORDER = 256
MODES = 32
RANK = 4
WINDOW = 720
EPSILON = 1e-05

LANES = 128
CORES = 2
HALVES = 2
SLOT = 24
KIND = 16
EXTRA = 36
f32 = jnp.float32
bf16 = jnp.bfloat16


def up(value, multiple):
    return -(-value // multiple) * multiple


def legendre_table():
    one, two = np.float32(1.0), np.float32(2.0)
    lags = np.arange(WINDOW).astype(np.float32)
    points = one - (two * (lags + np.float32(0.5))) * np.float32(1.0 / WINDOW)
    lower, this = np.zeros_like(points), np.ones_like(points)
    rows = []
    for degree in np.arange(ORDER).astype(np.float32):
        rows.append(this)
        upper = ((two * degree + one) * points * this - degree * lower) / (degree + one)
        lower, this = this, upper
    return np.stack(rows)


def in_blocks(values, steps):
    blocks = WINDOW // steps
    framed = np.zeros(values.shape[:-1] + (blocks, LANES))
    framed[..., :steps] = values.reshape(values.shape[:-1] + (blocks, steps))
    return framed.reshape(values.shape[:-1] + (blocks * LANES,))


def halves(values):
    high = values.astype(np.float32).astype(ml_dtypes.bfloat16)
    low = (values - high.astype(np.float64)).astype(ml_dtypes.bfloat16)
    return high, low


def constants(steps):
    legendre = legendre_table()
    degree = np.arange(ORDER).astype(np.float32)
    weights = legendre * ((np.float32(2.0) * degree + np.float32(1.0)) / np.float32(WINDOW))[:, None]
    flipped = in_blocks(weights[:, ::-1], steps)
    high, low = halves(flipped)
    table = {}
    table["weights"] = flipped.astype(np.float32)
    table["weights_t"] = np.concatenate([high.T, low.T], 1)
    table["endpoint"] = legendre[:, 0][None, :].astype(np.float32)
    mode = np.arange(MODES)[:, None]
    step = np.arange(WINDOW)[None, :]
    angle = 2.0 * math.pi / WINDOW * (mode * step % WINDOW)
    cosine, sine = np.cos(angle), np.sin(angle)
    back = 2.0 * math.pi / WINDOW * (mode * (WINDOW - 1 - step) % WINDOW)
    table["turn"] = np.concatenate(
        [in_blocks(v, steps) for v in (cosine, sine, np.cos(back), np.sin(back))]
    ).astype(np.float32)
    scale = np.where(np.arange(MODES) == 0, 1.0, 2.0) / WINDOW
    table["scale"] = np.tile(scale, 4)[None, :].astype(np.float32)
    high, low = halves(in_blocks(np.concatenate([cosine, -sine]), steps))
    table["to_modes"] = np.concatenate([high.T, low.T], 1)
    wave = in_blocks(np.concatenate([scale[:, None] * cosine, -scale[:, None] * sine]), steps)
    table["from_modes"] = np.concatenate(halves(wave), 1)
    lane = np.arange(LANES)
    upper = (lane[:, None] <= lane[None, :]).astype(np.float32)
    ones = np.ones((LANES, LANES), np.float32)
    for name, part in (("earlier", upper), ("later", upper.T)):
        both = np.concatenate([part, ones], 1)
        table[name] = np.concatenate([both, both]).astype(ml_dtypes.bfloat16)
    return table


def split(value):
    high = value.astype(bf16)
    return high, (value - high.astype(f32)).astype(bf16)


def dot(a, b):
    return lax.dot_general(a, b, (((1,), (0,)), ((), ())), preferred_element_type=f32)


def dot_nt(a, b):
    return lax.dot_general(a, b, (((1,), (1,)), ((), ())), preferred_element_type=f32)


def stacked_dot(value, table):
    rows, width = value.shape[0], table.shape[1] // 2
    high, low = split(value)
    out = dot(jnp.concatenate([high, low], 0), table)
    return out[:rows, :width] + out[:rows, width:] + out[rows:, :width]


def scan_lanes(value, table):
    high, low = split(value)
    out = dot(jnp.concatenate([high, low], 1), table)
    return out[:, :LANES], out[:, LANES:]


def scan_lanes_exactly(value, table):
    high, low = split(value)
    last = (value - high.astype(f32) - low.astype(f32)).astype(bf16)
    out = dot(jnp.concatenate([high, low], 1), table) + dot(last, table[:LANES])
    return out[:, :LANES], out[:, LANES:]


def unpacked(ref, i, kind, count, steps):
    rows = ref.shape[0] // count
    if i < KIND:
        return ref[pl.ds(KIND * kind + i, count, stride=rows), :]
    lane = lax.broadcasted_iota(jnp.int32, (count, LANES), 1)
    value = None
    for p in reversed(range(3)):
        row = ref[pl.ds(KIND * kind + 4 * (i - KIND) + p, count, stride=rows), :]
        row = pltpu.roll(row, LANES - steps + EXTRA * p, 1)
        value = row if value is None else jnp.where(lane < EXTRA * (p + 1), row, value)
    return value


def pack_extra(ref, value, i, kind, rows, steps):
    count = value.shape[0]
    lane = lax.broadcasted_iota(jnp.int32, (count, LANES), 1)
    behind = (lane >= steps) & (lane < steps + EXTRA)
    for p in range(3):
        at = pl.ds(KIND * kind + 4 * (i - KIND) + p, count, stride=rows)
        ref[at, :] = jnp.where(behind, pltpu.roll(value, steps - EXTRA * p, 1), ref[at, :])


def owner_order(half):
    return [k ^ 1 for k in range(half)]


def owner_orders(blocks):
    half = blocks // HALVES
    return [[h * half + k for k in owner_order(half)] for h in range(HALVES)]


def first_order(blocks):
    return sum(owner_orders(blocks)[::-1], [])


def share_order(devices):
    sharing = devices // HALVES
    if sharing == 16:
        return [15, 1, 12, 8, 14, 11, 7, 3, 4, 2, 5, 6, 0, 10, 9, 13]
    return [int(k) for k in np.random.default_rng(0).permutation(sharing)]


def places(place_ref, blocks):
    block, core = place_ref[0] // CORES, place_ref[0] % CORES
    half = blocks // HALVES
    place = jnp.int32(0)
    for k, member in enumerate(owner_order(half)):
        place = jnp.where(block % half == member, k, place)
    return block, core, block // half, place


def to_wide(blocks, windows):
    per = len(blocks) // windows
    return jnp.concatenate(
        [jnp.concatenate(blocks[w * per : (w + 1) * per], 1) for w in range(windows)], 0
    )


def to_blocks(wide, windows):
    per = wide.shape[1] // LANES
    return [
        wide[w * SLOT : (w + 1) * SLOT, b * LANES : (b + 1) * LANES]
        for w in range(windows)
        for b in range(per)
    ]


def fetch(pairs, sems):
    copies = [pltpu.make_async_copy(a, b, sems.at[k]) for k, (a, b) in enumerate(pairs)]
    for copy in copies:
        copy.start()

    def ready(*which):
        for k in which:
            copies[k].wait()

    return ready


def blocks_of(value):
    return [value[k * SLOT : (k + 1) * SLOT] for k in range(value.shape[0] // SLOT)]


def same_rows(groups_ref, start, rows):
    channels = groups_ref.shape[1]
    ids = groups_ref[...].astype(f32)
    row = lax.broadcasted_iota(jnp.int32, (rows, channels), 0) + start
    lane = lax.broadcasted_iota(jnp.int32, (rows, channels), 1)
    column = jnp.sum(jnp.where(row == lane, ids, 0.0), axis=1, keepdims=True)
    return column == ids


def own_lanes(place, width, count, blocks):
    row = lax.broadcasted_iota(jnp.int32, (SLOT, width), 0)
    lane = lax.broadcasted_iota(jnp.int32, (SLOT, width), 1)
    return (lane == row * blocks + place) & (row < count)


def send_kernel(
    own,
    series_hbm,
    cot_hbm,
    mixing_hbm,
    groups_hbm,
    send_ref,
    grad_ref,
    series_ref,
    cot_ref,
    mixing_ref,
    groups_ref,
    pad_ref,
    sems,
):
    channels, steps = cot_ref.shape[1:]
    sets = channels // own
    ready = fetch(
        [
            (groups_hbm, groups_ref),
            (mixing_hbm, mixing_ref),
            (cot_hbm, cot_ref),
            (series_hbm, series_ref),
        ],
        sems,
    )
    rows = 2 * KIND
    pad_ref[...] = jnp.zeros_like(pad_ref)
    ready(2)
    pad_ref[:, :steps] = cot_ref[0]
    ready(0, 1)
    chunk = channels if channels <= 512 else 256
    total = None
    for start in range(0, channels, chunk):
        same = same_rows(groups_ref, start, chunk)
        masked = jnp.where(same, mixing_ref[start : start + chunk, :], 0.0)
        high, low = split(masked.T)
        both = jnp.concatenate(split(pad_ref[start : start + chunk, :]), 1)
        out = dot(jnp.concatenate([high, low], 0), both)
        part = out[:channels, :LANES] + out[:channels, LANES:] + out[channels:, :LANES]
        total = part if total is None else total + part
    lane = lax.broadcasted_iota(jnp.int32, (channels, LANES), 1)
    spot = lane == LANES - 2
    behind = (lane[:sets] >= steps) & (lane[:sets] < steps + EXTRA)
    sums = jnp.sum(pad_ref[...], axis=1, keepdims=True)
    grad_ref[...] = total
    ready(3)
    pad_ref[:, :steps] = series_ref[0]
    pad_ref[...] = jnp.where(spot, sums, pad_ref[...])
    for kind, ref in enumerate((pad_ref, grad_ref)):
        for i in range(KIND):
            value = ref[sets * i : sets * (i + 1), :]
            if kind and i < own - KIND:
                there = sets * (KIND + i)
                value = jnp.where(spot[:sets], sums[there : there + sets], value)
            there, p = sets * (KIND + i // 4), i % 4
            if there < channels and p < 3:
                extra = pltpu.roll(ref[there : there + sets, :], steps - EXTRA * p, 1)
                value = jnp.where(behind, extra, value)
            send_ref[pl.ds(KIND * kind + i, sets, stride=rows), :] = value
    for half in range(1, HALVES):
        send_ref[half * sets * rows : (half + 1) * sets * rows, :] = send_ref[0 : sets * rows, :]


def table_kernel(
    own,
    place_ref,
    cot_hbm,
    mixing_hbm,
    groups_hbm,
    gain_hbm,
    bias_hbm,
    out_bias_hbm,
    mode_in_hbm,
    mode_out_hbm,
    mode_re_hbm,
    mode_im_hbm,
    weights_hbm,
    endpoint_hbm,
    turn_hbm,
    scale_hbm,
    later_hbm,
    ahead_ref,
    lines_ref,
    own_ref,
    columns_ref,
    masked_ref,
    same_ref,
    cot_pad_ref,
    cot_send_ref,
    cot_ref,
    mixing_ref,
    groups_ref,
    gain_ref,
    bias_ref,
    out_bias_ref,
    mode_in_ref,
    mode_out_ref,
    mode_re_ref,
    mode_im_ref,
    weights_ref,
    endpoint_ref,
    turn_ref,
    scale_ref,
    later_ref,
    turned_ref,
    sems,
):
    ready = fetch(
        [
            (mode_in_hbm, mode_in_ref),
            (mode_out_hbm, mode_out_ref),
            (endpoint_hbm, endpoint_ref),
            (weights_hbm, weights_ref),
            (mode_re_hbm, mode_re_ref),
            (mode_im_hbm, mode_im_ref),
            (scale_hbm, scale_ref),
            (turn_hbm, turn_ref),
            (later_hbm, later_ref),
            (groups_hbm, groups_ref),
            (mixing_hbm, mixing_ref),
            (cot_hbm, cot_ref),
            (gain_hbm, gain_ref),
            (bias_hbm, bias_ref),
            (out_bias_hbm, out_bias_ref),
        ],
        sems,
    )
    channels, steps = cot_ref.shape[1:]
    width = ahead_ref.shape[0]
    per = width // LANES
    sets = channels // own
    count = 2 * MODES
    lines_ref[...] = jnp.zeros_like(lines_ref)
    turned_ref[...] = jnp.zeros_like(turned_ref)
    cot_pad_ref[...] = jnp.zeros_like(cot_pad_ref)
    same_ref[...] = jnp.zeros_like(same_ref)
    ready(0, 1, 2, 3)
    kernel = lax.dot_general(
        mode_in_ref[...],
        weights_ref[...],
        (((1,), (0,)), ((), ())),
        precision=lax.Precision.HIGHEST,
        preferred_element_type=f32,
    )
    lines_ref[0:RANK, :] = kernel
    mix = jnp.sum(mode_out_ref[...] * endpoint_ref[...], axis=1, keepdims=True)
    ready(4, 5, 6)
    scale = scale_ref[:, 0:count]
    gain_re, gain_im = mode_re_ref[...], mode_im_ref[...]
    signed = jnp.concatenate([gain_re, -gain_im], 1) * scale
    sign = jnp.where(lax.broadcasted_iota(jnp.int32, (RANK, count), 1) < MODES, 1.0, -1.0)
    lines_ref[8 : 8 + RANK, 0:count] = signed * mix
    lines_ref[16 : 16 + RANK, 0:count] = sign * scale * mix
    lines_ref[24 : 24 + RANK, 0:count] = signed
    turned_ref[0:RANK, 0:count] = jnp.concatenate([gain_re, gain_im], 1) * mix
    columns = turned_ref[...].T[0:count]
    response = None
    for r in range(RANK):
        term = columns[:, r : r + 1] * kernel[r : r + 1, :]
        response = term if response is None else response + term
    ready(7, 8)
    real, imag = response[:MODES], response[MODES:]
    cosine, sine = turn_ref[0:MODES], turn_ref[MODES : 2 * MODES]
    cos_b, sin_b = turn_ref[2 * MODES : 3 * MODES], turn_ref[3 * MODES : 4 * MODES]
    turned = jnp.concatenate([real * cos_b + imag * sin_b, imag * cos_b - real * sin_b], 0)
    rows = jnp.concatenate([turned[:, b * LANES : (b + 1) * LANES] for b in range(per)], 0)
    local, total = scan_lanes_exactly(rows, later_ref[...])
    run = jnp.zeros((count, LANES), f32)
    suffix = [None] * per
    for b in reversed(range(per)):
        suffix[b] = local[b * count : (b + 1) * count] + run
        run = run + total[b * count : (b + 1) * count]
    for b in range(per):
        at = slice(b * LANES, (b + 1) * LANES)
        c, s = cosine[:, at], sine[:, at]
        parts = []
        for value in (suffix[b], run - suffix[b]):
            re, im = value[:MODES], value[MODES:]
            parts += [re * c + im * s, im * c - re * s]
        high, low = split(jnp.concatenate(parts, 0).T)
        ahead_ref[at, 0:LANES] = high
        ahead_ref[at, LANES : 2 * LANES] = low
    ready(9, 10, 11, 12, 13, 14)
    chunk = channels if channels <= 512 else 256
    for start in range(0, channels, chunk):
        at = slice(start, start + chunk)
        same = same_rows(groups_ref, start, chunk)
        high, low = split(jnp.where(same, mixing_ref[at, :], 0.0))
        masked_ref[0, at, :] = high
        masked_ref[1, at, :] = low
        same_ref[at, 0:channels] = jnp.where(same, 1.0, 0.0)
        row = lax.broadcasted_iota(jnp.int32, (chunk, channels), 0) + start
        lane = lax.broadcasted_iota(jnp.int32, (chunk, channels), 1)
        for k, ref in enumerate((gain_ref, bias_ref, out_bias_ref)):
            columns_ref[at, k : k + 1] = jnp.sum(
                jnp.where(row == lane, ref[...], 0.0), axis=1, keepdims=True
            )
    unused, unused, unused, place = places(place_ref, sets * HALVES)
    mine = own_lanes(place, channels, own, sets)
    gain = jnp.sum(jnp.where(mine, gain_ref[...], 0.0), axis=1, keepdims=True)
    gain = jnp.where(lax.broadcasted_iota(jnp.int32, (SLOT, 1), 0) < own, gain, 1.0)
    bias = jnp.sum(jnp.where(mine, bias_ref[...], 0.0), axis=1, keepdims=True)
    own_ref[0:SLOT, :] = jnp.broadcast_to(gain, (SLOT, LANES))
    own_ref[SLOT : 2 * SLOT, :] = jnp.broadcast_to(bias, (SLOT, LANES))
    own_ref[2 * SLOT : 3 * SLOT, :] = jnp.broadcast_to(1.0 / gain, (SLOT, LANES))
    own_ref[3 * SLOT :, :] = jnp.broadcast_to(scale_ref[...], (8, LANES))
    cot_pad_ref[:, :steps] = cot_ref[0]
    most = cot_send_ref.shape[0]
    lane = lax.broadcasted_iota(jnp.int32, (channels - most, LANES), 1)
    behind = (lane >= steps) & (lane < steps + EXTRA)
    cot_send_ref[...] = cot_pad_ref[0:most, :]
    for p in range(3):
        at = pl.ds(p, channels - most, stride=3)
        moved = pltpu.roll(cot_pad_ref[most:, :], steps - EXTRA * p, 1)
        cot_send_ref[at, :] = jnp.where(behind, moved, cot_send_ref[at, :])


def normalized(x, blocks, steps, earlier):
    rows = x.shape[0]
    local, total = scan_lanes(jnp.concatenate([x, x * x], 0), earlier)
    first, second = blocks_of(local[:rows]), blocks_of(local[rows:])
    first_all, second_all = blocks_of(total[:rows]), blocks_of(total[rows:])
    run_one = jnp.zeros((SLOT, LANES), f32)
    run_two = jnp.zeros((SLOT, LANES), f32)
    lane = lax.broadcasted_iota(jnp.int32, (SLOT, LANES), 1)
    found = []
    for k in range(blocks):
        inverse = 1.0 / (lane + (k * steps + 1 + WINDOW)).astype(f32)
        mean = (first[k] + run_one) * inverse
        variance = (second[k] + run_two + WINDOW) * inverse - mean * mean + EPSILON
        found.append((mean, variance, run_one, run_two))
        run_one = run_one + first_all[k]
        run_two = run_two + second_all[k]
    return found


def owned(recv_ref, tail_ref, own, blocks, steps):
    lane = lax.broadcasted_iota(jnp.int32, (blocks, LANES), 1)
    tail_ref[...] = jnp.zeros_like(tail_ref)
    for kind in range(2):
        for i in range(KIND, own):
            tail_ref[pl.ds(8 * kind + i - KIND, blocks, stride=16), :] = jnp.where(
                lane < steps, unpacked(recv_ref, i, kind, blocks, steps), 0.0
            )
    got = recv_ref[...].reshape(blocks, 2 * KIND, LANES)
    got = jnp.where(lax.broadcasted_iota(jnp.int32, got.shape, 2) < steps, got, 0.0)
    tail = tail_ref[...].reshape(blocks, 16, LANES)
    x = jnp.concatenate([got[:, 0:KIND], tail[:, 0:8]], 1)
    grad = jnp.concatenate([got[:, KIND : 2 * KIND], tail[:, 8:16]], 1)
    order = first_order(blocks)
    slots = [order.index(b) for b in range(blocks)]
    return [x[k] for k in slots], [grad[k] for k in slots]


def forward_kernel(
    own,
    blocks,
    steps,
    place_ref,
    recv_ref,
    own_ref,
    ahead_ref,
    from_modes_ref,
    to_modes_ref,
    earlier_ref,
    send_ref,
    mean_ref,
    inverse_ref,
    centered_ref,
    shifted_ref,
    grad_ref,
    normal_grad_ref,
    waves_ref,
    tail_ref,
    back_tail_ref,
):
    windows = blocks * steps // WINDOW
    x, grad = owned(recv_ref, tail_ref, own, blocks, steps)
    found = normalized(jnp.concatenate(x, 0), blocks, steps, earlier_ref[...])
    gain, bias, over = own_ref[0:SLOT], own_ref[SLOT : 2 * SLOT], own_ref[2 * SLOT : 3 * SLOT]
    row = lax.broadcasted_iota(jnp.int32, (SLOT, LANES), 0)
    lane = lax.broadcasted_iota(jnp.int32, (SLOT, LANES), 1)
    held = (row < own) & (lane < steps)
    normal, spreads, recon_grad = [], [], []
    for k in range(blocks):
        at = slice(k * SLOT, (k + 1) * SLOT)
        mean, variance = found[k][:2]
        inverse = lax.rsqrt(variance)
        spread = variance * inverse
        centered = (x[k] - mean) * inverse
        normal.append(gain * centered + bias)
        spreads.append(spread)
        recon_grad.append(jnp.where(held, grad[k] * spread * over, 0.0))
        mean_ref[at, :] = mean
        inverse_ref[at, :] = inverse
        centered_ref[at, :] = centered
        grad_ref[at, :] = grad[k]
    spectra = stacked_dot(to_wide(normal, windows), ahead_ref[...])
    waves = stacked_dot(to_wide(recon_grad, windows), to_modes_ref[...])
    count = 2 * MODES
    current, before = spectra[:, :count], spectra[:, count:]
    zero = jnp.zeros((SLOT, count), f32)
    after = zero
    if windows > 1:
        current = current + jnp.concatenate([zero, before[:-SLOT]], 0)
        after = jnp.concatenate([waves[SLOT:], zero], 0)
    recon = stacked_dot(current, from_modes_ref[...])
    waves = jnp.concatenate([waves, after], 1)
    waves_ref[...] = waves
    recon = to_blocks(recon, windows)
    normal_grad = to_blocks(convolved_back(waves * own_ref[3 * SLOT : 3 * SLOT + 1], ahead_ref[...]), windows)
    backs = []
    for b in range(blocks):
        at = slice(b * SLOT, (b + 1) * SLOT)
        shifted = (recon[b] - bias) * over
        shifted_ref[at, :] = shifted
        normal_grad_ref[at, :] = normal_grad[b]
        backs.append(shifted * spreads[b] + found[b][0])
    unused, unused, half, unused = places(place_ref, blocks)
    first = half == 0
    sets = blocks // HALVES
    count = 3 * KIND
    one, two = lane == LANES - 2, lane == LANES - 1
    for k, b in enumerate(owner_orders(blocks)[0]):
        c = b + sets
        arrays = [
            jnp.where(first, backs[b], backs[c]),
            jnp.where(first, backs[c], backs[b]),
            jnp.where(first, normal_grad[b], normal_grad[c]),
        ]
        run_one = jnp.where(first, found[b][2], found[c][2])
        run_two = jnp.where(first, found[b][3], found[c][3])
        arrays[0] = jnp.where(one, run_one, jnp.where(two, run_two, arrays[0]))
        send_ref[k * count : k * count + KIND, :] = arrays[0][:KIND]
        tail = jnp.where(one[:8], run_one[KIND:], jnp.where(two[:8], run_two[KIND:], arrays[1][:8]))
        send_ref[k * count + KIND : k * count + KIND + 8, :] = tail
        send_ref[k * count + KIND + 8 : k * count + 2 * KIND, :] = arrays[1][8:KIND]
        send_ref[k * count + 2 * KIND : k * count + 3 * KIND, :] = arrays[2][:KIND]
        for kind in range(3):
            back_tail_ref[(3 * k + kind) * 8 : (3 * k + kind + 1) * 8, :] = arrays[kind][KIND:]
    for kind in range(3):
        for i in range(KIND, own):
            value = back_tail_ref[pl.ds(8 * kind + i - KIND, sets, stride=24), :]
            pack_extra(send_ref, value, i, kind, count, steps)


def backward_kernel(
    own,
    blocks,
    steps,
    wide,
    place_ref,
    recv_ref,
    own_ref,
    mean_ref,
    inverse_ref,
    centered_ref,
    shifted_ref,
    grad_ref,
    normal_grad_ref,
    waves_ref,
    lines_ref,
    turn_hbm,
    weights_t_hbm,
    earlier_hbm,
    misc_ref,
    starts_ref,
    turn_ref,
    weights_t_ref,
    earlier_ref,
    sems,
):
    ready = fetch(
        [(turn_hbm, turn_ref), (earlier_hbm, earlier_ref), (weights_t_hbm, weights_t_ref)], sems
    )
    windows = blocks * steps // WINDOW
    count = 2 * MODES
    mean, inverse, centered, shifted, grad, normal_grad = (
        blocks_of(ref[...])
        for ref in (
            mean_ref,
            inverse_ref,
            centered_ref,
            shifted_ref,
            grad_ref,
            normal_grad_ref,
        )
    )
    gain, bias, over = own_ref[0:SLOT], own_ref[SLOT : 2 * SLOT], own_ref[2 * SLOT : 3 * SLOT]
    row = lax.broadcasted_iota(jnp.int32, (SLOT, LANES), 0)
    lane = lax.broadcasted_iota(jnp.int32, (SLOT, LANES), 1)
    held = (row < own) & (lane < steps)
    waves = waves_ref[...]
    gain_sum = jnp.zeros((SLOT, LANES), f32)
    bias_sum = jnp.zeros((SLOT, LANES), f32)
    normal, ones, twos = [], [], []
    for k in range(blocks):
        over_q = 1.0 / (lane + (k * steps + 1 + WINDOW)).astype(f32)
        normal.append(jnp.where(held, gain * centered[k] + bias, 0.0))
        recon_grad = grad[k] / inverse[k] * over
        gain_sum = gain_sum + normal_grad[k] * centered[k] - recon_grad * shifted[k]
        bias_sum = bias_sum + normal_grad[k] - recon_grad
        first, second = statistics(
            grad[k],
            shifted[k],
            normal_grad[k] * gain * inverse[k],
            centered[k],
            mean[k],
            inverse[k],
            over_q,
        )
        ones.append(jnp.where(held, first, 0.0))
        twos.append(jnp.where(held, second, 0.0))
    gain_sum, bias_sum = jnp.where(held, gain_sum, 0.0), jnp.where(held, bias_sum, 0.0)
    ready(1)
    high, low = split(jnp.concatenate(ones + twos, 0))
    total = blocks_of(dot(jnp.concatenate([high, low], 1), earlier_ref[:, LANES:]))
    run_one = jnp.zeros((SLOT, LANES), f32)
    run_two = jnp.zeros((SLOT, LANES), f32)
    unused, unused, half, place = places(place_ref, blocks)
    first = half == 0
    sets = blocks // HALVES
    starts = [None] * blocks
    for k in reversed(range(blocks)):
        both = jnp.where(lane == row, run_one, jnp.where(lane == row + 32, run_two, 0.0))
        starts[k] = jnp.sum(both, 0, keepdims=True)
        run_one = run_one + total[k]
        run_two = run_two + total[blocks + k]
    for at, device in enumerate(share_order(blocks * CORES)):
        k = device // CORES
        starts_ref[at : at + 1, :] = jnp.where(first, starts[k], starts[k + sets])
    signal = to_wide(normal, windows)
    high, low = split(signal)
    w_high, w_low = split(waves.T)
    pairs = dot(
        jnp.concatenate([w_high, w_high, w_low], 1), jnp.concatenate([high, low, high], 0)
    )
    ready(0)
    cosine, sine = turn_ref[0:MODES], turn_ref[MODES : 2 * MODES]
    cos_b, sin_b = turn_ref[2 * MODES : 3 * MODES], turn_ref[3 * MODES : 4 * MODES]

    def turned(value):
        re, im = value[:MODES], value[MODES:]
        return jnp.concatenate([re * cosine - im * sine, -(re * sine + im * cosine)], 0)

    per = pairs.shape[1] // LANES
    after = turned(pairs[count:])
    left = turned(pairs[:count]) - after
    after = sum(after[:, b * LANES : (b + 1) * LANES] for b in range(per))
    local, total = scan_lanes(
        jnp.concatenate([left[:, b * LANES : (b + 1) * LANES] for b in range(per)], 0),
        earlier_ref[...],
    )
    run = jnp.broadcast_to(jnp.sum(after, 1, keepdims=True), (count, LANES))
    sums = []
    for b in range(per):
        sums.append(local[b * count : (b + 1) * count] + run)
        run = run + total[b * count : (b + 1) * count]
    sums = jnp.concatenate(sums, 1)
    re, im = sums[:MODES], sums[MODES:]
    crossed = jnp.concatenate([re * cos_b + im * sin_b, im * cos_b - re * sin_b], 0)
    high, low = split(crossed)
    s_high, s_low = split(lines_ref[8:16, 0:count])
    kernel_grad = dot(
        jnp.concatenate([s_high, s_high, s_low], 1), jnp.concatenate([high, low, high], 0)
    )
    k_high, k_low = split(lines_ref[0:8, :])
    overlap = dot_nt(
        jnp.concatenate([k_high, k_high, k_low], 1), jnp.concatenate([high, low, high], 1)
    )
    modes = overlap * lines_ref[16:24, 0:count]
    mix_grad = jnp.sum(overlap * lines_ref[24:32, 0:count], axis=1, keepdims=True)
    ready(2)
    mode_in_grad = stacked_dot(kernel_grad, weights_t_ref[...])
    misc_ref[...] = jnp.zeros_like(misc_ref)
    misc_ref[0:RANK, :] = mode_in_grad[0:RANK, :LANES]
    misc_ref[RANK : 2 * RANK, :] = mode_in_grad[0:RANK, LANES:]
    misc_ref[8 : 8 + RANK, 0:count] = modes[0:RANK]
    misc_ref[8 : 8 + RANK, count : 2 * count] = jnp.broadcast_to(mix_grad, (8, count))[0:RANK]
    mine = own_lanes(place, wide, own, sets)
    at = 12
    gain_row = jnp.sum(
        jnp.where(mine, jnp.sum(gain_sum, 1, keepdims=True), 0.0), axis=0, keepdims=True
    )
    bias_row = jnp.sum(
        jnp.where(mine, jnp.sum(bias_sum, 1, keepdims=True), 0.0), axis=0, keepdims=True
    )
    cot_sum = jnp.sum(recv_ref[...].reshape(blocks, 2 * KIND, LANES), axis=0)[:SLOT]
    cot_row = jnp.sum(
        jnp.where(mine, cot_sum[:, LANES - 2 : LANES - 1], 0.0), axis=0, keepdims=True
    )
    for value in (gain_row, bias_row, cot_row):
        for j in range(wide // LANES):
            misc_ref[at : at + 1, :] = value[:, j * LANES : (j + 1) * LANES]
            at += 1


def convolved_back(waves, ahead):
    rows = waves.shape[0]
    high, low = split(waves)
    out = dot_nt(jnp.concatenate([high, low], 0), ahead[:, :LANES])
    return out[:rows] + out[rows:] + dot_nt(high, ahead[:, LANES:])


def statistics(grad, shifted, scaled, centered, mean, inverse, over_q):
    variance_grad = (grad * shifted - scaled * centered) * (0.5 * inverse)
    first = (grad - scaled - 2.0 * mean * variance_grad) * over_q
    return first, variance_grad * over_q


def pieces(channels, devices):
    tiles, rest = channels // LANES, channels % LANES
    each = channels // devices
    rest_rows = channels * rest // LANES
    misc_rows = 12 + 3 * (up(channels, LANES) // LANES)
    extra = up(rest_rows + misc_rows, devices) // devices
    return tiles, rest, each, rest_rows, misc_rows, extra


def gathered(recv_ref, kind, own, steps, dense_ref):
    sets = recv_ref.shape[0] // (3 * KIND)
    for i in range(own):
        dense_ref[sets * i : sets * (i + 1), :] = unpacked(recv_ref, i, kind, sets, steps)


def mix_kernel(
    own,
    devices,
    steps,
    recv_ref,
    same_ref,
    cot_ref,
    cot_partner_ref,
    misc_ref,
    starts_ref,
    send_ref,
    dense_ref,
    partner_ref,
    cot_all_ref,
    misc_all_ref,
):
    channels = same_ref.shape[0]
    tiles, rest, each, rest_rows, misc_rows, extra = pieces(channels, devices)
    slot = send_ref.shape[0] // devices
    most = cot_partner_ref.shape[0]
    cot = cot_partner_ref[...]
    cot_all_ref[0:most, :] = jnp.where(
        lax.broadcasted_iota(jnp.int32, cot.shape, 1) < steps, cot, 0.0
    )
    lane = lax.broadcasted_iota(jnp.int32, (channels - most, LANES), 1)
    cot = jnp.zeros((channels - most, LANES), f32)
    for p in reversed(range(3)):
        row = cot_partner_ref[pl.ds(p, channels - most, stride=3), :]
        row = pltpu.roll(row, LANES - steps + EXTRA * p, 1)
        cot = jnp.where(lane < min(EXTRA * (p + 1), steps), row, cot)
    cot_all_ref[most:, :] = cot
    three = []
    for kind, ref in enumerate((dense_ref, partner_ref)):
        if ref.shape[0] > channels:
            ref[channels:, :] = jnp.zeros((ref.shape[0] - channels, LANES), f32)
        gathered(recv_ref, kind, own, steps, ref)
        high, low = split(ref[...])
        three += [high, low, high]
    three = jnp.concatenate(three, 1)
    chunk = channels if channels <= 512 else devices
    for start in range(0, channels, chunk):
        at = slice(start, start + chunk)
        six = []
        for ref in (cot_ref, cot_all_ref):
            high, low = split(ref[at, :])
            six += [high, high, low]
        grad = dot_nt(jnp.concatenate(six, 1), three)
        for j in range(tiles):
            lanes = slice(j * LANES, (j + 1) * LANES)
            tile = grad[:, lanes] * same_ref[at, lanes]
            for i in range(chunk // devices):
                send_ref[pl.ds(j * each + start // devices + i, devices, stride=slot), :] = tile[
                    devices * i : devices * (i + 1)
                ]
        if rest:
            lanes = slice(tiles * LANES, tiles * LANES + LANES)
            last = grad[:, lanes] * same_ref[at, lanes]
            folded = last[0:rest_rows]
            for g in range(1, LANES // rest):
                folded = folded + pltpu.roll(
                    last[g * rest_rows : (g + 1) * rest_rows], g * rest, 1
                )
            misc_all_ref[0:rest_rows, :] = folded
    end = rest_rows + misc_rows
    misc_all_ref[rest_rows:end, :] = misc_ref[0:misc_rows, :]
    if misc_all_ref.shape[0] > end:
        misc_all_ref[end:, :] = jnp.zeros((misc_all_ref.shape[0] - end, LANES), f32)
    for k in range(extra):
        send_ref[pl.ds(tiles * each + k, devices, stride=slot), :] = misc_all_ref[
            devices * k : devices * (k + 1), :
        ]
    for k in range(tiles * each + extra, slot - 1):
        send_ref[pl.ds(k, devices, stride=slot), :] = jnp.zeros((devices, LANES), f32)
    send_ref[pl.ds(slot - 1, devices, stride=slot), :] = starts_ref[...]


def steps_kernel(
    own,
    devices,
    place_ref,
    recv_ref,
    shares_ref,
    grad_ref,
    columns_ref,
    masked_ref,
    series_hbm,
    cot_hbm,
    earlier_hbm,
    later_hbm,
    out_ref,
    series_grad_ref,
    series_ref,
    cot_ref,
    earlier_ref,
    later_ref,
    dense_ref,
    back_ref,
    sums_ref,
    pad_ref,
    sems,
):
    ready = fetch(
        [
            (series_hbm, series_ref),
            (cot_hbm, cot_ref),
            (earlier_hbm, earlier_ref),
            (later_hbm, later_ref),
        ],
        sems,
    )
    channels, steps = series_ref.shape[1:]
    sets = channels // own
    block, core, unused, unused = places(place_ref, sets * HALVES)
    gathered(recv_ref, 0, own, steps, dense_ref)
    gathered(recv_ref, 2, own, steps, back_ref)
    for i in range(own):
        sums_ref[sets * i : sets * (i + 1), :] = recv_ref[pl.ds(i, sets, stride=3 * KIND), :]
    pad_ref[...] = jnp.zeros_like(pad_ref)
    gain, bias, shift = (columns_ref[:, k : k + 1] for k in range(3))
    restored = dense_ref[...]
    both = jnp.concatenate(split(restored), 1)
    ready(0)
    pad_ref[:, :steps] = series_ref[0]
    chunk = channels if channels <= 512 else 256
    for start in range(0, channels, chunk):
        at = slice(start, start + chunk)
        out = dot(jnp.concatenate([masked_ref[0, at, :], masked_ref[1, at, :]], 0), both)
        mixed = out[:chunk, :LANES] + out[:chunk, LANES:] + out[chunk:, :LANES]
        out_ref[0, at, :] = (pad_ref[at, :] + mixed + shift[at])[:, :steps]
    x = pad_ref[...]
    ready(2)
    local, unused = scan_lanes(jnp.concatenate([x, x * x], 0), earlier_ref[...])
    lane = lax.broadcasted_iota(jnp.int32, (channels, LANES), 1)
    over_q = 1.0 / (lane + (block * steps + 1 + WINDOW)).astype(f32)
    mean = (local[:channels] + sums_ref[:, LANES - 2 : LANES - 1]) * over_q
    variance = (local[channels:] + sums_ref[:, LANES - 1 : LANES] + WINDOW) * over_q
    inverse = lax.rsqrt(variance - mean * mean + EPSILON)
    centered = (x - mean) * inverse
    scaled = back_ref[...] * gain * inverse
    first, second = statistics(
        grad_ref[...], (restored - mean) * inverse, scaled, centered, mean, inverse, over_q
    )
    held = lane < steps
    ready(3)
    local, unused = scan_lanes(
        jnp.concatenate([jnp.where(held, first, 0.0), jnp.where(held, second, 0.0)], 0),
        later_ref[...],
    )
    slot = shares_ref.shape[0] // devices
    rows = []
    order = share_order(devices * HALVES)
    for owner in owner_orders(sets * HALVES)[0]:
        even, odd = (order.index(owner * CORES + r) * slot + slot - 1 for r in range(CORES))
        rows.append(
            jnp.where(core == 0, shares_ref[even : even + 1, :], shares_ref[odd : odd + 1, :])
        )
    later = jnp.concatenate(rows, 0)
    part = scaled + local[:channels] + 2.0 * x * local[channels:]
    ready(1)
    for i in range(own):
        at = slice(sets * i, sets * (i + 1))
        sums = later[:, i : i + 1] + 2.0 * x[at] * later[:, 32 + i : 33 + i]
        series_grad_ref[0, at, :] = cot_ref[0, at, :] + (part[at] + sums)[:, :steps]


def sum_kernel(devices, recv_ref, send_ref):
    slot = recv_ref.shape[0] // devices
    total = recv_ref[0:slot, :]
    for s in range(1, devices):
        total = total + recv_ref[s * slot : (s + 1) * slot, :]
    for s in range(devices):
        send_ref[s * slot : (s + 1) * slot, :] = total


def spread_kernel(
    devices,
    recv_ref,
    endpoint_ref,
    gain_ref,
    bias_ref,
    mode_in_ref,
    mode_out_ref,
    mode_re_ref,
    mode_im_ref,
    mixing_ref,
    out_bias_ref,
    misc_ref,
):
    channels = mixing_ref.shape[0]
    tiles, rest, each, rest_rows, misc_rows, extra = pieces(channels, devices)
    slot = recv_ref.shape[0] // devices
    for j in range(tiles):
        for i in range(each):
            mixing_ref[devices * i : devices * (i + 1), j * LANES : (j + 1) * LANES] = recv_ref[
                pl.ds(j * each + i, devices, stride=slot), :
            ]
    for k in range(extra):
        misc_ref[devices * k : devices * (k + 1), :] = recv_ref[
            pl.ds(tiles * each + k, devices, stride=slot), :
        ]
    if rest:
        folded = misc_ref[0:rest_rows, :]
        for g in range(LANES // rest):
            piece = folded if g == 0 else pltpu.roll(folded, LANES - g * rest, 1)
            mixing_ref[g * rest_rows : (g + 1) * rest_rows, tiles * LANES :] = piece[:, :rest]
    at = rest_rows
    mode_in_ref[:, 0:LANES] = misc_ref[at : at + RANK, :]
    mode_in_ref[:, LANES : 2 * LANES] = misc_ref[at + RANK : at + 2 * RANK, :]
    modes = misc_ref[at + 8 : at + 8 + RANK, :]
    mode_re_ref[...] = modes[:, 0:MODES]
    mode_im_ref[...] = modes[:, MODES : 2 * MODES]
    mode_out_ref[...] = modes[:, 2 * MODES : 2 * MODES + 1] * endpoint_ref[...]
    at += 12
    for ref in (gain_ref, bias_ref, out_bias_ref):
        for start in range(0, channels, LANES):
            size = min(LANES, channels - start)
            ref[:, start : start + size] = misc_ref[at : at + 1, 0:size]
            at += 1


def call(kernel, outs, smem=(), vmem=(), hbm=(), scratch=(), cost=None, limit=None):
    in_vmem = pl.BlockSpec(memory_space=pltpu.VMEM)
    in_smem = pl.BlockSpec(memory_space=pltpu.SMEM)
    in_hbm = pl.BlockSpec(memory_space=pltpu.HBM)
    held = [pltpu.VMEM(a.shape, a.dtype) for a in hbm] + list(scratch)
    if hbm:
        held.append(pltpu.SemaphoreType.DMA((len(hbm),)))
    hbm = [pltpu.with_memory_space_constraint(a, pltpu.HBM) for a in hbm]
    return pl.pallas_call(
        kernel,
        out_shape=tuple(jax.ShapeDtypeStruct(shape, kind) for shape, kind in outs),
        in_specs=[in_smem] * len(smem) + [in_vmem] * len(vmem) + [in_hbm] * len(hbm),
        out_specs=tuple(in_vmem for unused in outs),
        scratch_shapes=held,
        compiler_params=pltpu.CompilerParams(vmem_limit_bytes=limit),
        cost_estimate=cost,
    )(*smem, *vmem, *hbm)


def exchange(value, axis, orders):
    count = len(orders[0])
    out = lax.all_to_all(
        value.reshape(count, value.shape[0] // count, value.shape[1]),
        axis,
        split_axis=0,
        concat_axis=0,
        axis_index_groups=orders,
    )
    return out.reshape(value.shape)


def body(
    series,
    group_ids,
    rev_gain,
    rev_bias,
    mode_in,
    mode_out,
    mode_re,
    mode_im,
    mixing,
    out_bias,
    cotangent,
):
    samples, channels, steps = series.shape
    blocks = lax.axis_size("seq")
    sets = blocks // HALVES
    devices = blocks * lax.axis_size("rep")
    sharing = devices // HALVES
    own = channels // sets
    width = WINDOW // steps * LANES
    padded = up(channels, LANES)
    place = lax.axis_index(("seq", "rep")).astype(jnp.int32).reshape(1)
    halves_of = owner_orders(blocks)
    all_of = [first_order(blocks)]
    shares_of = [[h * sharing + k for k in share_order(devices)] for h in range(HALVES)]
    const = {name: jnp.asarray(value) for name, value in constants(steps).items()}
    groups = group_ids.reshape(1, channels)
    limit = (16 if channels <= 512 else 56) * 2**20
    run = functools.partial(call, limit=limit)
    busy = pl.CostEstimate(flops=4_000_000_000, bytes_accessed=8_000_000, transcendentals=0)
    brief = pl.CostEstimate(flops=100_000_000, bytes_accessed=1_000_000, transcendentals=0)

    send, restored_grad = run(
        functools.partial(send_kernel, own),
        [((blocks * 2 * KIND, LANES), f32), ((channels, LANES), f32)],
        hbm=(series, cotangent, mixing, groups),
        scratch=[pltpu.VMEM((channels, LANES), f32)],
        cost=brief,
    )
    ahead, lines, mine, columns, masked, same, cot, cot_send = run(
        functools.partial(table_kernel, own),
        [
            ((width, 2 * LANES), bf16),
            ((32, width), f32),
            ((3 * SLOT + 8, LANES), f32),
            ((channels, LANES), f32),
            ((2, channels, channels), bf16),
            ((channels, padded), f32),
            ((channels, LANES), f32),
            ((channels * 3 // 4, LANES), f32),
        ],
        smem=(place,),
        hbm=(
            cotangent,
            mixing,
            groups,
            rev_gain.reshape(1, channels),
            rev_bias.reshape(1, channels),
            out_bias.reshape(1, channels),
            mode_in.T,
            mode_out.T,
            mode_re,
            mode_im,
            const["weights"],
            const["endpoint"],
            const["turn"],
            const["scale"],
            const["later"],
        ),
        scratch=[pltpu.VMEM((LANES, LANES), f32)],
        cost=busy,
    )
    owned_rows = exchange(send, "seq", all_of)
    rows = blocks * SLOT
    windows = blocks * steps // WINDOW
    send, *kept = run(
        functools.partial(forward_kernel, own, blocks, steps),
        [((sets * 3 * KIND, LANES), f32)]
        + [((rows, LANES), f32)] * 6
        + [((windows * SLOT, LANES), f32)],
        smem=(place,),
        vmem=(
            owned_rows,
            mine,
            ahead,
            const["from_modes"],
            const["to_modes"],
            const["earlier"],
        ),
        scratch=[pltpu.VMEM((blocks * 16, LANES), f32), pltpu.VMEM((sets * 24, LANES), f32)],
        cost=brief,
    )
    there = exchange(send, "seq", halves_of)
    cot_send, kept[0] = lax.optimization_barrier((cot_send, kept[0]))
    cot_partner = lax.ppermute(cot_send, "seq", [(k, (k + sets) % blocks) for k in range(blocks)])
    tiles, rest, each, rest_rows, misc_rows, extra = pieces(channels, sharing)
    slot = up(tiles * each + extra + 1, 8)
    misc, starts = run(
        functools.partial(backward_kernel, own, blocks, steps, padded),
        [
            ((up(misc_rows, 8), LANES), f32),
            ((sharing, LANES), f32),
        ],
        smem=(place,),
        vmem=(owned_rows, mine, *kept, lines),
        hbm=(const["turn"], const["weights_t"], const["earlier"]),
        cost=busy,
    )
    (send,) = run(
        functools.partial(mix_kernel, own, sharing, steps),
        [((sharing * slot, LANES), f32)],
        vmem=(there, same, cot, cot_partner, misc, starts),
        scratch=[
            pltpu.VMEM((padded, LANES), f32),
            pltpu.VMEM((padded, LANES), f32),
            pltpu.VMEM((channels, LANES), f32),
            pltpu.VMEM((up(extra * sharing, 8), LANES), f32),
        ],
        cost=brief,
    )
    shares = exchange(send, ("seq", "rep"), shares_of)
    (send,) = run(
        functools.partial(sum_kernel, sharing),
        [((sharing * slot, LANES), f32)],
        vmem=(shares,),
        cost=brief,
    )
    sums = exchange(send, ("seq", "rep"), shares_of)
    layer_out, series_grad = run(
        functools.partial(steps_kernel, own, sharing),
        [((1, channels, steps), f32), ((1, channels, steps), f32)],
        smem=(place,),
        vmem=(there, shares, restored_grad, columns, masked),
        hbm=(series, cotangent, const["earlier"], const["later"]),
        scratch=[pltpu.VMEM((channels, LANES), f32)] * 4,
        cost=busy,
    )
    outs = run(
        functools.partial(spread_kernel, sharing),
        [
            ((1, channels), f32),
            ((1, channels), f32),
            ((RANK, ORDER), f32),
            ((RANK, ORDER), f32),
            ((RANK, MODES), f32),
            ((RANK, MODES), f32),
            ((channels, channels), f32),
            ((1, channels), f32),
        ],
        vmem=(sums, const["endpoint"]),
        scratch=[pltpu.VMEM((up(extra * sharing, 8), LANES), f32)],
        cost=brief,
    )
    return (
        layer_out,
        series_grad,
        outs[0].reshape(channels),
        outs[1].reshape(channels),
        outs[2].T,
        outs[3].T,
        outs[4],
        outs[5],
        outs[6],
        outs[7].reshape(channels),
    )


def solution(mesh):
    time_split = P("rep", None, "seq")
    in_specs = (time_split,) + (P(),) * 9 + (time_split,)
    out_specs = (time_split, time_split) + (P(),) * 8
    return jax.shard_map(body, mesh=mesh, in_specs=in_specs, out_specs=out_specs, check_vma=False)
```

```python
import functools
import math

import jax
import jax.numpy as jnp
import ml_dtypes
import numpy as np
from jax import lax
from jax.experimental import pallas as pl
from jax.experimental.pallas import tpu as pltpu
from jax.sharding import PartitionSpec as P

ORDER = 256
MODES = 32
RANK = 4
WINDOW = 720
EPSILON = 1e-05

LANES = 128
CORES = 2
HALVES = 2
SLOT = 24
KIND = 16
EXTRA = 36
f32 = jnp.float32
bf16 = jnp.bfloat16


def up(value, multiple):
    return -(-value // multiple) * multiple


def legendre_table():
    one, two = np.float32(1.0), np.float32(2.0)
    lags = np.arange(WINDOW).astype(np.float32)
    points = one - (two * (lags + np.float32(0.5))) * np.float32(1.0 / WINDOW)
    lower, this = np.zeros_like(points), np.ones_like(points)
    rows = []
    for degree in np.arange(ORDER).astype(np.float32):
        rows.append(this)
        upper = ((two * degree + one) * points * this - degree * lower) / (degree + one)
        lower, this = this, upper
    return np.stack(rows)


def in_blocks(values, steps):
    blocks = WINDOW // steps
    framed = np.zeros(values.shape[:-1] + (blocks, LANES))
    framed[..., :steps] = values.reshape(values.shape[:-1] + (blocks, steps))
    return framed.reshape(values.shape[:-1] + (blocks * LANES,))


def halves(values):
    high = values.astype(np.float32).astype(ml_dtypes.bfloat16)
    low = (values - high.astype(np.float64)).astype(ml_dtypes.bfloat16)
    return high, low


def constants(steps):
    legendre = legendre_table()
    degree = np.arange(ORDER).astype(np.float32)
    weights = legendre * ((np.float32(2.0) * degree + np.float32(1.0)) / np.float32(WINDOW))[:, None]
    flipped = in_blocks(weights[:, ::-1], steps)
    high, low = halves(flipped)
    table = {}
    table["weights"] = flipped.astype(np.float32)
    table["weights_t"] = np.concatenate([high.T, low.T], 1)
    table["endpoint"] = legendre[:, 0][None, :].astype(np.float32)
    mode = np.arange(MODES)[:, None]
    step = np.arange(WINDOW)[None, :]
    angle = 2.0 * math.pi / WINDOW * (mode * step % WINDOW)
    cosine, sine = np.cos(angle), np.sin(angle)
    back = 2.0 * math.pi / WINDOW * (mode * (WINDOW - 1 - step) % WINDOW)
    table["turn"] = np.concatenate(
        [in_blocks(v, steps) for v in (cosine, sine, np.cos(back), np.sin(back))]
    ).astype(np.float32)
    scale = np.where(np.arange(MODES) == 0, 1.0, 2.0) / WINDOW
    table["scale"] = np.tile(scale, 4)[None, :].astype(np.float32)
    high, low = halves(in_blocks(np.concatenate([cosine, -sine]), steps))
    table["to_modes"] = np.concatenate([high.T, low.T], 1)
    wave = in_blocks(np.concatenate([scale[:, None] * cosine, -scale[:, None] * sine]), steps)
    table["from_modes"] = np.concatenate(halves(wave), 1)
    lane = np.arange(LANES)
    upper = (lane[:, None] <= lane[None, :]).astype(np.float32)
    ones = np.ones((LANES, LANES), np.float32)
    for name, part in (("earlier", upper), ("later", upper.T)):
        both = np.concatenate([part, ones], 1)
        table[name] = np.concatenate([both, both]).astype(ml_dtypes.bfloat16)
    return table


def split(value):
    high = value.astype(bf16)
    return high, (value - high.astype(f32)).astype(bf16)


def dot(a, b):
    return lax.dot_general(a, b, (((1,), (0,)), ((), ())), preferred_element_type=f32)


def dot_nt(a, b):
    return lax.dot_general(a, b, (((1,), (1,)), ((), ())), preferred_element_type=f32)


def stacked_dot(value, table):
    rows, width = value.shape[0], table.shape[1] // 2
    high, low = split(value)
    out = dot(jnp.concatenate([high, low], 0), table)
    return out[:rows, :width] + out[:rows, width:] + out[rows:, :width]


def scan_lanes(value, table):
    high, low = split(value)
    out = dot(jnp.concatenate([high, low], 1), table)
    return out[:, :LANES], out[:, LANES:]


def scan_lanes_exactly(value, table):
    high, low = split(value)
    last = (value - high.astype(f32) - low.astype(f32)).astype(bf16)
    out = dot(jnp.concatenate([high, low], 1), table) + dot(last, table[:LANES])
    return out[:, :LANES], out[:, LANES:]


def unpacked(ref, i, kind, count, steps):
    rows = ref.shape[0] // count
    if i < KIND:
        return ref[pl.ds(KIND * kind + i, count, stride=rows), :]
    lane = lax.broadcasted_iota(jnp.int32, (count, LANES), 1)
    value = None
    for p in reversed(range(3)):
        row = ref[pl.ds(KIND * kind + 4 * (i - KIND) + p, count, stride=rows), :]
        row = pltpu.roll(row, LANES - steps + EXTRA * p, 1)
        value = row if value is None else jnp.where(lane < EXTRA * (p + 1), row, value)
    return value


def pack_extra(ref, value, i, kind, rows, steps):
    count = value.shape[0]
    lane = lax.broadcasted_iota(jnp.int32, (count, LANES), 1)
    behind = (lane >= steps) & (lane < steps + EXTRA)
    for p in range(3):
        at = pl.ds(KIND * kind + 4 * (i - KIND) + p, count, stride=rows)
        ref[at, :] = jnp.where(behind, pltpu.roll(value, steps - EXTRA * p, 1), ref[at, :])


def owner_order(half):
    return [k ^ 1 for k in range(half)]


def owner_orders(blocks):
    half = blocks // HALVES
    return [[h * half + k for k in owner_order(half)] for h in range(HALVES)]


def first_order(blocks):
    return sum(owner_orders(blocks)[::-1], [])


def share_order(devices):
    sharing = devices // HALVES
    if sharing == 16:
        return [15, 1, 12, 8, 14, 11, 7, 3, 4, 2, 5, 6, 0, 10, 9, 13]
    return [int(k) for k in np.random.default_rng(0).permutation(sharing)]


def places(place_ref, blocks):
    block, core = place_ref[0] // CORES, place_ref[0] % CORES
    half = blocks // HALVES
    place = jnp.int32(0)
    for k, member in enumerate(owner_order(half)):
        place = jnp.where(block % half == member, k, place)
    return block, core, block // half, place


def to_wide(blocks, windows):
    per = len(blocks) // windows
    return jnp.concatenate(
        [jnp.concatenate(blocks[w * per : (w + 1) * per], 1) for w in range(windows)], 0
    )


def to_blocks(wide, windows):
    per = wide.shape[1] // LANES
    return [
        wide[w * SLOT : (w + 1) * SLOT, b * LANES : (b + 1) * LANES]
        for w in range(windows)
        for b in range(per)
    ]


def fetch(pairs, sems):
    copies = [pltpu.make_async_copy(a, b, sems.at[k]) for k, (a, b) in enumerate(pairs)]
    for copy in copies:
        copy.start()

    def ready(*which):
        for k in which:
            copies[k].wait()

    return ready


def blocks_of(value):
    return [value[k * SLOT : (k + 1) * SLOT] for k in range(value.shape[0] // SLOT)]


def same_rows(groups_ref, start, rows):
    channels = groups_ref.shape[1]
    ids = groups_ref[...].astype(f32)
    row = lax.broadcasted_iota(jnp.int32, (rows, channels), 0) + start
    lane = lax.broadcasted_iota(jnp.int32, (rows, channels), 1)
    column = jnp.sum(jnp.where(row == lane, ids, 0.0), axis=1, keepdims=True)
    return column == ids


def own_lanes(place, width, count, blocks):
    row = lax.broadcasted_iota(jnp.int32, (SLOT, width), 0)
    lane = lax.broadcasted_iota(jnp.int32, (SLOT, width), 1)
    return (lane == row * blocks + place) & (row < count)


def send_kernel(
    own,
    series_hbm,
    cot_hbm,
    mixing_hbm,
    groups_hbm,
    send_ref,
    grad_ref,
    series_ref,
    cot_ref,
    mixing_ref,
    groups_ref,
    pad_ref,
    sems,
):
    channels, steps = cot_ref.shape[1:]
    sets = channels // own
    ready = fetch(
        [
            (groups_hbm, groups_ref),
            (mixing_hbm, mixing_ref),
            (cot_hbm, cot_ref),
            (series_hbm, series_ref),
        ],
        sems,
    )
    rows = 2 * KIND
    pad_ref[...] = jnp.zeros_like(pad_ref)
    ready(2)
    pad_ref[:, :steps] = cot_ref[0]
    ready(0, 1)
    chunk = channels if channels <= 512 else 256
    total = None
    for start in range(0, channels, chunk):
        same = same_rows(groups_ref, start, chunk)
        masked = jnp.where(same, mixing_ref[start : start + chunk, :], 0.0)
        high, low = split(masked.T)
        both = jnp.concatenate(split(pad_ref[start : start + chunk, :]), 1)
        out = dot(jnp.concatenate([high, low], 0), both)
        part = out[:channels, :LANES] + out[:channels, LANES:] + out[channels:, :LANES]
        total = part if total is None else total + part
    lane = lax.broadcasted_iota(jnp.int32, (channels, LANES), 1)
    spot = lane == LANES - 2
    behind = (lane[:sets] >= steps) & (lane[:sets] < steps + EXTRA)
    sums = jnp.sum(pad_ref[...], axis=1, keepdims=True)
    grad_ref[...] = total
    ready(3)
    pad_ref[:, :steps] = series_ref[0]
    pad_ref[...] = jnp.where(spot, sums, pad_ref[...])
    for kind, ref in enumerate((pad_ref, grad_ref)):
        for i in range(KIND):
            value = ref[sets * i : sets * (i + 1), :]
            if kind and i < own - KIND:
                there = sets * (KIND + i)
                value = jnp.where(spot[:sets], sums[there : there + sets], value)
            there, p = sets * (KIND + i // 4), i % 4
            if there < channels and p < 3:
                extra = pltpu.roll(ref[there : there + sets, :], steps - EXTRA * p, 1)
                value = jnp.where(behind, extra, value)
            send_ref[pl.ds(KIND * kind + i, sets, stride=rows), :] = value
    for half in range(1, HALVES):
        send_ref[half * sets * rows : (half + 1) * sets * rows, :] = send_ref[0 : sets * rows, :]


def table_kernel(
    own,
    place_ref,
    cot_hbm,
    mixing_hbm,
    groups_hbm,
    gain_hbm,
    bias_hbm,
    out_bias_hbm,
    mode_in_hbm,
    mode_out_hbm,
    mode_re_hbm,
    mode_im_hbm,
    weights_hbm,
    endpoint_hbm,
    turn_hbm,
    scale_hbm,
    later_hbm,
    ahead_ref,
    lines_ref,
    own_ref,
    columns_ref,
    masked_ref,
    same_ref,
    cot3_ref,
    cot_send_ref,
    cot_ref,
    mixing_ref,
    groups_ref,
    gain_ref,
    bias_ref,
    out_bias_ref,
    mode_in_ref,
    mode_out_ref,
    mode_re_ref,
    mode_im_ref,
    weights_ref,
    endpoint_ref,
    turn_ref,
    scale_ref,
    later_ref,
    turned_ref,
    cot_pad_ref,
    sems,
):
    ready = fetch(
        [
            (mode_in_hbm, mode_in_ref),
            (mode_out_hbm, mode_out_ref),
            (endpoint_hbm, endpoint_ref),
            (weights_hbm, weights_ref),
            (mode_re_hbm, mode_re_ref),
            (mode_im_hbm, mode_im_ref),
            (scale_hbm, scale_ref),
            (turn_hbm, turn_ref),
            (later_hbm, later_ref),
            (groups_hbm, groups_ref),
            (mixing_hbm, mixing_ref),
            (cot_hbm, cot_ref),
            (gain_hbm, gain_ref),
            (bias_hbm, bias_ref),
            (out_bias_hbm, out_bias_ref),
        ],
        sems,
    )
    channels, steps = cot_ref.shape[1:]
    width = ahead_ref.shape[0]
    per = width // LANES
    sets = channels // own
    count = 2 * MODES
    lines_ref[...] = jnp.zeros_like(lines_ref)
    turned_ref[...] = jnp.zeros_like(turned_ref)
    same_ref[...] = jnp.zeros_like(same_ref)
    ready(0, 1, 2, 3)
    kernel = lax.dot_general(
        mode_in_ref[...],
        weights_ref[...],
        (((1,), (0,)), ((), ())),
        precision=lax.Precision.HIGHEST,
        preferred_element_type=f32,
    )
    lines_ref[0:RANK, :] = kernel
    mix = jnp.sum(mode_out_ref[...] * endpoint_ref[...], axis=1, keepdims=True)
    ready(4, 5, 6)
    scale = scale_ref[:, 0:count]
    gain_re, gain_im = mode_re_ref[...], mode_im_ref[...]
    signed = jnp.concatenate([gain_re, -gain_im], 1) * scale
    sign = jnp.where(lax.broadcasted_iota(jnp.int32, (RANK, count), 1) < MODES, 1.0, -1.0)
    lines_ref[8 : 8 + RANK, 0:count] = signed * mix
    lines_ref[16 : 16 + RANK, 0:count] = sign * scale * mix
    lines_ref[24 : 24 + RANK, 0:count] = signed
    turned_ref[0:RANK, 0:count] = jnp.concatenate([gain_re, gain_im], 1) * mix
    columns = turned_ref[...].T[0:count]
    response = None
    for r in range(RANK):
        term = columns[:, r : r + 1] * kernel[r : r + 1, :]
        response = term if response is None else response + term
    ready(7, 8)
    real, imag = response[:MODES], response[MODES:]
    cosine, sine = turn_ref[0:MODES], turn_ref[MODES : 2 * MODES]
    cos_b, sin_b = turn_ref[2 * MODES : 3 * MODES], turn_ref[3 * MODES : 4 * MODES]
    turned = jnp.concatenate([real * cos_b + imag * sin_b, imag * cos_b - real * sin_b], 0)
    rows = jnp.concatenate([turned[:, b * LANES : (b + 1) * LANES] for b in range(per)], 0)
    local, total = scan_lanes_exactly(rows, later_ref[...])
    run = jnp.zeros((count, LANES), f32)
    suffix = [None] * per
    for b in reversed(range(per)):
        suffix[b] = local[b * count : (b + 1) * count] + run
        run = run + total[b * count : (b + 1) * count]
    for b in range(per):
        at = slice(b * LANES, (b + 1) * LANES)
        c, s = cosine[:, at], sine[:, at]
        parts = []
        for value in (suffix[b], run - suffix[b]):
            re, im = value[:MODES], value[MODES:]
            parts += [re * c + im * s, im * c - re * s]
        high, low = split(jnp.concatenate(parts, 0).T)
        ahead_ref[at, 0:LANES] = high
        ahead_ref[at, LANES : 2 * LANES] = low
    ready(9, 10, 11, 12, 13, 14)
    chunk = channels if channels <= 512 else 256
    for start in range(0, channels, chunk):
        at = slice(start, start + chunk)
        same = same_rows(groups_ref, start, chunk)
        high, low = split(jnp.where(same, mixing_ref[at, :], 0.0))
        masked_ref[0, at, :] = high
        masked_ref[1, at, :] = low
        same_ref[at, 0:channels] = jnp.where(same, 1.0, 0.0)
        row = lax.broadcasted_iota(jnp.int32, (chunk, channels), 0) + start
        lane = lax.broadcasted_iota(jnp.int32, (chunk, channels), 1)
        for k, ref in enumerate((gain_ref, bias_ref, out_bias_ref)):
            columns_ref[at, k : k + 1] = jnp.sum(
                jnp.where(row == lane, ref[...], 0.0), axis=1, keepdims=True
            )
    unused, unused, unused, place = places(place_ref, sets * HALVES)
    mine = own_lanes(place, channels, own, sets)
    gain = jnp.sum(jnp.where(mine, gain_ref[...], 0.0), axis=1, keepdims=True)
    gain = jnp.where(lax.broadcasted_iota(jnp.int32, (SLOT, 1), 0) < own, gain, 1.0)
    bias = jnp.sum(jnp.where(mine, bias_ref[...], 0.0), axis=1, keepdims=True)
    own_ref[0:SLOT, :] = jnp.broadcast_to(gain, (SLOT, LANES))
    own_ref[SLOT : 2 * SLOT, :] = jnp.broadcast_to(bias, (SLOT, LANES))
    own_ref[2 * SLOT : 3 * SLOT, :] = jnp.broadcast_to(1.0 / gain, (SLOT, LANES))
    own_ref[3 * SLOT :, :] = jnp.broadcast_to(scale_ref[...], (8, LANES))
    cot_pad_ref[...] = jnp.zeros_like(cot_pad_ref)
    cot_pad_ref[:, :steps] = cot_ref[0]
    high, low = split(cot_pad_ref[...])
    cot3_ref[...] = jnp.concatenate([high, high, low], 1)
    most = cot_send_ref.shape[0]
    lane = lax.broadcasted_iota(jnp.int32, (channels - most, LANES), 1)
    behind = (lane >= steps) & (lane < steps + EXTRA)
    cot_send_ref[...] = cot_pad_ref[0:most, :]
    for p in range(3):
        at = pl.ds(p, channels - most, stride=3)
        moved = pltpu.roll(cot_pad_ref[most:, :], steps - EXTRA * p, 1)
        cot_send_ref[at, :] = jnp.where(behind, moved, cot_send_ref[at, :])


def normalized(x, blocks, steps, earlier):
    rows = x.shape[0]
    local, total = scan_lanes(jnp.concatenate([x, x * x], 0), earlier)
    first, second = blocks_of(local[:rows]), blocks_of(local[rows:])
    first_all, second_all = blocks_of(total[:rows]), blocks_of(total[rows:])
    run_one = jnp.zeros((SLOT, LANES), f32)
    run_two = jnp.zeros((SLOT, LANES), f32)
    lane = lax.broadcasted_iota(jnp.int32, (SLOT, LANES), 1)
    found = []
    for k in range(blocks):
        inverse = 1.0 / (lane + (k * steps + 1 + WINDOW)).astype(f32)
        mean = (first[k] + run_one) * inverse
        variance = (second[k] + run_two + WINDOW) * inverse - mean * mean + EPSILON
        found.append((mean, variance, run_one, run_two))
        run_one = run_one + first_all[k]
        run_two = run_two + second_all[k]
    return found


def owned(recv_ref, tail_ref, own, blocks, steps):
    lane = lax.broadcasted_iota(jnp.int32, (blocks, LANES), 1)
    tail_ref[...] = jnp.zeros_like(tail_ref)
    for kind in range(2):
        for i in range(KIND, own):
            tail_ref[pl.ds(8 * kind + i - KIND, blocks, stride=16), :] = jnp.where(
                lane < steps, unpacked(recv_ref, i, kind, blocks, steps), 0.0
            )
    got = recv_ref[...].reshape(blocks, 2 * KIND, LANES)
    got = jnp.where(lax.broadcasted_iota(jnp.int32, got.shape, 2) < steps, got, 0.0)
    tail = tail_ref[...].reshape(blocks, 16, LANES)
    x = jnp.concatenate([got[:, 0:KIND], tail[:, 0:8]], 1)
    grad = jnp.concatenate([got[:, KIND : 2 * KIND], tail[:, 8:16]], 1)
    order = first_order(blocks)
    slots = [order.index(b) for b in range(blocks)]
    return [x[k] for k in slots], [grad[k] for k in slots]


def forward_kernel(
    own,
    blocks,
    steps,
    place_ref,
    recv_ref,
    own_ref,
    ahead_ref,
    from_modes_ref,
    to_modes_ref,
    earlier_ref,
    send_ref,
    mean_ref,
    inverse_ref,
    centered_ref,
    shifted_ref,
    grad_ref,
    normal_grad_ref,
    waves_ref,
    tail_ref,
    back_tail_ref,
):
    windows = blocks * steps // WINDOW
    x, grad = owned(recv_ref, tail_ref, own, blocks, steps)
    found = normalized(jnp.concatenate(x, 0), blocks, steps, earlier_ref[...])
    gain, bias, over = own_ref[0:SLOT], own_ref[SLOT : 2 * SLOT], own_ref[2 * SLOT : 3 * SLOT]
    row = lax.broadcasted_iota(jnp.int32, (SLOT, LANES), 0)
    lane = lax.broadcasted_iota(jnp.int32, (SLOT, LANES), 1)
    held = (row < own) & (lane < steps)
    normal, spreads, recon_grad = [], [], []
    for k in range(blocks):
        at = slice(k * SLOT, (k + 1) * SLOT)
        mean, variance = found[k][:2]
        inverse = lax.rsqrt(variance)
        spread = variance * inverse
        centered = (x[k] - mean) * inverse
        normal.append(gain * centered + bias)
        spreads.append(spread)
        recon_grad.append(jnp.where(held, grad[k] * spread * over, 0.0))
        mean_ref[at, :] = mean
        inverse_ref[at, :] = inverse
        centered_ref[at, :] = centered
        grad_ref[at, :] = grad[k]
    spectra = stacked_dot(to_wide(normal, windows), ahead_ref[...])
    waves = stacked_dot(to_wide(recon_grad, windows), to_modes_ref[...])
    count = 2 * MODES
    current, before = spectra[:, :count], spectra[:, count:]
    zero = jnp.zeros((SLOT, count), f32)
    after = zero
    if windows > 1:
        current = current + jnp.concatenate([zero, before[:-SLOT]], 0)
        after = jnp.concatenate([waves[SLOT:], zero], 0)
    recon = stacked_dot(current, from_modes_ref[...])
    waves = jnp.concatenate([waves, after], 1)
    waves_ref[...] = waves
    recon = to_blocks(recon, windows)
    normal_grad = to_blocks(convolved_back(waves * own_ref[3 * SLOT : 3 * SLOT + 1], ahead_ref[...]), windows)
    backs = []
    for b in range(blocks):
        at = slice(b * SLOT, (b + 1) * SLOT)
        shifted = (recon[b] - bias) * over
        shifted_ref[at, :] = shifted
        normal_grad_ref[at, :] = normal_grad[b]
        backs.append(shifted * spreads[b] + found[b][0])
    unused, unused, half, unused = places(place_ref, blocks)
    first = half == 0
    sets = blocks // HALVES
    count = 3 * KIND
    one, two = lane == LANES - 2, lane == LANES - 1
    for k, b in enumerate(owner_orders(blocks)[0]):
        c = b + sets
        arrays = [
            jnp.where(first, backs[b], backs[c]),
            jnp.where(first, backs[c], backs[b]),
            jnp.where(first, normal_grad[b], normal_grad[c]),
        ]
        run_one = jnp.where(first, found[b][2], found[c][2])
        run_two = jnp.where(first, found[b][3], found[c][3])
        arrays[0] = jnp.where(one, run_one, jnp.where(two, run_two, arrays[0]))
        send_ref[k * count : k * count + KIND, :] = arrays[0][:KIND]
        tail = jnp.where(one[:8], run_one[KIND:], jnp.where(two[:8], run_two[KIND:], arrays[1][:8]))
        send_ref[k * count + KIND : k * count + KIND + 8, :] = tail
        send_ref[k * count + KIND + 8 : k * count + 2 * KIND, :] = arrays[1][8:KIND]
        send_ref[k * count + 2 * KIND : k * count + 3 * KIND, :] = arrays[2][:KIND]
        for kind in range(3):
            back_tail_ref[(3 * k + kind) * 8 : (3 * k + kind + 1) * 8, :] = arrays[kind][KIND:]
    for kind in range(3):
        for i in range(KIND, own):
            value = back_tail_ref[pl.ds(8 * kind + i - KIND, sets, stride=24), :]
            pack_extra(send_ref, value, i, kind, count, steps)


def backward_kernel(
    own,
    blocks,
    steps,
    wide,
    place_ref,
    recv_ref,
    own_ref,
    mean_ref,
    inverse_ref,
    centered_ref,
    shifted_ref,
    grad_ref,
    normal_grad_ref,
    waves_ref,
    lines_ref,
    turn_hbm,
    weights_t_hbm,
    earlier_hbm,
    misc_ref,
    starts_ref,
    turn_ref,
    weights_t_ref,
    earlier_ref,
    sems,
):
    ready = fetch(
        [(turn_hbm, turn_ref), (earlier_hbm, earlier_ref), (weights_t_hbm, weights_t_ref)], sems
    )
    windows = blocks * steps // WINDOW
    count = 2 * MODES
    mean, inverse, centered, shifted, grad, normal_grad = (
        blocks_of(ref[...])
        for ref in (
            mean_ref,
            inverse_ref,
            centered_ref,
            shifted_ref,
            grad_ref,
            normal_grad_ref,
        )
    )
    gain, bias, over = own_ref[0:SLOT], own_ref[SLOT : 2 * SLOT], own_ref[2 * SLOT : 3 * SLOT]
    row = lax.broadcasted_iota(jnp.int32, (SLOT, LANES), 0)
    lane = lax.broadcasted_iota(jnp.int32, (SLOT, LANES), 1)
    held = (row < own) & (lane < steps)
    waves = waves_ref[...]
    gain_sum = jnp.zeros((SLOT, LANES), f32)
    bias_sum = jnp.zeros((SLOT, LANES), f32)
    normal, ones, twos = [], [], []
    for k in range(blocks):
        over_q = 1.0 / (lane + (k * steps + 1 + WINDOW)).astype(f32)
        normal.append(jnp.where(held, gain * centered[k] + bias, 0.0))
        recon_grad = grad[k] / inverse[k] * over
        gain_sum = gain_sum + normal_grad[k] * centered[k] - recon_grad * shifted[k]
        bias_sum = bias_sum + normal_grad[k] - recon_grad
        first, second = statistics(
            grad[k],
            shifted[k],
            normal_grad[k] * gain * inverse[k],
            centered[k],
            mean[k],
            inverse[k],
            over_q,
        )
        ones.append(jnp.where(held, first, 0.0))
        twos.append(jnp.where(held, second, 0.0))
    gain_sum, bias_sum = jnp.where(held, gain_sum, 0.0), jnp.where(held, bias_sum, 0.0)
    ready(1)
    high, low = split(jnp.concatenate(ones + twos, 0))
    total = blocks_of(dot(jnp.concatenate([high, low], 1), earlier_ref[:, LANES:]))
    run_one = jnp.zeros((SLOT, LANES), f32)
    run_two = jnp.zeros((SLOT, LANES), f32)
    unused, unused, half, place = places(place_ref, blocks)
    first = half == 0
    sets = blocks // HALVES
    starts = [None] * blocks
    for k in reversed(range(blocks)):
        both = jnp.where(lane == row, run_one, jnp.where(lane == row + 32, run_two, 0.0))
        starts[k] = jnp.sum(both, 0, keepdims=True)
        run_one = run_one + total[k]
        run_two = run_two + total[blocks + k]
    for at, device in enumerate(share_order(blocks * CORES)):
        k = device // CORES
        starts_ref[at : at + 1, :] = jnp.where(first, starts[k], starts[k + sets])
    signal = to_wide(normal, windows)
    high, low = split(signal)
    w_high, w_low = split(waves.T)
    pairs = dot(
        jnp.concatenate([w_high, w_high, w_low], 1), jnp.concatenate([high, low, high], 0)
    )
    ready(0)
    cosine, sine = turn_ref[0:MODES], turn_ref[MODES : 2 * MODES]
    cos_b, sin_b = turn_ref[2 * MODES : 3 * MODES], turn_ref[3 * MODES : 4 * MODES]

    def turned(value):
        re, im = value[:MODES], value[MODES:]
        return jnp.concatenate([re * cosine - im * sine, -(re * sine + im * cosine)], 0)

    per = pairs.shape[1] // LANES
    after = turned(pairs[count:])
    left = turned(pairs[:count]) - after
    after = sum(after[:, b * LANES : (b + 1) * LANES] for b in range(per))
    local, total = scan_lanes(
        jnp.concatenate([left[:, b * LANES : (b + 1) * LANES] for b in range(per)], 0),
        earlier_ref[...],
    )
    run = jnp.broadcast_to(jnp.sum(after, 1, keepdims=True), (count, LANES))
    sums = []
    for b in range(per):
        sums.append(local[b * count : (b + 1) * count] + run)
        run = run + total[b * count : (b + 1) * count]
    sums = jnp.concatenate(sums, 1)
    re, im = sums[:MODES], sums[MODES:]
    crossed = jnp.concatenate([re * cos_b + im * sin_b, im * cos_b - re * sin_b], 0)
    high, low = split(crossed)
    s_high, s_low = split(lines_ref[8:16, 0:count])
    kernel_grad = dot(
        jnp.concatenate([s_high, s_high, s_low], 1), jnp.concatenate([high, low, high], 0)
    )
    k_high, k_low = split(lines_ref[0:8, :])
    overlap = dot_nt(
        jnp.concatenate([k_high, k_high, k_low], 1), jnp.concatenate([high, low, high], 1)
    )
    modes = overlap * lines_ref[16:24, 0:count]
    mix_grad = jnp.sum(overlap * lines_ref[24:32, 0:count], axis=1, keepdims=True)
    ready(2)
    mode_in_grad = stacked_dot(kernel_grad, weights_t_ref[...])
    misc_ref[...] = jnp.zeros_like(misc_ref)
    misc_ref[0:RANK, :] = mode_in_grad[0:RANK, :LANES]
    misc_ref[RANK : 2 * RANK, :] = mode_in_grad[0:RANK, LANES:]
    misc_ref[8 : 8 + RANK, 0:count] = modes[0:RANK]
    misc_ref[8 : 8 + RANK, count : 2 * count] = jnp.broadcast_to(mix_grad, (8, count))[0:RANK]
    mine = own_lanes(place, wide, own, sets)
    at = 12
    gain_row = jnp.sum(
        jnp.where(mine, jnp.sum(gain_sum, 1, keepdims=True), 0.0), axis=0, keepdims=True
    )
    bias_row = jnp.sum(
        jnp.where(mine, jnp.sum(bias_sum, 1, keepdims=True), 0.0), axis=0, keepdims=True
    )
    cot_sum = jnp.sum(recv_ref[...].reshape(blocks, 2 * KIND, LANES), axis=0)[:SLOT]
    cot_row = jnp.sum(
        jnp.where(mine, cot_sum[:, LANES - 2 : LANES - 1], 0.0), axis=0, keepdims=True
    )
    for value in (gain_row, bias_row, cot_row):
        for j in range(wide // LANES):
            misc_ref[at : at + 1, :] = value[:, j * LANES : (j + 1) * LANES]
            at += 1


def convolved_back(waves, ahead):
    rows = waves.shape[0]
    high, low = split(waves)
    out = dot_nt(jnp.concatenate([high, low], 0), ahead[:, :LANES])
    return out[:rows] + out[rows:] + dot_nt(high, ahead[:, LANES:])


def statistics(grad, shifted, scaled, centered, mean, inverse, over_q):
    variance_grad = (grad * shifted - scaled * centered) * (0.5 * inverse)
    first = (grad - scaled - 2.0 * mean * variance_grad) * over_q
    return first, variance_grad * over_q


def pieces(channels, devices):
    tiles, rest = channels // LANES, channels % LANES
    each = channels // devices
    rest_rows = channels * rest // LANES
    misc_rows = 12 + 3 * (up(channels, LANES) // LANES)
    extra = up(rest_rows + misc_rows, devices) // devices
    return tiles, rest, each, rest_rows, misc_rows, extra


def gathered(recv_ref, kind, own, steps, dense_ref):
    sets = recv_ref.shape[0] // (3 * KIND)
    for i in range(own):
        dense_ref[sets * i : sets * (i + 1), :] = unpacked(recv_ref, i, kind, sets, steps)


def mix_kernel(
    own,
    devices,
    steps,
    recv_ref,
    same_ref,
    cot3_ref,
    cot_partner_ref,
    misc_ref,
    starts_ref,
    send_ref,
    dense_ref,
    partner_ref,
    cot_all_ref,
    misc_all_ref,
):
    channels = same_ref.shape[0]
    tiles, rest, each, rest_rows, misc_rows, extra = pieces(channels, devices)
    slot = send_ref.shape[0] // devices
    most = cot_partner_ref.shape[0]
    cot = cot_partner_ref[...]
    cot_all_ref[0:most, :] = jnp.where(
        lax.broadcasted_iota(jnp.int32, cot.shape, 1) < steps, cot, 0.0
    )
    lane = lax.broadcasted_iota(jnp.int32, (channels - most, LANES), 1)
    cot = jnp.zeros((channels - most, LANES), f32)
    for p in reversed(range(3)):
        row = cot_partner_ref[pl.ds(p, channels - most, stride=3), :]
        row = pltpu.roll(row, LANES - steps + EXTRA * p, 1)
        cot = jnp.where(lane < min(EXTRA * (p + 1), steps), row, cot)
    cot_all_ref[most:, :] = cot
    three = []
    for kind, ref in enumerate((dense_ref, partner_ref)):
        if ref.shape[0] > channels:
            ref[channels:, :] = jnp.zeros((ref.shape[0] - channels, LANES), f32)
        gathered(recv_ref, kind, own, steps, ref)
        high, low = split(ref[...])
        three += [high, low, high]
    three = jnp.concatenate(three, 1)
    chunk = channels if channels <= 512 else devices
    for start in range(0, channels, chunk):
        at = slice(start, start + chunk)
        high, low = split(cot_all_ref[at, :])
        grad = dot_nt(jnp.concatenate([cot3_ref[at, :], high, high, low], 1), three)
        for j in range(tiles):
            lanes = slice(j * LANES, (j + 1) * LANES)
            tile = grad[:, lanes] * same_ref[at, lanes]
            for i in range(chunk // devices):
                send_ref[pl.ds(j * each + start // devices + i, devices, stride=slot), :] = tile[
                    devices * i : devices * (i + 1)
                ]
        if rest:
            lanes = slice(tiles * LANES, tiles * LANES + LANES)
            last = grad[:, lanes] * same_ref[at, lanes]
            folded = last[0:rest_rows]
            for g in range(1, LANES // rest):
                folded = folded + pltpu.roll(
                    last[g * rest_rows : (g + 1) * rest_rows], g * rest, 1
                )
            misc_all_ref[0:rest_rows, :] = folded
    end = rest_rows + misc_rows
    misc_all_ref[rest_rows:end, :] = misc_ref[0:misc_rows, :]
    if misc_all_ref.shape[0] > end:
        misc_all_ref[end:, :] = jnp.zeros((misc_all_ref.shape[0] - end, LANES), f32)
    for k in range(extra):
        send_ref[pl.ds(tiles * each + k, devices, stride=slot), :] = misc_all_ref[
            devices * k : devices * (k + 1), :
        ]
    for k in range(tiles * each + extra, slot - 1):
        send_ref[pl.ds(k, devices, stride=slot), :] = jnp.zeros((devices, LANES), f32)
    send_ref[pl.ds(slot - 1, devices, stride=slot), :] = starts_ref[...]


def steps_kernel(
    own,
    devices,
    place_ref,
    recv_ref,
    shares_ref,
    grad_ref,
    columns_ref,
    masked_ref,
    series_hbm,
    cot_hbm,
    earlier_hbm,
    later_hbm,
    out_ref,
    series_grad_ref,
    series_ref,
    cot_ref,
    earlier_ref,
    later_ref,
    dense_ref,
    back_ref,
    sums_ref,
    pad_ref,
    sems,
):
    ready = fetch(
        [
            (series_hbm, series_ref),
            (cot_hbm, cot_ref),
            (earlier_hbm, earlier_ref),
            (later_hbm, later_ref),
        ],
        sems,
    )
    channels, steps = series_ref.shape[1:]
    sets = channels // own
    block, core, unused, unused = places(place_ref, sets * HALVES)
    gathered(recv_ref, 0, own, steps, dense_ref)
    gathered(recv_ref, 2, own, steps, back_ref)
    for i in range(own):
        sums_ref[sets * i : sets * (i + 1), :] = recv_ref[pl.ds(i, sets, stride=3 * KIND), :]
    pad_ref[...] = jnp.zeros_like(pad_ref)
    gain, bias, shift = (columns_ref[:, k : k + 1] for k in range(3))
    restored = dense_ref[...]
    both = jnp.concatenate(split(restored), 1)
    ready(0)
    pad_ref[:, :steps] = series_ref[0]
    chunk = channels if channels <= 512 else 256
    for start in range(0, channels, chunk):
        at = slice(start, start + chunk)
        out = dot(jnp.concatenate([masked_ref[0, at, :], masked_ref[1, at, :]], 0), both)
        mixed = out[:chunk, :LANES] + out[:chunk, LANES:] + out[chunk:, :LANES]
        out_ref[0, at, :] = (pad_ref[at, :] + mixed + shift[at])[:, :steps]
    x = pad_ref[...]
    ready(2)
    local, unused = scan_lanes(jnp.concatenate([x, x * x], 0), earlier_ref[...])
    lane = lax.broadcasted_iota(jnp.int32, (channels, LANES), 1)
    over_q = 1.0 / (lane + (block * steps + 1 + WINDOW)).astype(f32)
    mean = (local[:channels] + sums_ref[:, LANES - 2 : LANES - 1]) * over_q
    variance = (local[channels:] + sums_ref[:, LANES - 1 : LANES] + WINDOW) * over_q
    inverse = lax.rsqrt(variance - mean * mean + EPSILON)
    centered = (x - mean) * inverse
    scaled = back_ref[...] * gain * inverse
    first, second = statistics(
        grad_ref[...], (restored - mean) * inverse, scaled, centered, mean, inverse, over_q
    )
    held = lane < steps
    ready(3)
    local, unused = scan_lanes(
        jnp.concatenate([jnp.where(held, first, 0.0), jnp.where(held, second, 0.0)], 0),
        later_ref[...],
    )
    slot = shares_ref.shape[0] // devices
    rows = []
    order = share_order(devices * HALVES)
    for owner in owner_orders(sets * HALVES)[0]:
        even, odd = (order.index(owner * CORES + r) * slot + slot - 1 for r in range(CORES))
        rows.append(
            jnp.where(core == 0, shares_ref[even : even + 1, :], shares_ref[odd : odd + 1, :])
        )
    later = jnp.concatenate(rows, 0)
    part = scaled + local[:channels] + 2.0 * x * local[channels:]
    ready(1)
    for i in range(own):
        at = slice(sets * i, sets * (i + 1))
        sums = later[:, i : i + 1] + 2.0 * x[at] * later[:, 32 + i : 33 + i]
        series_grad_ref[0, at, :] = cot_ref[0, at, :] + (part[at] + sums)[:, :steps]


def sum_kernel(devices, recv_ref, send_ref):
    slot = recv_ref.shape[0] // devices
    total = recv_ref[0:slot, :]
    for s in range(1, devices):
        total = total + recv_ref[s * slot : (s + 1) * slot, :]
    for s in range(devices):
        send_ref[s * slot : (s + 1) * slot, :] = total


def spread_kernel(
    devices,
    recv_ref,
    endpoint_ref,
    gain_ref,
    bias_ref,
    mode_in_ref,
    mode_out_ref,
    mode_re_ref,
    mode_im_ref,
    mixing_ref,
    out_bias_ref,
    misc_ref,
):
    channels = mixing_ref.shape[0]
    tiles, rest, each, rest_rows, misc_rows, extra = pieces(channels, devices)
    slot = recv_ref.shape[0] // devices
    for j in range(tiles):
        for i in range(each):
            mixing_ref[devices * i : devices * (i + 1), j * LANES : (j + 1) * LANES] = recv_ref[
                pl.ds(j * each + i, devices, stride=slot), :
            ]
    for k in range(extra):
        misc_ref[devices * k : devices * (k + 1), :] = recv_ref[
            pl.ds(tiles * each + k, devices, stride=slot), :
        ]
    if rest:
        folded = misc_ref[0:rest_rows, :]
        for g in range(LANES // rest):
            piece = folded if g == 0 else pltpu.roll(folded, LANES - g * rest, 1)
            mixing_ref[g * rest_rows : (g + 1) * rest_rows, tiles * LANES :] = piece[:, :rest]
    at = rest_rows
    mode_in_ref[:, 0:LANES] = misc_ref[at : at + RANK, :]
    mode_in_ref[:, LANES : 2 * LANES] = misc_ref[at + RANK : at + 2 * RANK, :]
    modes = misc_ref[at + 8 : at + 8 + RANK, :]
    mode_re_ref[...] = modes[:, 0:MODES]
    mode_im_ref[...] = modes[:, MODES : 2 * MODES]
    mode_out_ref[...] = modes[:, 2 * MODES : 2 * MODES + 1] * endpoint_ref[...]
    at += 12
    for ref in (gain_ref, bias_ref, out_bias_ref):
        for start in range(0, channels, LANES):
            size = min(LANES, channels - start)
            ref[:, start : start + size] = misc_ref[at : at + 1, 0:size]
            at += 1


def call(kernel, outs, smem=(), vmem=(), hbm=(), scratch=(), cost=None, limit=None):
    in_vmem = pl.BlockSpec(memory_space=pltpu.VMEM)
    in_smem = pl.BlockSpec(memory_space=pltpu.SMEM)
    in_hbm = pl.BlockSpec(memory_space=pltpu.HBM)
    held = [pltpu.VMEM(a.shape, a.dtype) for a in hbm] + list(scratch)
    if hbm:
        held.append(pltpu.SemaphoreType.DMA((len(hbm),)))
    hbm = [pltpu.with_memory_space_constraint(a, pltpu.HBM) for a in hbm]
    return pl.pallas_call(
        kernel,
        out_shape=tuple(jax.ShapeDtypeStruct(shape, kind) for shape, kind in outs),
        in_specs=[in_smem] * len(smem) + [in_vmem] * len(vmem) + [in_hbm] * len(hbm),
        out_specs=tuple(in_vmem for unused in outs),
        scratch_shapes=held,
        compiler_params=pltpu.CompilerParams(vmem_limit_bytes=limit),
        cost_estimate=cost,
    )(*smem, *vmem, *hbm)


def exchange(value, axis, orders):
    count = len(orders[0])
    out = lax.all_to_all(
        value.reshape(count, value.shape[0] // count, value.shape[1]),
        axis,
        split_axis=0,
        concat_axis=0,
        axis_index_groups=orders,
    )
    return out.reshape(value.shape)


def body(
    series,
    group_ids,
    rev_gain,
    rev_bias,
    mode_in,
    mode_out,
    mode_re,
    mode_im,
    mixing,
    out_bias,
    cotangent,
):
    samples, channels, steps = series.shape
    blocks = lax.axis_size("seq")
    sets = blocks // HALVES
    devices = blocks * lax.axis_size("rep")
    sharing = devices // HALVES
    own = channels // sets
    width = WINDOW // steps * LANES
    padded = up(channels, LANES)
    place = lax.axis_index(("seq", "rep")).astype(jnp.int32).reshape(1)
    halves_of = owner_orders(blocks)
    all_of = [first_order(blocks)]
    shares_of = [[h * sharing + k for k in share_order(devices)] for h in range(HALVES)]
    const = {name: jnp.asarray(value) for name, value in constants(steps).items()}
    groups = group_ids.reshape(1, channels)
    limit = (16 if channels <= 512 else 56) * 2**20
    run = functools.partial(call, limit=limit)
    busy = pl.CostEstimate(flops=4_000_000_000, bytes_accessed=8_000_000, transcendentals=0)
    brief = pl.CostEstimate(flops=100_000_000, bytes_accessed=1_000_000, transcendentals=0)

    send, restored_grad = run(
        functools.partial(send_kernel, own),
        [((blocks * 2 * KIND, LANES), f32), ((channels, LANES), f32)],
        hbm=(series, cotangent, mixing, groups),
        scratch=[pltpu.VMEM((channels, LANES), f32)],
        cost=brief,
    )
    ahead, lines, mine, columns, masked, same, cot, cot_send = run(
        functools.partial(table_kernel, own),
        [
            ((width, 2 * LANES), bf16),
            ((32, width), f32),
            ((3 * SLOT + 8, LANES), f32),
            ((channels, LANES), f32),
            ((2, channels, channels), bf16),
            ((channels, padded), f32),
            ((channels, 3 * LANES), bf16),
            ((channels * 3 // 4, LANES), f32),
        ],
        smem=(place,),
        hbm=(
            cotangent,
            mixing,
            groups,
            rev_gain.reshape(1, channels),
            rev_bias.reshape(1, channels),
            out_bias.reshape(1, channels),
            mode_in.T,
            mode_out.T,
            mode_re,
            mode_im,
            const["weights"],
            const["endpoint"],
            const["turn"],
            const["scale"],
            const["later"],
        ),
        scratch=[pltpu.VMEM((LANES, LANES), f32), pltpu.VMEM((channels, LANES), f32)],
        cost=busy,
    )
    owned_rows = exchange(send, "seq", all_of)
    rows = blocks * SLOT
    windows = blocks * steps // WINDOW
    send, *kept = run(
        functools.partial(forward_kernel, own, blocks, steps),
        [((sets * 3 * KIND, LANES), f32)]
        + [((rows, LANES), f32)] * 6
        + [((windows * SLOT, LANES), f32)],
        smem=(place,),
        vmem=(
            owned_rows,
            mine,
            ahead,
            const["from_modes"],
            const["to_modes"],
            const["earlier"],
        ),
        scratch=[pltpu.VMEM((blocks * 16, LANES), f32), pltpu.VMEM((sets * 24, LANES), f32)],
        cost=brief,
    )
    there = exchange(send, "seq", halves_of)
    cot_send, kept[0] = lax.optimization_barrier((cot_send, kept[0]))
    cot_partner = lax.ppermute(cot_send, "seq", [(k, (k + sets) % blocks) for k in range(blocks)])
    tiles, rest, each, rest_rows, misc_rows, extra = pieces(channels, sharing)
    slot = up(tiles * each + extra + 1, 8)
    misc, starts = run(
        functools.partial(backward_kernel, own, blocks, steps, padded),
        [
            ((up(misc_rows, 8), LANES), f32),
            ((sharing, LANES), f32),
        ],
        smem=(place,),
        vmem=(owned_rows, mine, *kept, lines),
        hbm=(const["turn"], const["weights_t"], const["earlier"]),
        cost=busy,
    )
    (send,) = run(
        functools.partial(mix_kernel, own, sharing, steps),
        [((sharing * slot, LANES), f32)],
        vmem=(there, same, cot, cot_partner, misc, starts),
        scratch=[
            pltpu.VMEM((padded, LANES), f32),
            pltpu.VMEM((padded, LANES), f32),
            pltpu.VMEM((channels, LANES), f32),
            pltpu.VMEM((up(extra * sharing, 8), LANES), f32),
        ],
        cost=brief,
    )
    shares = exchange(send, ("seq", "rep"), shares_of)
    (send,) = run(
        functools.partial(sum_kernel, sharing),
        [((sharing * slot, LANES), f32)],
        vmem=(shares,),
        cost=brief,
    )
    sums = exchange(send, ("seq", "rep"), shares_of)
    layer_out, series_grad = run(
        functools.partial(steps_kernel, own, sharing),
        [((1, channels, steps), f32), ((1, channels, steps), f32)],
        smem=(place,),
        vmem=(there, shares, restored_grad, columns, masked),
        hbm=(series, cotangent, const["earlier"], const["later"]),
        scratch=[pltpu.VMEM((channels, LANES), f32)] * 4,
        cost=busy,
    )
    outs = run(
        functools.partial(spread_kernel, sharing),
        [
            ((1, channels), f32),
            ((1, channels), f32),
            ((RANK, ORDER), f32),
            ((RANK, ORDER), f32),
            ((RANK, MODES), f32),
            ((RANK, MODES), f32),
            ((channels, channels), f32),
            ((1, channels), f32),
        ],
        vmem=(sums, const["endpoint"]),
        scratch=[pltpu.VMEM((up(extra * sharing, 8), LANES), f32)],
        cost=brief,
    )
    return (
        layer_out,
        series_grad,
        outs[0].reshape(channels),
        outs[1].reshape(channels),
        outs[2].T,
        outs[3].T,
        outs[4],
        outs[5],
        outs[6],
        outs[7].reshape(channels),
    )


def solution(mesh):
    time_split = P("rep", None, "seq")
    in_specs = (time_split,) + (P(),) * 9 + (time_split,)
    out_specs = (time_split, time_split) + (P(),) * 8
    return jax.shard_map(body, mesh=mesh, in_specs=in_specs, out_specs=out_specs, check_vma=False)
```

```python
import functools
import math

import jax
import jax.numpy as jnp
import ml_dtypes
import numpy as np
from jax import lax
from jax.experimental import pallas as pl
from jax.experimental.pallas import tpu as pltpu
from jax.sharding import PartitionSpec as P

ORDER = 256
MODES = 32
RANK = 4
WINDOW = 720
EPSILON = 1e-05

LANES = 128
CORES = 2
HALVES = 2
SLOT = 24
KIND = 16
EXTRA = 36
f32 = jnp.float32
bf16 = jnp.bfloat16


def up(value, multiple):
    return -(-value // multiple) * multiple


def legendre_table():
    one, two = np.float32(1.0), np.float32(2.0)
    lags = np.arange(WINDOW).astype(np.float32)
    points = one - (two * (lags + np.float32(0.5))) * np.float32(1.0 / WINDOW)
    lower, this = np.zeros_like(points), np.ones_like(points)
    rows = []
    for degree in np.arange(ORDER).astype(np.float32):
        rows.append(this)
        upper = ((two * degree + one) * points * this - degree * lower) / (degree + one)
        lower, this = this, upper
    return np.stack(rows)


def in_blocks(values, steps):
    blocks = WINDOW // steps
    framed = np.zeros(values.shape[:-1] + (blocks, LANES))
    framed[..., :steps] = values.reshape(values.shape[:-1] + (blocks, steps))
    return framed.reshape(values.shape[:-1] + (blocks * LANES,))


def halves(values):
    high = values.astype(np.float32).astype(ml_dtypes.bfloat16)
    low = (values - high.astype(np.float64)).astype(ml_dtypes.bfloat16)
    return high, low


def constants(steps):
    legendre = legendre_table()
    degree = np.arange(ORDER).astype(np.float32)
    weights = legendre * ((np.float32(2.0) * degree + np.float32(1.0)) / np.float32(WINDOW))[:, None]
    flipped = in_blocks(weights[:, ::-1], steps)
    high, low = halves(flipped)
    table = {}
    table["weights"] = flipped.astype(np.float32)
    table["weights_t"] = np.concatenate([high.T, low.T], 1)
    table["endpoint"] = legendre[:, 0][None, :].astype(np.float32)
    mode = np.arange(MODES)[:, None]
    step = np.arange(WINDOW)[None, :]
    angle = 2.0 * math.pi / WINDOW * (mode * step % WINDOW)
    cosine, sine = np.cos(angle), np.sin(angle)
    back = 2.0 * math.pi / WINDOW * (mode * (WINDOW - 1 - step) % WINDOW)
    table["turn"] = np.concatenate(
        [in_blocks(v, steps) for v in (cosine, sine, np.cos(back), np.sin(back))]
    ).astype(np.float32)
    scale = np.where(np.arange(MODES) == 0, 1.0, 2.0) / WINDOW
    table["scale"] = np.tile(scale, 4)[None, :].astype(np.float32)
    high, low = halves(in_blocks(np.concatenate([cosine, -sine]), steps))
    table["to_modes"] = np.concatenate([high.T, low.T], 1)
    wave = in_blocks(np.concatenate([scale[:, None] * cosine, -scale[:, None] * sine]), steps)
    table["from_modes"] = np.concatenate(halves(wave), 1)
    lane = np.arange(LANES)
    upper = (lane[:, None] <= lane[None, :]).astype(np.float32)
    ones = np.ones((LANES, LANES), np.float32)
    for name, part in (("earlier", upper), ("later", upper.T)):
        both = np.concatenate([part, ones], 1)
        table[name] = np.concatenate([both, both]).astype(ml_dtypes.bfloat16)
    return table


def split(value):
    high = value.astype(bf16)
    return high, (value - high.astype(f32)).astype(bf16)


def dot(a, b):
    return lax.dot_general(a, b, (((1,), (0,)), ((), ())), preferred_element_type=f32)


def dot_nt(a, b):
    return lax.dot_general(a, b, (((1,), (1,)), ((), ())), preferred_element_type=f32)


def stacked_dot(value, table):
    rows, width = value.shape[0], table.shape[1] // 2
    high, low = split(value)
    out = dot(jnp.concatenate([high, low], 0), table)
    return out[:rows, :width] + out[:rows, width:] + out[rows:, :width]


def scan_lanes(value, table):
    high, low = split(value)
    out = dot(jnp.concatenate([high, low], 1), table)
    return out[:, :LANES], out[:, LANES:]


def scan_lanes_exactly(value, table):
    high, low = split(value)
    last = (value - high.astype(f32) - low.astype(f32)).astype(bf16)
    out = dot(jnp.concatenate([high, low], 1), table) + dot(last, table[:LANES])
    return out[:, :LANES], out[:, LANES:]


def unpacked(ref, i, kind, count, steps):
    rows = ref.shape[0] // count
    if i < KIND:
        return ref[pl.ds(KIND * kind + i, count, stride=rows), :]
    lane = lax.broadcasted_iota(jnp.int32, (count, LANES), 1)
    value = None
    for p in reversed(range(3)):
        row = ref[pl.ds(KIND * kind + 4 * (i - KIND) + p, count, stride=rows), :]
        row = pltpu.roll(row, LANES - steps + EXTRA * p, 1)
        value = row if value is None else jnp.where(lane < EXTRA * (p + 1), row, value)
    return value


def pack_extra(ref, value, i, kind, rows, steps):
    count = value.shape[0]
    lane = lax.broadcasted_iota(jnp.int32, (count, LANES), 1)
    behind = (lane >= steps) & (lane < steps + EXTRA)
    for p in range(3):
        at = pl.ds(KIND * kind + 4 * (i - KIND) + p, count, stride=rows)
        ref[at, :] = jnp.where(behind, pltpu.roll(value, steps - EXTRA * p, 1), ref[at, :])


def owner_order(half):
    if half == 8:
        return [1, 6, 4, 7, 2, 5, 3, 0]
    return [k ^ 1 for k in range(half)]


def owner_orders(blocks):
    half = blocks // HALVES
    return [[h * half + k for k in owner_order(half)] for h in range(HALVES)]


def first_order(blocks):
    return sum(owner_orders(blocks)[::-1], [])


def share_order(devices):
    sharing = devices // HALVES
    if sharing == 16:
        return [15, 1, 12, 8, 14, 11, 7, 3, 4, 2, 5, 6, 0, 10, 9, 13]
    return [int(k) for k in np.random.default_rng(0).permutation(sharing)]


def places(place_ref, blocks):
    block, core = place_ref[0] // CORES, place_ref[0] % CORES
    half = blocks // HALVES
    place = jnp.int32(0)
    for k, member in enumerate(owner_order(half)):
        place = jnp.where(block % half == member, k, place)
    return block, core, block // half, place


def to_wide(blocks, windows):
    per = len(blocks) // windows
    return jnp.concatenate(
        [jnp.concatenate(blocks[w * per : (w + 1) * per], 1) for w in range(windows)], 0
    )


def to_blocks(wide, windows):
    per = wide.shape[1] // LANES
    return [
        wide[w * SLOT : (w + 1) * SLOT, b * LANES : (b + 1) * LANES]
        for w in range(windows)
        for b in range(per)
    ]


def fetch(pairs, sems):
    copies = [pltpu.make_async_copy(a, b, sems.at[k]) for k, (a, b) in enumerate(pairs)]
    for copy in copies:
        copy.start()

    def ready(*which):
        for k in which:
            copies[k].wait()

    return ready


def blocks_of(value):
    return [value[k * SLOT : (k + 1) * SLOT] for k in range(value.shape[0] // SLOT)]


def same_rows(groups_ref, start, rows):
    channels = groups_ref.shape[1]
    ids = groups_ref[...].astype(f32)
    row = lax.broadcasted_iota(jnp.int32, (rows, channels), 0) + start
    lane = lax.broadcasted_iota(jnp.int32, (rows, channels), 1)
    column = jnp.sum(jnp.where(row == lane, ids, 0.0), axis=1, keepdims=True)
    return column == ids


def own_lanes(place, width, count, blocks):
    row = lax.broadcasted_iota(jnp.int32, (SLOT, width), 0)
    lane = lax.broadcasted_iota(jnp.int32, (SLOT, width), 1)
    return (lane == row * blocks + place) & (row < count)


def send_kernel(
    own,
    series_hbm,
    cot_hbm,
    mixing_hbm,
    groups_hbm,
    send_ref,
    grad_ref,
    series_ref,
    cot_ref,
    mixing_ref,
    groups_ref,
    pad_ref,
    sems,
):
    channels, steps = cot_ref.shape[1:]
    sets = channels // own
    ready = fetch(
        [
            (groups_hbm, groups_ref),
            (mixing_hbm, mixing_ref),
            (cot_hbm, cot_ref),
            (series_hbm, series_ref),
        ],
        sems,
    )
    rows = 2 * KIND
    pad_ref[...] = jnp.zeros_like(pad_ref)
    ready(2)
    pad_ref[:, :steps] = cot_ref[0]
    ready(0, 1)
    chunk = channels if channels <= 512 else 256
    total = None
    for start in range(0, channels, chunk):
        same = same_rows(groups_ref, start, chunk)
        masked = jnp.where(same, mixing_ref[start : start + chunk, :], 0.0)
        high, low = split(masked.T)
        both = jnp.concatenate(split(pad_ref[start : start + chunk, :]), 1)
        out = dot(jnp.concatenate([high, low], 0), both)
        part = out[:channels, :LANES] + out[:channels, LANES:] + out[channels:, :LANES]
        total = part if total is None else total + part
    lane = lax.broadcasted_iota(jnp.int32, (channels, LANES), 1)
    spot = lane == LANES - 2
    behind = (lane[:sets] >= steps) & (lane[:sets] < steps + EXTRA)
    sums = jnp.sum(pad_ref[...], axis=1, keepdims=True)
    grad_ref[...] = total
    ready(3)
    pad_ref[:, :steps] = series_ref[0]
    pad_ref[...] = jnp.where(spot, sums, pad_ref[...])
    for kind, ref in enumerate((pad_ref, grad_ref)):
        for i in range(KIND):
            value = ref[sets * i : sets * (i + 1), :]
            if kind and i < own - KIND:
                there = sets * (KIND + i)
                value = jnp.where(spot[:sets], sums[there : there + sets], value)
            there, p = sets * (KIND + i // 4), i % 4
            if there < channels and p < 3:
                extra = pltpu.roll(ref[there : there + sets, :], steps - EXTRA * p, 1)
                value = jnp.where(behind, extra, value)
            send_ref[pl.ds(KIND * kind + i, sets, stride=rows), :] = value
    for half in range(1, HALVES):
        send_ref[half * sets * rows : (half + 1) * sets * rows, :] = send_ref[0 : sets * rows, :]


def table_kernel(
    own,
    place_ref,
    cot_hbm,
    mixing_hbm,
    groups_hbm,
    gain_hbm,
    bias_hbm,
    out_bias_hbm,
    mode_in_hbm,
    mode_out_hbm,
    mode_re_hbm,
    mode_im_hbm,
    weights_hbm,
    endpoint_hbm,
    turn_hbm,
    scale_hbm,
    later_hbm,
    ahead_ref,
    lines_ref,
    own_ref,
    columns_ref,
    masked_ref,
    same_ref,
    cot_pad_ref,
    cot_send_ref,
    cot_ref,
    mixing_ref,
    groups_ref,
    gain_ref,
    bias_ref,
    out_bias_ref,
    mode_in_ref,
    mode_out_ref,
    mode_re_ref,
    mode_im_ref,
    weights_ref,
    endpoint_ref,
    turn_ref,
    scale_ref,
    later_ref,
    turned_ref,
    sems,
):
    ready = fetch(
        [
            (mode_in_hbm, mode_in_ref),
            (mode_out_hbm, mode_out_ref),
            (endpoint_hbm, endpoint_ref),
            (weights_hbm, weights_ref),
            (mode_re_hbm, mode_re_ref),
            (mode_im_hbm, mode_im_ref),
            (scale_hbm, scale_ref),
            (turn_hbm, turn_ref),
            (later_hbm, later_ref),
            (groups_hbm, groups_ref),
            (mixing_hbm, mixing_ref),
            (cot_hbm, cot_ref),
            (gain_hbm, gain_ref),
            (bias_hbm, bias_ref),
            (out_bias_hbm, out_bias_ref),
        ],
        sems,
    )
    channels, steps = cot_ref.shape[1:]
    width = ahead_ref.shape[0]
    per = width // LANES
    sets = channels // own
    count = 2 * MODES
    lines_ref[...] = jnp.zeros_like(lines_ref)
    turned_ref[...] = jnp.zeros_like(turned_ref)
    cot_pad_ref[...] = jnp.zeros_like(cot_pad_ref)
    same_ref[...] = jnp.zeros_like(same_ref)
    ready(0, 1, 2, 3)
    kernel = lax.dot_general(
        mode_in_ref[...],
        weights_ref[...],
        (((1,), (0,)), ((), ())),
        precision=lax.Precision.HIGHEST,
        preferred_element_type=f32,
    )
    lines_ref[0:RANK, :] = kernel
    mix = jnp.sum(mode_out_ref[...] * endpoint_ref[...], axis=1, keepdims=True)
    ready(4, 5, 6)
    scale = scale_ref[:, 0:count]
    gain_re, gain_im = mode_re_ref[...], mode_im_ref[...]
    signed = jnp.concatenate([gain_re, -gain_im], 1) * scale
    sign = jnp.where(lax.broadcasted_iota(jnp.int32, (RANK, count), 1) < MODES, 1.0, -1.0)
    lines_ref[8 : 8 + RANK, 0:count] = signed * mix
    lines_ref[16 : 16 + RANK, 0:count] = sign * scale * mix
    lines_ref[24 : 24 + RANK, 0:count] = signed
    turned_ref[0:RANK, 0:count] = jnp.concatenate([gain_re, gain_im], 1) * mix
    columns = turned_ref[...].T[0:count]
    response = None
    for r in range(RANK):
        term = columns[:, r : r + 1] * kernel[r : r + 1, :]
        response = term if response is None else response + term
    ready(7, 8)
    real, imag = response[:MODES], response[MODES:]
    cosine, sine = turn_ref[0:MODES], turn_ref[MODES : 2 * MODES]
    cos_b, sin_b = turn_ref[2 * MODES : 3 * MODES], turn_ref[3 * MODES : 4 * MODES]
    turned = jnp.concatenate([real * cos_b + imag * sin_b, imag * cos_b - real * sin_b], 0)
    rows = jnp.concatenate([turned[:, b * LANES : (b + 1) * LANES] for b in range(per)], 0)
    local, total = scan_lanes_exactly(rows, later_ref[...])
    run = jnp.zeros((count, LANES), f32)
    suffix = [None] * per
    for b in reversed(range(per)):
        suffix[b] = local[b * count : (b + 1) * count] + run
        run = run + total[b * count : (b + 1) * count]
    for b in range(per):
        at = slice(b * LANES, (b + 1) * LANES)
        c, s = cosine[:, at], sine[:, at]
        parts = []
        for value in (suffix[b], run - suffix[b]):
            re, im = value[:MODES], value[MODES:]
            parts += [re * c + im * s, im * c - re * s]
        high, low = split(jnp.concatenate(parts, 0).T)
        ahead_ref[at, 0:LANES] = high
        ahead_ref[at, LANES : 2 * LANES] = low
    ready(9, 10, 11, 12, 13, 14)
    chunk = channels if channels <= 512 else 256
    for start in range(0, channels, chunk):
        at = slice(start, start + chunk)
        same = same_rows(groups_ref, start, chunk)
        high, low = split(jnp.where(same, mixing_ref[at, :], 0.0))
        masked_ref[0, at, :] = high
        masked_ref[1, at, :] = low
        same_ref[at, 0:channels] = jnp.where(same, 1.0, 0.0)
        row = lax.broadcasted_iota(jnp.int32, (chunk, channels), 0) + start
        lane = lax.broadcasted_iota(jnp.int32, (chunk, channels), 1)
        for k, ref in enumerate((gain_ref, bias_ref, out_bias_ref)):
            columns_ref[at, k : k + 1] = jnp.sum(
                jnp.where(row == lane, ref[...], 0.0), axis=1, keepdims=True
            )
    unused, unused, unused, place = places(place_ref, sets * HALVES)
    mine = own_lanes(place, channels, own, sets)
    gain = jnp.sum(jnp.where(mine, gain_ref[...], 0.0), axis=1, keepdims=True)
    gain = jnp.where(lax.broadcasted_iota(jnp.int32, (SLOT, 1), 0) < own, gain, 1.0)
    bias = jnp.sum(jnp.where(mine, bias_ref[...], 0.0), axis=1, keepdims=True)
    own_ref[0:SLOT, :] = jnp.broadcast_to(gain, (SLOT, LANES))
    own_ref[SLOT : 2 * SLOT, :] = jnp.broadcast_to(bias, (SLOT, LANES))
    own_ref[2 * SLOT : 3 * SLOT, :] = jnp.broadcast_to(1.0 / gain, (SLOT, LANES))
    own_ref[3 * SLOT :, :] = jnp.broadcast_to(scale_ref[...], (8, LANES))
    cot_pad_ref[:, :steps] = cot_ref[0]
    most = cot_send_ref.shape[0]
    lane = lax.broadcasted_iota(jnp.int32, (channels - most, LANES), 1)
    behind = (lane >= steps) & (lane < steps + EXTRA)
    cot_send_ref[...] = cot_pad_ref[0:most, :]
    for p in range(3):
        at = pl.ds(p, channels - most, stride=3)
        moved = pltpu.roll(cot_pad_ref[most:, :], steps - EXTRA * p, 1)
        cot_send_ref[at, :] = jnp.where(behind, moved, cot_send_ref[at, :])


def normalized(x, blocks, steps, earlier):
    rows = x.shape[0]
    local, total = scan_lanes(jnp.concatenate([x, x * x], 0), earlier)
    first, second = blocks_of(local[:rows]), blocks_of(local[rows:])
    first_all, second_all = blocks_of(total[:rows]), blocks_of(total[rows:])
    run_one = jnp.zeros((SLOT, LANES), f32)
    run_two = jnp.zeros((SLOT, LANES), f32)
    lane = lax.broadcasted_iota(jnp.int32, (SLOT, LANES), 1)
    found = []
    for k in range(blocks):
        inverse = 1.0 / (lane + (k * steps + 1 + WINDOW)).astype(f32)
        mean = (first[k] + run_one) * inverse
        variance = (second[k] + run_two + WINDOW) * inverse - mean * mean + EPSILON
        found.append((mean, variance, run_one, run_two))
        run_one = run_one + first_all[k]
        run_two = run_two + second_all[k]
    return found


def owned(recv_ref, tail_ref, own, blocks, steps):
    lane = lax.broadcasted_iota(jnp.int32, (blocks, LANES), 1)
    tail_ref[...] = jnp.zeros_like(tail_ref)
    for kind in range(2):
        for i in range(KIND, own):
            tail_ref[pl.ds(8 * kind + i - KIND, blocks, stride=16), :] = jnp.where(
                lane < steps, unpacked(recv_ref, i, kind, blocks, steps), 0.0
            )
    got = recv_ref[...].reshape(blocks, 2 * KIND, LANES)
    got = jnp.where(lax.broadcasted_iota(jnp.int32, got.shape, 2) < steps, got, 0.0)
    tail = tail_ref[...].reshape(blocks, 16, LANES)
    x = jnp.concatenate([got[:, 0:KIND], tail[:, 0:8]], 1)
    grad = jnp.concatenate([got[:, KIND : 2 * KIND], tail[:, 8:16]], 1)
    order = first_order(blocks)
    slots = [order.index(b) for b in range(blocks)]
    return [x[k] for k in slots], [grad[k] for k in slots]


def forward_kernel(
    own,
    blocks,
    steps,
    place_ref,
    recv_ref,
    own_ref,
    ahead_ref,
    from_modes_ref,
    to_modes_ref,
    earlier_ref,
    send_ref,
    mean_ref,
    inverse_ref,
    centered_ref,
    shifted_ref,
    grad_ref,
    normal_grad_ref,
    waves_ref,
    tail_ref,
    back_tail_ref,
):
    windows = blocks * steps // WINDOW
    x, grad = owned(recv_ref, tail_ref, own, blocks, steps)
    found = normalized(jnp.concatenate(x, 0), blocks, steps, earlier_ref[...])
    gain, bias, over = own_ref[0:SLOT], own_ref[SLOT : 2 * SLOT], own_ref[2 * SLOT : 3 * SLOT]
    row = lax.broadcasted_iota(jnp.int32, (SLOT, LANES), 0)
    lane = lax.broadcasted_iota(jnp.int32, (SLOT, LANES), 1)
    held = (row < own) & (lane < steps)
    normal, spreads, recon_grad = [], [], []
    for k in range(blocks):
        at = slice(k * SLOT, (k + 1) * SLOT)
        mean, variance = found[k][:2]
        inverse = lax.rsqrt(variance)
        spread = variance * inverse
        centered = (x[k] - mean) * inverse
        normal.append(gain * centered + bias)
        spreads.append(spread)
        recon_grad.append(jnp.where(held, grad[k] * spread * over, 0.0))
        mean_ref[at, :] = mean
        inverse_ref[at, :] = inverse
        centered_ref[at, :] = centered
        grad_ref[at, :] = grad[k]
    spectra = stacked_dot(to_wide(normal, windows), ahead_ref[...])
    waves = stacked_dot(to_wide(recon_grad, windows), to_modes_ref[...])
    count = 2 * MODES
    current, before = spectra[:, :count], spectra[:, count:]
    zero = jnp.zeros((SLOT, count), f32)
    after = zero
    if windows > 1:
        current = current + jnp.concatenate([zero, before[:-SLOT]], 0)
        after = jnp.concatenate([waves[SLOT:], zero], 0)
    recon = stacked_dot(current, from_modes_ref[...])
    waves = jnp.concatenate([waves, after], 1)
    waves_ref[...] = waves
    recon = to_blocks(recon, windows)
    normal_grad = to_blocks(convolved_back(waves * own_ref[3 * SLOT : 3 * SLOT + 1], ahead_ref[...]), windows)
    backs = []
    for b in range(blocks):
        at = slice(b * SLOT, (b + 1) * SLOT)
        shifted = (recon[b] - bias) * over
        shifted_ref[at, :] = shifted
        normal_grad_ref[at, :] = normal_grad[b]
        backs.append(shifted * spreads[b] + found[b][0])
    unused, unused, half, unused = places(place_ref, blocks)
    first = half == 0
    sets = blocks // HALVES
    count = 3 * KIND
    one, two = lane == LANES - 2, lane == LANES - 1
    for k, b in enumerate(owner_orders(blocks)[0]):
        c = b + sets
        arrays = [
            jnp.where(first, backs[b], backs[c]),
            jnp.where(first, backs[c], backs[b]),
            jnp.where(first, normal_grad[b], normal_grad[c]),
        ]
        run_one = jnp.where(first, found[b][2], found[c][2])
        run_two = jnp.where(first, found[b][3], found[c][3])
        arrays[0] = jnp.where(one, run_one, jnp.where(two, run_two, arrays[0]))
        send_ref[k * count : k * count + KIND, :] = arrays[0][:KIND]
        tail = jnp.where(one[:8], run_one[KIND:], jnp.where(two[:8], run_two[KIND:], arrays[1][:8]))
        send_ref[k * count + KIND : k * count + KIND + 8, :] = tail
        send_ref[k * count + KIND + 8 : k * count + 2 * KIND, :] = arrays[1][8:KIND]
        send_ref[k * count + 2 * KIND : k * count + 3 * KIND, :] = arrays[2][:KIND]
        for kind in range(3):
            back_tail_ref[(3 * k + kind) * 8 : (3 * k + kind + 1) * 8, :] = arrays[kind][KIND:]
    for kind in range(3):
        for i in range(KIND, own):
            value = back_tail_ref[pl.ds(8 * kind + i - KIND, sets, stride=24), :]
            pack_extra(send_ref, value, i, kind, count, steps)


def backward_kernel(
    own,
    blocks,
    steps,
    wide,
    place_ref,
    recv_ref,
    own_ref,
    mean_ref,
    inverse_ref,
    centered_ref,
    shifted_ref,
    grad_ref,
    normal_grad_ref,
    waves_ref,
    lines_ref,
    turn_hbm,
    weights_t_hbm,
    earlier_hbm,
    misc_ref,
    starts_ref,
    turn_ref,
    weights_t_ref,
    earlier_ref,
    sems,
):
    ready = fetch(
        [(turn_hbm, turn_ref), (earlier_hbm, earlier_ref), (weights_t_hbm, weights_t_ref)], sems
    )
    windows = blocks * steps // WINDOW
    count = 2 * MODES
    mean, inverse, centered, shifted, grad, normal_grad = (
        blocks_of(ref[...])
        for ref in (
            mean_ref,
            inverse_ref,
            centered_ref,
            shifted_ref,
            grad_ref,
            normal_grad_ref,
        )
    )
    gain, bias, over = own_ref[0:SLOT], own_ref[SLOT : 2 * SLOT], own_ref[2 * SLOT : 3 * SLOT]
    row = lax.broadcasted_iota(jnp.int32, (SLOT, LANES), 0)
    lane = lax.broadcasted_iota(jnp.int32, (SLOT, LANES), 1)
    held = (row < own) & (lane < steps)
    waves = waves_ref[...]
    gain_sum = jnp.zeros((SLOT, LANES), f32)
    bias_sum = jnp.zeros((SLOT, LANES), f32)
    normal, ones, twos = [], [], []
    for k in range(blocks):
        over_q = 1.0 / (lane + (k * steps + 1 + WINDOW)).astype(f32)
        normal.append(jnp.where(held, gain * centered[k] + bias, 0.0))
        recon_grad = grad[k] / inverse[k] * over
        gain_sum = gain_sum + normal_grad[k] * centered[k] - recon_grad * shifted[k]
        bias_sum = bias_sum + normal_grad[k] - recon_grad
        first, second = statistics(
            grad[k],
            shifted[k],
            normal_grad[k] * gain * inverse[k],
            centered[k],
            mean[k],
            inverse[k],
            over_q,
        )
        ones.append(jnp.where(held, first, 0.0))
        twos.append(jnp.where(held, second, 0.0))
    gain_sum, bias_sum = jnp.where(held, gain_sum, 0.0), jnp.where(held, bias_sum, 0.0)
    ready(1)
    high, low = split(jnp.concatenate(ones + twos, 0))
    total = blocks_of(dot(jnp.concatenate([high, low], 1), earlier_ref[:, LANES:]))
    run_one = jnp.zeros((SLOT, LANES), f32)
    run_two = jnp.zeros((SLOT, LANES), f32)
    unused, unused, half, place = places(place_ref, blocks)
    first = half == 0
    sets = blocks // HALVES
    starts = [None] * blocks
    for k in reversed(range(blocks)):
        both = jnp.where(lane == row, run_one, jnp.where(lane == row + 32, run_two, 0.0))
        starts[k] = jnp.sum(both, 0, keepdims=True)
        run_one = run_one + total[k]
        run_two = run_two + total[blocks + k]
    for at, device in enumerate(share_order(blocks * CORES)):
        k = device // CORES
        starts_ref[at : at + 1, :] = jnp.where(first, starts[k], starts[k + sets])
    signal = to_wide(normal, windows)
    high, low = split(signal)
    w_high, w_low = split(waves.T)
    pairs = dot(
        jnp.concatenate([w_high, w_high, w_low], 1), jnp.concatenate([high, low, high], 0)
    )
    ready(0)
    cosine, sine = turn_ref[0:MODES], turn_ref[MODES : 2 * MODES]
    cos_b, sin_b = turn_ref[2 * MODES : 3 * MODES], turn_ref[3 * MODES : 4 * MODES]

    def turned(value):
        re, im = value[:MODES], value[MODES:]
        return jnp.concatenate([re * cosine - im * sine, -(re * sine + im * cosine)], 0)

    per = pairs.shape[1] // LANES
    after = turned(pairs[count:])
    left = turned(pairs[:count]) - after
    after = sum(after[:, b * LANES : (b + 1) * LANES] for b in range(per))
    local, total = scan_lanes(
        jnp.concatenate([left[:, b * LANES : (b + 1) * LANES] for b in range(per)], 0),
        earlier_ref[...],
    )
    run = jnp.broadcast_to(jnp.sum(after, 1, keepdims=True), (count, LANES))
    sums = []
    for b in range(per):
        sums.append(local[b * count : (b + 1) * count] + run)
        run = run + total[b * count : (b + 1) * count]
    sums = jnp.concatenate(sums, 1)
    re, im = sums[:MODES], sums[MODES:]
    crossed = jnp.concatenate([re * cos_b + im * sin_b, im * cos_b - re * sin_b], 0)
    high, low = split(crossed)
    s_high, s_low = split(lines_ref[8:16, 0:count])
    kernel_grad = dot(
        jnp.concatenate([s_high, s_high, s_low], 1), jnp.concatenate([high, low, high], 0)
    )
    k_high, k_low = split(lines_ref[0:8, :])
    overlap = dot_nt(
        jnp.concatenate([k_high, k_high, k_low], 1), jnp.concatenate([high, low, high], 1)
    )
    modes = overlap * lines_ref[16:24, 0:count]
    mix_grad = jnp.sum(overlap * lines_ref[24:32, 0:count], axis=1, keepdims=True)
    ready(2)
    mode_in_grad = stacked_dot(kernel_grad, weights_t_ref[...])
    misc_ref[...] = jnp.zeros_like(misc_ref)
    misc_ref[0:RANK, :] = mode_in_grad[0:RANK, :LANES]
    misc_ref[RANK : 2 * RANK, :] = mode_in_grad[0:RANK, LANES:]
    misc_ref[8 : 8 + RANK, 0:count] = modes[0:RANK]
    misc_ref[8 : 8 + RANK, count : 2 * count] = jnp.broadcast_to(mix_grad, (8, count))[0:RANK]
    mine = own_lanes(place, wide, own, sets)
    at = 12
    gain_row = jnp.sum(
        jnp.where(mine, jnp.sum(gain_sum, 1, keepdims=True), 0.0), axis=0, keepdims=True
    )
    bias_row = jnp.sum(
        jnp.where(mine, jnp.sum(bias_sum, 1, keepdims=True), 0.0), axis=0, keepdims=True
    )
    cot_sum = jnp.sum(recv_ref[...].reshape(blocks, 2 * KIND, LANES), axis=0)[:SLOT]
    cot_row = jnp.sum(
        jnp.where(mine, cot_sum[:, LANES - 2 : LANES - 1], 0.0), axis=0, keepdims=True
    )
    for value in (gain_row, bias_row, cot_row):
        for j in range(wide // LANES):
            misc_ref[at : at + 1, :] = value[:, j * LANES : (j + 1) * LANES]
            at += 1


def convolved_back(waves, ahead):
    rows = waves.shape[0]
    high, low = split(waves)
    out = dot_nt(jnp.concatenate([high, low], 0), ahead[:, :LANES])
    return out[:rows] + out[rows:] + dot_nt(high, ahead[:, LANES:])


def statistics(grad, shifted, scaled, centered, mean, inverse, over_q):
    variance_grad = (grad * shifted - scaled * centered) * (0.5 * inverse)
    first = (grad - scaled - 2.0 * mean * variance_grad) * over_q
    return first, variance_grad * over_q


def pieces(channels, devices):
    tiles, rest = channels // LANES, channels % LANES
    each = channels // devices
    rest_rows = channels * rest // LANES
    misc_rows = 12 + 3 * (up(channels, LANES) // LANES)
    extra = up(rest_rows + misc_rows, devices) // devices
    return tiles, rest, each, rest_rows, misc_rows, extra


def gathered(recv_ref, kind, own, steps, dense_ref):
    sets = recv_ref.shape[0] // (3 * KIND)
    for i in range(own):
        dense_ref[sets * i : sets * (i + 1), :] = unpacked(recv_ref, i, kind, sets, steps)


def mix_kernel(
    own,
    devices,
    steps,
    recv_ref,
    same_ref,
    cot_ref,
    cot_partner_ref,
    misc_ref,
    starts_ref,
    send_ref,
    dense_ref,
    partner_ref,
    cot_all_ref,
    misc_all_ref,
):
    channels = same_ref.shape[0]
    tiles, rest, each, rest_rows, misc_rows, extra = pieces(channels, devices)
    slot = send_ref.shape[0] // devices
    most = cot_partner_ref.shape[0]
    cot = cot_partner_ref[...]
    cot_all_ref[0:most, :] = jnp.where(
        lax.broadcasted_iota(jnp.int32, cot.shape, 1) < steps, cot, 0.0
    )
    lane = lax.broadcasted_iota(jnp.int32, (channels - most, LANES), 1)
    cot = jnp.zeros((channels - most, LANES), f32)
    for p in reversed(range(3)):
        row = cot_partner_ref[pl.ds(p, channels - most, stride=3), :]
        row = pltpu.roll(row, LANES - steps + EXTRA * p, 1)
        cot = jnp.where(lane < min(EXTRA * (p + 1), steps), row, cot)
    cot_all_ref[most:, :] = cot
    three = []
    for kind, ref in enumerate((dense_ref, partner_ref)):
        if ref.shape[0] > channels:
            ref[channels:, :] = jnp.zeros((ref.shape[0] - channels, LANES), f32)
        gathered(recv_ref, kind, own, steps, ref)
        high, low = split(ref[...])
        three += [high, low, high]
    three = jnp.concatenate(three, 1)
    chunk = channels if channels <= 512 else devices
    for start in range(0, channels, chunk):
        at = slice(start, start + chunk)
        six = []
        for ref in (cot_ref, cot_all_ref):
            high, low = split(ref[at, :])
            six += [high, high, low]
        grad = dot_nt(jnp.concatenate(six, 1), three)
        for j in range(tiles):
            lanes = slice(j * LANES, (j + 1) * LANES)
            tile = grad[:, lanes] * same_ref[at, lanes]
            for i in range(chunk // devices):
                send_ref[pl.ds(j * each + start // devices + i, devices, stride=slot), :] = tile[
                    devices * i : devices * (i + 1)
                ]
        if rest:
            lanes = slice(tiles * LANES, tiles * LANES + LANES)
            last = grad[:, lanes] * same_ref[at, lanes]
            folded = last[0:rest_rows]
            for g in range(1, LANES // rest):
                folded = folded + pltpu.roll(
                    last[g * rest_rows : (g + 1) * rest_rows], g * rest, 1
                )
            misc_all_ref[0:rest_rows, :] = folded
    end = rest_rows + misc_rows
    misc_all_ref[rest_rows:end, :] = misc_ref[0:misc_rows, :]
    if misc_all_ref.shape[0] > end:
        misc_all_ref[end:, :] = jnp.zeros((misc_all_ref.shape[0] - end, LANES), f32)
    for k in range(extra):
        send_ref[pl.ds(tiles * each + k, devices, stride=slot), :] = misc_all_ref[
            devices * k : devices * (k + 1), :
        ]
    for k in range(tiles * each + extra, slot - 1):
        send_ref[pl.ds(k, devices, stride=slot), :] = jnp.zeros((devices, LANES), f32)
    send_ref[pl.ds(slot - 1, devices, stride=slot), :] = starts_ref[...]


def steps_kernel(
    own,
    devices,
    place_ref,
    recv_ref,
    shares_ref,
    grad_ref,
    columns_ref,
    masked_ref,
    series_hbm,
    cot_hbm,
    earlier_hbm,
    later_hbm,
    out_ref,
    series_grad_ref,
    series_ref,
    cot_ref,
    earlier_ref,
    later_ref,
    dense_ref,
    back_ref,
    sums_ref,
    pad_ref,
    sems,
):
    ready = fetch(
        [
            (series_hbm, series_ref),
            (cot_hbm, cot_ref),
            (earlier_hbm, earlier_ref),
            (later_hbm, later_ref),
        ],
        sems,
    )
    channels, steps = series_ref.shape[1:]
    sets = channels // own
    block, core, unused, unused = places(place_ref, sets * HALVES)
    gathered(recv_ref, 0, own, steps, dense_ref)
    gathered(recv_ref, 2, own, steps, back_ref)
    for i in range(own):
        sums_ref[sets * i : sets * (i + 1), :] = recv_ref[pl.ds(i, sets, stride=3 * KIND), :]
    pad_ref[...] = jnp.zeros_like(pad_ref)
    gain, bias, shift = (columns_ref[:, k : k + 1] for k in range(3))
    restored = dense_ref[...]
    both = jnp.concatenate(split(restored), 1)
    ready(0)
    pad_ref[:, :steps] = series_ref[0]
    chunk = channels if channels <= 512 else 256
    for start in range(0, channels, chunk):
        at = slice(start, start + chunk)
        out = dot(jnp.concatenate([masked_ref[0, at, :], masked_ref[1, at, :]], 0), both)
        mixed = out[:chunk, :LANES] + out[:chunk, LANES:] + out[chunk:, :LANES]
        out_ref[0, at, :] = (pad_ref[at, :] + mixed + shift[at])[:, :steps]
    x = pad_ref[...]
    ready(2)
    local, unused = scan_lanes(jnp.concatenate([x, x * x], 0), earlier_ref[...])
    lane = lax.broadcasted_iota(jnp.int32, (channels, LANES), 1)
    over_q = 1.0 / (lane + (block * steps + 1 + WINDOW)).astype(f32)
    mean = (local[:channels] + sums_ref[:, LANES - 2 : LANES - 1]) * over_q
    variance = (local[channels:] + sums_ref[:, LANES - 1 : LANES] + WINDOW) * over_q
    inverse = lax.rsqrt(variance - mean * mean + EPSILON)
    centered = (x - mean) * inverse
    scaled = back_ref[...] * gain * inverse
    first, second = statistics(
        grad_ref[...], (restored - mean) * inverse, scaled, centered, mean, inverse, over_q
    )
    held = lane < steps
    ready(3)
    local, unused = scan_lanes(
        jnp.concatenate([jnp.where(held, first, 0.0), jnp.where(held, second, 0.0)], 0),
        later_ref[...],
    )
    slot = shares_ref.shape[0] // devices
    rows = []
    order = share_order(devices * HALVES)
    for owner in owner_orders(sets * HALVES)[0]:
        even, odd = (order.index(owner * CORES + r) * slot + slot - 1 for r in range(CORES))
        rows.append(
            jnp.where(core == 0, shares_ref[even : even + 1, :], shares_ref[odd : odd + 1, :])
        )
    later = jnp.concatenate(rows, 0)
    part = scaled + local[:channels] + 2.0 * x * local[channels:]
    ready(1)
    for i in range(own):
        at = slice(sets * i, sets * (i + 1))
        sums = later[:, i : i + 1] + 2.0 * x[at] * later[:, 32 + i : 33 + i]
        series_grad_ref[0, at, :] = cot_ref[0, at, :] + (part[at] + sums)[:, :steps]


def sum_kernel(devices, recv_ref, send_ref):
    slot = recv_ref.shape[0] // devices
    total = recv_ref[0:slot, :]
    for s in range(1, devices):
        total = total + recv_ref[s * slot : (s + 1) * slot, :]
    for s in range(devices):
        send_ref[s * slot : (s + 1) * slot, :] = total


def spread_kernel(
    devices,
    recv_ref,
    endpoint_ref,
    gain_ref,
    bias_ref,
    mode_in_ref,
    mode_out_ref,
    mode_re_ref,
    mode_im_ref,
    mixing_ref,
    out_bias_ref,
    misc_ref,
):
    channels = mixing_ref.shape[0]
    tiles, rest, each, rest_rows, misc_rows, extra = pieces(channels, devices)
    slot = recv_ref.shape[0] // devices
    for j in range(tiles):
        for i in range(each):
            mixing_ref[devices * i : devices * (i + 1), j * LANES : (j + 1) * LANES] = recv_ref[
                pl.ds(j * each + i, devices, stride=slot), :
            ]
    for k in range(extra):
        misc_ref[devices * k : devices * (k + 1), :] = recv_ref[
            pl.ds(tiles * each + k, devices, stride=slot), :
        ]
    if rest:
        folded = misc_ref[0:rest_rows, :]
        for g in range(LANES // rest):
            piece = folded if g == 0 else pltpu.roll(folded, LANES - g * rest, 1)
            mixing_ref[g * rest_rows : (g + 1) * rest_rows, tiles * LANES :] = piece[:, :rest]
    at = rest_rows
    mode_in_ref[:, 0:LANES] = misc_ref[at : at + RANK, :]
    mode_in_ref[:, LANES : 2 * LANES] = misc_ref[at + RANK : at + 2 * RANK, :]
    modes = misc_ref[at + 8 : at + 8 + RANK, :]
    mode_re_ref[...] = modes[:, 0:MODES]
    mode_im_ref[...] = modes[:, MODES : 2 * MODES]
    mode_out_ref[...] = modes[:, 2 * MODES : 2 * MODES + 1] * endpoint_ref[...]
    at += 12
    for ref in (gain_ref, bias_ref, out_bias_ref):
        for start in range(0, channels, LANES):
            size = min(LANES, channels - start)
            ref[:, start : start + size] = misc_ref[at : at + 1, 0:size]
            at += 1


def call(kernel, outs, smem=(), vmem=(), hbm=(), scratch=(), cost=None, limit=None):
    in_vmem = pl.BlockSpec(memory_space=pltpu.VMEM)
    in_smem = pl.BlockSpec(memory_space=pltpu.SMEM)
    in_hbm = pl.BlockSpec(memory_space=pltpu.HBM)
    held = [pltpu.VMEM(a.shape, a.dtype) for a in hbm] + list(scratch)
    if hbm:
        held.append(pltpu.SemaphoreType.DMA((len(hbm),)))
    hbm = [pltpu.with_memory_space_constraint(a, pltpu.HBM) for a in hbm]
    return pl.pallas_call(
        kernel,
        out_shape=tuple(jax.ShapeDtypeStruct(shape, kind) for shape, kind in outs),
        in_specs=[in_smem] * len(smem) + [in_vmem] * len(vmem) + [in_hbm] * len(hbm),
        out_specs=tuple(in_vmem for unused in outs),
        scratch_shapes=held,
        compiler_params=pltpu.CompilerParams(vmem_limit_bytes=limit),
        cost_estimate=cost,
    )(*smem, *vmem, *hbm)


def exchange(value, axis, orders):
    count = len(orders[0])
    out = lax.all_to_all(
        value.reshape(count, value.shape[0] // count, value.shape[1]),
        axis,
        split_axis=0,
        concat_axis=0,
        axis_index_groups=orders,
    )
    return out.reshape(value.shape)


def body(
    series,
    group_ids,
    rev_gain,
    rev_bias,
    mode_in,
    mode_out,
    mode_re,
    mode_im,
    mixing,
    out_bias,
    cotangent,
):
    samples, channels, steps = series.shape
    blocks = lax.axis_size("seq")
    sets = blocks // HALVES
    devices = blocks * lax.axis_size("rep")
    sharing = devices // HALVES
    own = channels // sets
    width = WINDOW // steps * LANES
    padded = up(channels, LANES)
    place = lax.axis_index(("seq", "rep")).astype(jnp.int32).reshape(1)
    halves_of = owner_orders(blocks)
    all_of = [first_order(blocks)]
    shares_of = [[h * sharing + k for k in share_order(devices)] for h in range(HALVES)]
    const = {name: jnp.asarray(value) for name, value in constants(steps).items()}
    groups = group_ids.reshape(1, channels)
    limit = (16 if channels <= 512 else 56) * 2**20
    run = functools.partial(call, limit=limit)
    busy = pl.CostEstimate(flops=4_000_000_000, bytes_accessed=8_000_000, transcendentals=0)
    brief = pl.CostEstimate(flops=100_000_000, bytes_accessed=1_000_000, transcendentals=0)

    send, restored_grad = run(
        functools.partial(send_kernel, own),
        [((blocks * 2 * KIND, LANES), f32), ((channels, LANES), f32)],
        hbm=(series, cotangent, mixing, groups),
        scratch=[pltpu.VMEM((channels, LANES), f32)],
        cost=brief,
    )
    ahead, lines, mine, columns, masked, same, cot, cot_send = run(
        functools.partial(table_kernel, own),
        [
            ((width, 2 * LANES), bf16),
            ((32, width), f32),
            ((3 * SLOT + 8, LANES), f32),
            ((channels, LANES), f32),
            ((2, channels, channels), bf16),
            ((channels, padded), f32),
            ((channels, LANES), f32),
            ((channels * 3 // 4, LANES), f32),
        ],
        smem=(place,),
        hbm=(
            cotangent,
            mixing,
            groups,
            rev_gain.reshape(1, channels),
            rev_bias.reshape(1, channels),
            out_bias.reshape(1, channels),
            mode_in.T,
            mode_out.T,
            mode_re,
            mode_im,
            const["weights"],
            const["endpoint"],
            const["turn"],
            const["scale"],
            const["later"],
        ),
        scratch=[pltpu.VMEM((LANES, LANES), f32)],
        cost=busy,
    )
    owned_rows = exchange(send, "seq", all_of)
    rows = blocks * SLOT
    windows = blocks * steps // WINDOW
    send, *kept = run(
        functools.partial(forward_kernel, own, blocks, steps),
        [((sets * 3 * KIND, LANES), f32)]
        + [((rows, LANES), f32)] * 6
        + [((windows * SLOT, LANES), f32)],
        smem=(place,),
        vmem=(
            owned_rows,
            mine,
            ahead,
            const["from_modes"],
            const["to_modes"],
            const["earlier"],
        ),
        scratch=[pltpu.VMEM((blocks * 16, LANES), f32), pltpu.VMEM((sets * 24, LANES), f32)],
        cost=brief,
    )
    there = exchange(send, "seq", halves_of)
    cot_send, kept[0] = lax.optimization_barrier((cot_send, kept[0]))
    cot_partner = lax.ppermute(cot_send, "seq", [(k, (k + sets) % blocks) for k in range(blocks)])
    tiles, rest, each, rest_rows, misc_rows, extra = pieces(channels, sharing)
    slot = up(tiles * each + extra + 1, 8)
    misc, starts = run(
        functools.partial(backward_kernel, own, blocks, steps, padded),
        [
            ((up(misc_rows, 8), LANES), f32),
            ((sharing, LANES), f32),
        ],
        smem=(place,),
        vmem=(owned_rows, mine, *kept, lines),
        hbm=(const["turn"], const["weights_t"], const["earlier"]),
        cost=busy,
    )
    (send,) = run(
        functools.partial(mix_kernel, own, sharing, steps),
        [((sharing * slot, LANES), f32)],
        vmem=(there, same, cot, cot_partner, misc, starts),
        scratch=[
            pltpu.VMEM((padded, LANES), f32),
            pltpu.VMEM((padded, LANES), f32),
            pltpu.VMEM((channels, LANES), f32),
            pltpu.VMEM((up(extra * sharing, 8), LANES), f32),
        ],
        cost=brief,
    )
    shares = exchange(send, ("seq", "rep"), shares_of)
    (send,) = run(
        functools.partial(sum_kernel, sharing),
        [((sharing * slot, LANES), f32)],
        vmem=(shares,),
        cost=brief,
    )
    sums = exchange(send, ("seq", "rep"), shares_of)
    layer_out, series_grad = run(
        functools.partial(steps_kernel, own, sharing),
        [((1, channels, steps), f32), ((1, channels, steps), f32)],
        smem=(place,),
        vmem=(there, shares, restored_grad, columns, masked),
        hbm=(series, cotangent, const["earlier"], const["later"]),
        scratch=[pltpu.VMEM((channels, LANES), f32)] * 4,
        cost=busy,
    )
    outs = run(
        functools.partial(spread_kernel, sharing),
        [
            ((1, channels), f32),
            ((1, channels), f32),
            ((RANK, ORDER), f32),
            ((RANK, ORDER), f32),
            ((RANK, MODES), f32),
            ((RANK, MODES), f32),
            ((channels, channels), f32),
            ((1, channels), f32),
        ],
        vmem=(sums, const["endpoint"]),
        scratch=[pltpu.VMEM((up(extra * sharing, 8), LANES), f32)],
        cost=brief,
    )
    return (
        layer_out,
        series_grad,
        outs[0].reshape(channels),
        outs[1].reshape(channels),
        outs[2].T,
        outs[3].T,
        outs[4],
        outs[5],
        outs[6],
        outs[7].reshape(channels),
    )


def solution(mesh):
    time_split = P("rep", None, "seq")
    in_specs = (time_split,) + (P(),) * 9 + (time_split,)
    out_specs = (time_split, time_split) + (P(),) * 8
    return jax.shard_map(body, mesh=mesh, in_specs=in_specs, out_specs=out_specs, check_vma=False)
```
